32 devices in a mesh: frame: 8 (over z, x), head: 4 (over y, core).
Axes of the slice: x: 2, y: 2, z: 4, core: 2. Of those that a mesh axis runs over, the one named last changes fastest.
Arguments:
- query_proj: bfloat16 [16, 12288, 128], P('head', 'frame'), may hold values from -6 to 6
- key_proj: bfloat16 [16, 12288, 128], P('head', 'frame'), may hold values from -6 to 6
- value_proj: bfloat16 [16, 12288, 128], P('head', 'frame'), may hold values from -6 to 6
- lengths: int32 [16], replicated, may hold values from 384 to 1536, as said below
- out_weight: bfloat16 [1024, 1024], P('head'), may hold values from -0.1875 to 0.1875
Outputs:
- projected: bfloat16 [24576, 1024], P(('frame', 'head'))
The draws below stay inside these ranges and needn't reach their ends.
Inputs may be any that keep to these rules, and one draw needn't show every extreme that they name: `lengths`: some frame has all 1536 tokens valid.
All inputs are finite; a program needn't handle non-finite values.
Results may differ from the reference program's by a relative error of at most 0.0057.
Values may be sent and summed in bfloat16 or wider, within the bound.
No kernel may reach another device: no remote copies, remote signals or barrier semaphores. Data moves between devices by JAX's collectives and lax.ppermute only.
A program may use at most 192 MiB of HBM per device.

```python
import math
import jax
import jax.numpy as jnp
from jax import lax

D = 1024
HS = 64
HEADS = 16
FT = 1536
FRAMES = 16
TOKENS = 24576


def rough_normal(key, salt):
    base = jnp.clip(jax.random.normal(jax.random.fold_in(key, salt), (TOKENS, D)), -6.0, 6.0)
    return base


def pack_heads(flat):
    heads_count = D // HS
    return jnp.transpose(flat.reshape(TOKENS, heads_count, HS), (1, 0, 2)).reshape(heads_count, TOKENS // 2, 2 * HS)


def draw_query_proj(key, part):
    base = rough_normal(key, 11)
    return pack_heads(base).astype(jnp.bfloat16)


def draw_key_proj(key, part):
    base = rough_normal(key, 21)
    return pack_heads(base).astype(jnp.bfloat16)


def draw_lengths(key, part):
    counts = jax.random.randint(jax.random.fold_in(key, 3), (FRAMES,), FT // 4, FT + 1)
    full_frame = jax.random.randint(jax.random.fold_in(key, 4), (), 0, FRAMES)
    return jnp.where(jnp.arange(FRAMES) == full_frame, FT, counts).astype(jnp.int32)


def shard_levels(stream_key, dims, cuts, smallest, top_value):
    level, own = 1.0, jax.random.fold_in(stream_key, 6)
    for position, blocks in cuts:
        draws = jnp.exp(jax.random.uniform(jax.random.fold_in(own, position), (blocks,), jnp.float32, smallest / len(cuts), top_value / len(cuts)))
        level = level * jnp.repeat(draws, dims[position] // blocks).reshape([-1 if axis == position else 1 for axis in range(len(dims))])
    return level


def normal_values(rng, extent, scale, reach, split=(), held_as=jnp.bfloat16):
    factor_of = shard_levels(rng, extent, split, -0.22, 0.18) if split else 1.0
    drawn = jax.random.normal(rng, extent, jnp.float32) * scale * factor_of
    return jnp.minimum(jnp.maximum(drawn, -reach), reach).astype(held_as)


def setup_inputs(seed: int = 0) -> dict:
    key_list = jax.random.split(jax.random.key(seed), 6)
    return {
        "query_proj": draw_query_proj(jax.random.fold_in(key_list[5], 71), 0),
        "key_proj": draw_key_proj(jax.random.fold_in(key_list[5], 71), 0),
        "value_proj": normal_values(key_list[2], (HEADS, TOKENS // 2, 2 * HS), 1.0, 6.0, ((0, 4), (1, 8))),
        "lengths": draw_lengths(jax.random.fold_in(key_list[5], 71), 0),
        "out_weight": normal_values(key_list[4], (D, D), D ** -0.5, 0.1875, ((0, 4),)),
    }


def to_grid(packed):
    heads_count = D // HS
    return jnp.transpose(packed.reshape(heads_count, FRAMES, FT, HS), (1, 2, 0, 3))

def reference(query_proj, key_proj, value_proj, lengths, out_weight):
    heads_count = D // HS
    score_scale = 1.0 / math.sqrt(HS)
    strides = (0, 1, 4, 16)
    query_grid = to_grid(query_proj)
    key_grid = to_grid(key_proj)
    value_grid = to_grid(value_proj)
    positions = jnp.arange(FT, dtype=jnp.int32)

    def one_frame(frame_id):
        sources = [(frame_id - stride_len).astype(jnp.int32) for stride_len in strides]
        clipped = [jnp.maximum(source, 0).astype(jnp.int32) for source in sources]
        key_block = jnp.concatenate([lax.dynamic_index_in_dim(key_grid, where_at, 0, keepdims=False) for where_at in clipped], 0)
        value_block = jnp.concatenate([lax.dynamic_index_in_dim(value_grid, where_at, 0, keepdims=False) for where_at in clipped], 0)
        key_valid = jnp.concatenate([(positions < lengths[where_at]) & (source >= 0) for source, where_at in zip(sources, clipped)], 0)
        frame_queries = lax.dynamic_index_in_dim(query_grid, frame_id, 0, keepdims=False)

        def one_head(head_id):
            head_queries = lax.dynamic_index_in_dim(frame_queries, head_id, 1, keepdims=False)
            head_keys = lax.dynamic_index_in_dim(key_block, head_id, 1, keepdims=False)
            head_values = lax.dynamic_index_in_dim(value_block, head_id, 1, keepdims=False)
            scores = jnp.dot(head_queries, head_keys.T, preferred_element_type=jnp.float32) * score_scale
            scores = jnp.where(key_valid[None, :], scores, -jnp.inf)
            top_score = lax.optimization_barrier(jnp.max(scores, axis=1, keepdims=True))
            expon = jnp.where(key_valid[None, :], jnp.exp(scores - top_score), 0.0)
            weights = (expon / lax.optimization_barrier(jnp.sum(expon, axis=1, keepdims=True))).astype(jnp.bfloat16)
            return jnp.dot(weights, head_values, preferred_element_type=jnp.float32).astype(jnp.bfloat16)
        results = lax.map(one_head, jnp.arange(heads_count, dtype=jnp.int32))
        return jnp.transpose(results, (1, 0, 2)).reshape(FT, D)
    attended = lax.map(one_frame, jnp.arange(FRAMES, dtype=jnp.int32)).reshape(TOKENS, D)
    return jnp.dot(attended, out_weight, preferred_element_type=jnp.float32).astype(jnp.bfloat16)
```

```python
import functools
import math

import jax
import jax.numpy as jnp
from jax import lax
from jax.experimental import pallas as pl
from jax.experimental.pallas import tpu as pltpu
from jax.sharding import PartitionSpec as P

LANES = 128
STRIDES = (0, 1, 4, 16)
VMEM = 48 * 1024 * 1024
LOW = -1e30


def swapped(x):
    return pltpu.roll(x, LANES // 2, 1)


def left_half(rows):
    return lax.broadcasted_iota(jnp.int32, (rows, LANES), 1) < LANES // 2


def split_queries(q_ref, q2_ref, scale):
    pairs = q_ref.shape[0]
    scaled = q_ref[...].astype(jnp.float32) * scale
    high = scaled.astype(jnp.bfloat16).astype(jnp.float32)
    low = scaled - high
    left = left_half(pairs)
    q2_ref[:pairs] = jnp.where(left, high, swapped(low)).astype(jnp.bfloat16)
    q2_ref[pairs:] = jnp.where(left, swapped(high), low).astype(jnp.bfloat16)


def key_rows(k_ref, start, pairs):
    block = k_ref[pl.ds(start, pairs), :].astype(jnp.float32)
    turned = swapped(block)
    left = left_half(pairs)
    even = jnp.where(left, block, turned)
    odd = jnp.where(left, turned, block)
    return jnp.concatenate([even, odd], axis=0).astype(jnp.bfloat16)


def value_rows(v_ref, start, pairs, count):
    block = v_ref[pl.ds(start, pairs), :].astype(jnp.float32)
    turned = swapped(block)
    lane = lax.broadcasted_iota(jnp.int32, (pairs, LANES), 1)
    token = 2 * (start + lax.broadcasted_iota(jnp.int32, (pairs, LANES), 0))
    left = lane < LANES // 2
    ones = (lane < 3 * LANES // 4).astype(jnp.float32)
    even = jnp.where(token < count, jnp.where(left, block, ones), 0.0)
    odd = jnp.where(token + 1 < count, jnp.where(left, turned, ones), 0.0)
    return jnp.concatenate([even, odd], axis=0).astype(jnp.bfloat16)


def over_tiles(count, pairs, step, body):
    half = step // 2
    halves = (count + 2 * half - 1) // (2 * half)
    whole = halves // 2

    def one(i, carry):
        body(pl.multiple_of(i * step, step), step)
        return carry

    lax.fori_loop(0, whole, one, 0)

    @pl.when(halves % 2 == 1)
    def _():
        body(pl.multiple_of(whole * step, step), half)


def scores_of(q2_ref, keys, at, rows):
    return lax.dot_general(
        q2_ref[pl.ds(at, rows), :], keys, (((1,), (1,)), ((), ())), preferred_element_type=jnp.float32
    )


def attend_kernel(slots, scale, step, chunk, has_state, final, meta_ref, q_ref, *refs):
    sources = len(slots)
    k_refs, v_refs = refs[:sources], refs[sources : 2 * sources]
    refs = refs[2 * sources :]
    if has_state:
        state_ref, refs = refs[0], refs[1:]
    out_ref, q2_ref, acc_ref = refs
    pairs = q_ref.shape[0]
    tokens = 2 * pairs

    split_queries(q_ref, q2_ref, scale)
    if has_state:
        acc_ref[...] = state_ref[...]
    else:
        acc_ref[...] = jnp.zeros_like(acc_ref)

    largest = None
    for k_ref in k_refs:
        top = jnp.max(jnp.abs(k_ref[...]).astype(jnp.float32), axis=0, keepdims=True)
        largest = top if largest is None else jnp.maximum(largest, top)
    largest = jnp.maximum(largest, swapped(jnp.broadcast_to(largest, (8, LANES)))[:1])
    weighted = jnp.abs(q_ref[...].astype(jnp.float32)) * largest
    row = lax.broadcasted_iota(jnp.int32, (LANES, LANES), 0) < LANES // 2
    col = lax.broadcasted_iota(jnp.int32, (LANES, LANES), 1) < LANES // 2
    same = (row == col).astype(jnp.bfloat16)
    bound = jnp.max(jnp.dot(weighted.astype(jnp.bfloat16), same, preferred_element_type=jnp.float32)) * scale
    safe = bound * 1.02 < 100.0
    if has_state:
        safe = safe & (jnp.max(jnp.abs(acc_ref[:, LANES - 8 :])) == 0.0)

    @pl.when(safe)
    def _():
        for slot, k_ref, v_ref in zip(slots, k_refs, v_refs):
            count = meta_ref[slot]

            def body(start, width, k_ref=k_ref, v_ref=v_ref, count=count):
                keys = key_rows(k_ref, start, width)
                values = value_rows(v_ref, start, width, count)
                scores = scores_of(q2_ref, keys, 0, chunk)
                for at in range(0, tokens, chunk):
                    later = scores_of(q2_ref, keys, at + chunk, chunk) if at + chunk < tokens else None
                    weights = jnp.exp2(scores).astype(jnp.bfloat16)
                    acc_ref[pl.ds(at, chunk), :] += jnp.dot(weights, values, preferred_element_type=jnp.float32)
                    scores = later

            over_tiles(count, pairs, step, body)

    @pl.when(jnp.logical_not(safe))
    def _():
        if not has_state:
            acc_ref[...] = jnp.where(
                lax.broadcasted_iota(jnp.int32, acc_ref.shape, 1) >= 3 * LANES // 4, LOW, 0.0
            )
        rows = min(256, tokens)
        lane = lax.broadcasted_iota(jnp.int32, (rows, LANES), 1)
        for slot, k_ref, v_ref in zip(slots, k_refs, v_refs):
            count = meta_ref[slot]

            def body(start, width, k_ref=k_ref, v_ref=v_ref, count=count):
                keys = key_rows(k_ref, start, width)
                values = value_rows(v_ref, start, width, count)
                at_col = lax.broadcasted_iota(jnp.int32, (rows, 2 * width), 1)
                token = 2 * (start + jnp.where(at_col < width, at_col, at_col - width)) + (at_col >= width)

                def one(i, carry):
                    at = pl.multiple_of(i * rows, rows)
                    scores = jnp.where(token < count, scores_of(q2_ref, keys, at, rows), LOW)
                    old = acc_ref[pl.ds(at, rows), :]
                    before = old[:, LANES - 1 :]
                    top = jnp.maximum(before, jnp.max(scores, axis=1, keepdims=True))
                    weights = jnp.exp2(scores - top).astype(jnp.bfloat16)
                    added = jnp.dot(weights, values, preferred_element_type=jnp.float32)
                    acc_ref[pl.ds(at, rows), :] = jnp.where(
                        lane >= 3 * LANES // 4, top, old * jnp.exp2(before - top) + added
                    )
                    return carry

                lax.fori_loop(0, tokens // rows, one, 0)

            over_tiles(count, pairs, step, body)

    if final:
        lane = lax.broadcasted_iota(jnp.int32, (pairs, LANES), 1)

        def divided(rows):
            sums = jnp.where(lane < 3 * LANES // 4, rows, pltpu.roll(rows, LANES // 4, 1))
            return rows / swapped(sums)

        even, odd = divided(acc_ref[:pairs]), divided(acc_ref[pairs:])
        out_ref[...] = jnp.where(lane < LANES // 2, even, swapped(odd)).astype(out_ref.dtype).reshape(out_ref.shape)
    else:
        out_ref[...] = acc_ref[...]


def attend(meta, queries, within, sources, state, dests, name):
    heads = queries.shape[0]
    pairs = queries.shape[1] // 2
    head_size = LANES // 2
    scale = math.log2(math.e) / math.sqrt(head_size)
    step = min(256, pairs)
    chunk = min(512, 2 * pairs)
    in_specs = [pl.BlockSpec((None, pairs, LANES), lambda h, m: (h, within, 0))]
    arrays = [queries]
    for part in (1, 2):
        for source in sources:
            array, lead, half = source[part]
            if lead is None:
                spec = pl.BlockSpec((None, pairs, LANES), lambda h, m, half=half: (h, half, 0))
            else:
                spec = pl.BlockSpec(
                    (None, None, pairs, LANES), lambda h, m, half=half, lead=lead: (lead, h, half, 0)
                )
            in_specs.append(spec)
            arrays.append(array)
    state_spec = pl.BlockSpec((None, 2 * pairs, LANES), lambda h, m: (h, 0, 0))
    if state is not None:
        in_specs.append(state_spec)
        arrays.append(state)
    if dests is None:
        out_shape = jax.ShapeDtypeStruct((heads, 2 * pairs, LANES), jnp.float32)
        out_spec = state_spec
    else:
        out_shape = jax.ShapeDtypeStruct((dests, heads, pairs // dests, LANES), jnp.bfloat16)
        out_spec = pl.BlockSpec((dests, 1, pairs // dests, LANES), lambda h, m: (0, h, 0, 0))
    slots = tuple(source[0] for source in sources)
    work = heads * len(sources) * (2 * pairs) ** 2
    return pl.pallas_call(
        functools.partial(
            attend_kernel, slots, scale, step, chunk, state is not None, dests is not None
        ),
        out_shape=out_shape,
        grid_spec=pltpu.PrefetchScalarGridSpec(
            num_scalar_prefetch=1,
            grid=(heads,),
            in_specs=in_specs,
            out_specs=out_spec,
            scratch_shapes=[
                pltpu.VMEM((2 * pairs, LANES), jnp.bfloat16),
                pltpu.VMEM((2 * pairs, LANES), jnp.float32),
            ],
        ),
        compiler_params=pltpu.CompilerParams(vmem_limit_bytes=VMEM),
        cost_estimate=pl.CostEstimate(
            flops=work * 4 * head_size * 4, bytes_accessed=8 * heads * pairs * LANES * 2, transcendentals=work
        ),
        name=name,
    )(meta, *arrays)


def project_kernel(layout, rows, weight_ref, *refs):
    parts, out_ref = refs[:-1], refs[-1]
    lane = lax.broadcasted_iota(jnp.int32, (rows, LANES), 1) < LANES // 2
    even, odd = [], []
    for first in range(0, len(layout), 2):
        (p, s, k), (p2, s2, k2) = layout[first], layout[first + 1]
        a = parts[p][s, k].astype(jnp.float32)
        b = parts[p2][s2, k2].astype(jnp.float32)
        even.append(jnp.where(lane, a, swapped(b)).astype(jnp.bfloat16))
        odd.append(jnp.where(lane, swapped(a), b).astype(jnp.bfloat16))
    stacked = jnp.concatenate([jnp.concatenate(even, axis=1), jnp.concatenate(odd, axis=1)], axis=0)
    token = lax.broadcasted_iota(jnp.int32, (2 * rows, 2 * rows), 0)
    place = lax.broadcasted_iota(jnp.int32, (2 * rows, 2 * rows), 1)
    order = (place == token // 2 + (token % 2) * rows).astype(jnp.bfloat16)
    tokens = jnp.dot(order, stacked, preferred_element_type=jnp.float32).astype(jnp.bfloat16)
    out_ref[...] = jnp.dot(tokens, weight_ref[...], preferred_element_type=jnp.float32).astype(out_ref.dtype)


def project(parts, layout, weight):
    pairs = parts[0].shape[2]
    rows = LANES if pairs % LANES == 0 else pairs
    return pl.pallas_call(
        functools.partial(project_kernel, layout, rows),
        out_shape=jax.ShapeDtypeStruct((2 * pairs, weight.shape[1]), jnp.bfloat16),
        grid=(pairs // rows,),
        in_specs=[pl.BlockSpec(weight.shape, lambda i: (0, 0))]
        + [pl.BlockSpec((*part.shape[:2], rows, LANES), lambda i: (0, 0, i, 0)) for part in parts],
        out_specs=pl.BlockSpec((2 * rows, weight.shape[1]), lambda i: (i, 0)),
        compiler_params=pltpu.CompilerParams(vmem_limit_bytes=VMEM),
        name="project",
    )(weight, *parts)


def shifted(x, pairs):
    return lax.ppermute(x, "frame", pairs)


def shards(query_proj, key_proj, value_proj, lengths, out_weight):
    devices = lax.axis_size("frame")
    groups = lax.axis_size("head")
    index = lax.axis_index("frame")
    heads, rows, _ = query_proj.shape
    half = rows // 2
    frames = lengths.shape[0]
    weight = lax.all_gather(out_weight, "head", axis=0, tiled=True)

    odd = index % 2 == 1
    wanted = [2 * index + within - stride for within in range(2) for stride in STRIDES]
    wanted.append(jnp.where(odd, wanted[1], -1))
    wanted.append(jnp.where(odd, -1, wanted[1]))
    wanted = jnp.stack(wanted)
    table = jnp.arange(frames, dtype=jnp.int32)
    meta = jnp.sum(jnp.where(wanted[:, None] == table[None, :], lengths[None, :], 0), axis=1, dtype=jnp.int32)
    meta = jnp.minimum(meta, rows)

    last = jnp.stack((key_proj[:, half:], value_proj[:, half:]))
    first = jnp.stack((key_proj[:, :half], value_proj[:, :half]))
    by_two = [(i, i + 2) for i in range(devices - 2)]
    near_last = shifted(last, by_two)
    prev_odd = shifted(last, [(i, i + 1) for i in range(0, devices - 1, 2)])
    near_first = shifted(first, by_two)
    prev_even = shifted(near_last, [(i + 1, i) for i in range(2, devices - 1, 2)])

    def own(within):
        return (key_proj, None, within), (value_proj, None, within)

    def moved(array):
        return (array, 0, 0), (array, 1, 0)

    state_first = attend(meta, query_proj, 0, [(0, *own(0))], None, None, "first_own")
    state_last = attend(meta, query_proj, 1, [(4, *own(1)), (5, *own(0))], None, None, "last_own")
    sources_last = [(6, *moved(near_last))]
    sources_first = [(8, *moved(prev_odd)), (9, *moved(prev_even)), (2, *moved(near_first))]
    if devices > 8:
        by_eight = [(i, i + 8) for i in range(devices - 8)]
        sources_last.append((7, *moved(shifted(last, by_eight))))
        sources_first.append((3, *moved(shifted(first, by_eight))))
    dests = groups // 2
    out_last = attend(meta, query_proj, 1, sources_last, state_last, dests, "last_rest")
    out_first = attend(meta, query_proj, 0, sources_first, state_first, dests, "first_rest")
    out = jnp.concatenate((out_first, out_last), axis=0)
    got = lax.all_to_all(out, "head", split_axis=0, concat_axis=0, tiled=True)
    layout = tuple((0, head // heads, head % heads) for head in range(groups * heads))
    return project((got,), layout, weight)


def solution(mesh):
    return jax.shard_map(
        shards,
        mesh=mesh,
        in_specs=(
            P("head", "frame", None),
            P("head", "frame", None),
            P("head", "frame", None),
            P(),
            P("head", None),
        ),
        out_specs=P(("frame", "head"), None),
        check_vma=False,
    )
```

```python
import functools
import math

import jax
import jax.numpy as jnp
from jax import lax
from jax.experimental import pallas as pl
from jax.experimental.pallas import tpu as pltpu
from jax.sharding import PartitionSpec as P

LANES = 128
STRIDES = (0, 1, 4, 16)
VMEM = 40 * 1024 * 1024
LOW = -1e30
CHUNK = 512


def swapped(x):
    return pltpu.roll(x, LANES // 2, 1)


def left_half(rows):
    return lax.broadcasted_iota(jnp.int32, (rows, LANES), 1) < LANES // 2


def split_queries(queries, q2_ref, scale):
    pairs = queries.shape[0]
    scaled = queries * scale
    high = scaled.astype(jnp.bfloat16).astype(jnp.float32)
    low = scaled - high
    left = left_half(pairs)
    q2_ref[:pairs] = jnp.where(left, high, swapped(low)).astype(jnp.bfloat16)
    q2_ref[pairs:] = jnp.where(left, swapped(high), low).astype(jnp.bfloat16)


def unpack_keys(keys, out_ref, base, half):
    for at in range(0, keys.shape[0], half):
        block = keys[at : at + half].astype(jnp.float32)
        turned = swapped(block)
        left = left_half(half)
        row = base + 2 * at
        out_ref[row : row + half] = jnp.where(left, block, turned).astype(jnp.bfloat16)
        out_ref[row + half : row + 2 * half] = jnp.where(left, turned, block).astype(jnp.bfloat16)


def unpack_values(values, out_ref, base, half, count):
    lane = lax.broadcasted_iota(jnp.int32, (half, LANES), 1)
    left = lane < LANES // 2
    ones = (lane < 3 * LANES // 4).astype(jnp.float32)
    token = 2 * lax.broadcasted_iota(jnp.int32, (half, LANES), 0)
    for at in range(0, values.shape[0], half):
        block = values[at : at + half].astype(jnp.float32)
        turned = swapped(block)
        row = base + 2 * at
        even = jnp.where(token < count - 2 * at, jnp.where(left, block, ones), 0.0)
        odd = jnp.where(token < count - 2 * at - 1, jnp.where(left, turned, ones), 0.0)
        out_ref[row : row + half] = even.astype(jnp.bfloat16)
        out_ref[row + half : row + 2 * half] = odd.astype(jnp.bfloat16)


def scores_of(queries, keys):
    return lax.dot_general(queries, keys, (((1,), (1,)), ((), ())), preferred_element_type=jnp.float32)


def attend_kernel(sources, scale, half, chunk, has_state, final, meta_ref, q_ref, *refs):
    refs = list(refs)
    key_sets = [[refs.pop(0) for _ in range(ways)] for _, ways in sources]
    value_sets = [[refs.pop(0) for _ in range(ways)] for _, ways in sources]
    state_ref = refs.pop(0) if has_state else None
    if len(refs) > 6:
        refs.pop(0)
    out_ref, q2_ref, k2_ref, v2_ref, p_ref, acc_ref = refs
    if not final:
        acc_ref = out_ref
    pairs = q_ref.shape[0]
    tokens = 2 * pairs
    block = 2 * half
    spare = len(sources) * tokens

    def picked(ways):
        if len(ways) == 1:
            return ways[0][...]
        return jnp.where(meta_ref[meta_ref.shape[0] - 1] == 1, ways[0][...], ways[1][...])

    queries = q_ref[...].astype(jnp.float32)
    split_queries(queries, q2_ref, scale)
    counts = [meta_ref[slot] for slot, _ in sources]
    largest = None
    for at, (ways, count) in enumerate(zip(key_sets, counts)):
        keys = picked(ways)
        unpack_keys(keys, k2_ref, at * tokens, half)
        top = jnp.max(jnp.abs(keys).astype(jnp.float32), axis=0, keepdims=True)
        largest = top if largest is None else jnp.maximum(largest, top)
    for at, (ways, count) in enumerate(zip(value_sets, counts)):
        unpack_values(picked(ways), v2_ref, at * tokens, half, count)
    k2_ref[spare:] = jnp.zeros((block, LANES), jnp.bfloat16)
    v2_ref[spare:] = jnp.zeros((block, LANES), jnp.bfloat16)
    if has_state:
        acc_ref[...] = state_ref[...]
    else:
        acc_ref[...] = jnp.zeros(acc_ref.shape, acc_ref.dtype)

    largest = jnp.broadcast_to(largest, (8, LANES))
    largest = jnp.maximum(largest, swapped(largest))
    key_square = jnp.sum(jnp.where(left_half(8), largest * largest, 0.0)) * 0.125
    row = lax.broadcasted_iota(jnp.int32, (LANES, LANES), 0) < LANES // 2
    col = lax.broadcasted_iota(jnp.int32, (LANES, LANES), 1) < LANES // 2
    same = (row == col).astype(jnp.bfloat16)
    query_square = jnp.max(
        jnp.dot((queries * queries).astype(jnp.bfloat16), same, preferred_element_type=jnp.float32)
    )
    safe = query_square * key_square * (1.03 * scale * scale) < 1e4
    if has_state:
        safe = safe & (jnp.max(jnp.abs(state_ref[:, LANES - 8 :])) == 0.0)

    blocks = [(count + block - 1) // block for count in counts]

    def rows_of(index):
        place, rest = spare, index
        for at, number in enumerate(blocks):
            place = jnp.where((rest >= 0) & (rest < number), at * tokens + rest * block, place)
            rest = rest - number
        return pl.multiple_of(place, block)

    def tile(ref, index):
        first, second = rows_of(2 * index), rows_of(2 * index + 1)
        return jnp.concatenate([ref[pl.ds(first, block), :], ref[pl.ds(second, block), :]], axis=0)

    tiles = (sum(blocks) + 1) // 2

    @pl.when(safe & (tiles > 0))
    def _():
        def weigh(at, keys):
            scores = scores_of(q2_ref[at : at + chunk], keys)
            p_ref[at : at + chunk] = jnp.exp2(scores).astype(jnp.bfloat16)

        def add(at, values):
            acc_ref[at : at + chunk] += jnp.dot(
                p_ref[at : at + chunk], values, preferred_element_type=jnp.float32
            )

        first = tile(k2_ref, 0)
        for at in range(0, tokens, chunk):
            weigh(at, first)

        def one(index, carry):
            values, keys = tile(v2_ref, index - 1), tile(k2_ref, index)
            for at in range(0, tokens, chunk):
                add(at, values)
                weigh(at, keys)
            return carry

        lax.fori_loop(1, tiles, one, 0)
        last = tile(v2_ref, tiles - 1)
        for at in range(0, tokens, chunk):
            add(at, last)

    @pl.when(jnp.logical_not(safe))
    def _():
        if not has_state:
            acc_ref[...] = jnp.where(
                lax.broadcasted_iota(jnp.int32, acc_ref.shape, 1) >= 3 * LANES // 4, LOW, 0.0
            )
        rows = min(256, tokens)
        lane = lax.broadcasted_iota(jnp.int32, (rows, LANES), 1)
        col = lax.broadcasted_iota(jnp.int32, (rows, block), 1)
        token = jnp.where(col < half, 2 * col, 2 * (col - half) + 1)
        for at_source, (count, number) in enumerate(zip(counts, blocks)):

            def one(index, carry, at_source=at_source, count=count):
                place = pl.multiple_of(at_source * tokens + index * block, block)
                keys, values = k2_ref[pl.ds(place, block), :], v2_ref[pl.ds(place, block), :]

                def part(i, carry):
                    at = pl.multiple_of(i * rows, rows)
                    scores = scores_of(q2_ref[pl.ds(at, rows), :], keys)
                    scores = jnp.where(token < count - index * block, scores, LOW)
                    old = acc_ref[pl.ds(at, rows), :]
                    before = old[:, LANES - 1 :]
                    top = jnp.maximum(before, jnp.max(scores, axis=1, keepdims=True))
                    weights = jnp.exp2(scores - top).astype(jnp.bfloat16)
                    added = jnp.dot(weights, values, preferred_element_type=jnp.float32)
                    acc_ref[pl.ds(at, rows), :] = jnp.where(
                        lane >= 3 * LANES // 4, top, old * jnp.exp2(before - top) + added
                    )
                    return carry

                return lax.fori_loop(0, tokens // rows, part, carry)

            lax.fori_loop(0, number, one, 0)

    if final:
        lane = lax.broadcasted_iota(jnp.int32, (pairs, LANES), 1)
        left = lane < LANES // 2
        even, odd = acc_ref[:pairs], acc_ref[pairs:]
        own_sums = jnp.where(lane < 3 * LANES // 4, odd, pltpu.roll(odd, LANES // 4, 1))
        far_sums = swapped(jnp.where(lane < 3 * LANES // 4, even, pltpu.roll(even, LANES // 4, 1)))
        result = jnp.where(left, even, swapped(odd)) / jnp.where(left, far_sums, own_sums)
        out_ref[...] = result.astype(out_ref.dtype).reshape(out_ref.shape)


def attend(meta, queries, within, first_head, heads, sources, state, dests, out, name):
    pairs = queries.shape[1] // 2
    head_size = LANES // 2
    scale = math.log2(math.e) / math.sqrt(head_size)
    half = min(128, pairs)
    chunk = min(CHUNK, 2 * pairs)

    def spec(lead, part, start):
        if lead is None:
            return pl.BlockSpec((None, pairs, LANES), lambda h, m: (h + start, part, 0))
        return pl.BlockSpec((None, None, pairs, LANES), lambda h, m: (lead, h + start, part, 0))

    in_specs, arrays = [spec(None, within, first_head)], [queries]
    for part in (1, 2):
        for source in sources:
            for array, lead, part_of, start in source[part]:
                in_specs.append(spec(lead, part_of, start))
                arrays.append(array)
    if state is not None:
        in_specs.append(pl.BlockSpec((None, 2 * pairs, LANES), lambda h, m: (h + first_head, 0, 0)))
        arrays.append(state)
    aliases = {}
    if dests is None:
        out_shape = jax.ShapeDtypeStruct((heads, 2 * pairs, LANES), jnp.float32)
        out_spec = pl.BlockSpec((None, 2 * pairs, LANES), lambda h, m: (h, 0, 0))
    else:
        out_shape = jax.ShapeDtypeStruct((2 * dests, heads, pairs // dests, LANES), jnp.bfloat16)
        out_spec = pl.BlockSpec((dests, 1, pairs // dests, LANES), lambda h, m: (within, h, 0, 0))
        if out is not None:
            in_specs.append(pl.BlockSpec(memory_space=pl.ANY))
            aliases = {1 + len(arrays): 0}
            arrays.append(out)
    slots = tuple((source[0], len(source[1])) for source in sources)
    unpacked = len(sources) * 2 * pairs + 2 * half
    work = heads * len(sources) * (2 * pairs) ** 2
    return pl.pallas_call(
        functools.partial(attend_kernel, slots, scale, half, chunk, state is not None, dests is not None),
        out_shape=out_shape,
        grid_spec=pltpu.PrefetchScalarGridSpec(
            num_scalar_prefetch=1,
            grid=(heads,),
            in_specs=in_specs,
            out_specs=out_spec,
            scratch_shapes=[
                pltpu.VMEM((2 * pairs, LANES), jnp.bfloat16),
                pltpu.VMEM((unpacked, LANES), jnp.bfloat16),
                pltpu.VMEM((unpacked, LANES), jnp.bfloat16),
                pltpu.VMEM((2 * pairs, 4 * half), jnp.bfloat16),
                pltpu.VMEM((2 * pairs, LANES), jnp.float32),
            ],
        ),
        input_output_aliases=aliases,
        compiler_params=pltpu.CompilerParams(vmem_limit_bytes=VMEM),
        cost_estimate=pl.CostEstimate(
            flops=work * 4 * head_size * 4, bytes_accessed=8 * heads * pairs * LANES * 2, transcendentals=work
        ),
        name=name,
    )(meta, *arrays)


def project_kernel(layout, rows, weight_ref, *refs):
    parts, out_ref = refs[:-1], refs[-1]
    lane = lax.broadcasted_iota(jnp.int32, (rows, LANES), 1) < LANES // 2
    even, odd = [], []
    for first in range(0, len(layout), 2):
        (p, s, k), (p2, s2, k2) = layout[first], layout[first + 1]
        a = parts[p][s, k].astype(jnp.float32)
        b = parts[p2][s2, k2].astype(jnp.float32)
        even.append(jnp.where(lane, a, swapped(b)).astype(jnp.bfloat16))
        odd.append(jnp.where(lane, swapped(a), b).astype(jnp.bfloat16))
    stacked = jnp.concatenate([jnp.concatenate(even, axis=1), jnp.concatenate(odd, axis=1)], axis=0)
    token = lax.broadcasted_iota(jnp.int32, (2 * rows, 2 * rows), 0)
    place = lax.broadcasted_iota(jnp.int32, (2 * rows, 2 * rows), 1)
    order = (place == token // 2 + (token % 2) * rows).astype(jnp.bfloat16)
    tokens = jnp.dot(order, stacked, preferred_element_type=jnp.float32).astype(jnp.bfloat16)
    out_ref[...] = jnp.dot(tokens, weight_ref[...], preferred_element_type=jnp.float32).astype(out_ref.dtype)


def project(parts, layout, weight):
    pairs = parts[0].shape[2]
    rows = LANES if pairs % LANES == 0 else pairs
    return pl.pallas_call(
        functools.partial(project_kernel, layout, rows),
        out_shape=jax.ShapeDtypeStruct((2 * pairs, weight.shape[1]), jnp.bfloat16),
        grid=(pairs // rows,),
        in_specs=[pl.BlockSpec(weight.shape, lambda i: (0, 0))]
        + [pl.BlockSpec((*part.shape[:2], rows, LANES), lambda i: (0, 0, i, 0)) for part in parts],
        out_specs=pl.BlockSpec((2 * rows, weight.shape[1]), lambda i: (i, 0)),
        compiler_params=pltpu.CompilerParams(vmem_limit_bytes=VMEM + VMEM // 2),
        name="project",
    )(weight, *parts)


def shifted(x, pairs):
    return lax.ppermute(x, "frame", pairs)


def shards(query_proj, key_proj, value_proj, lengths, out_weight):
    devices = lax.axis_size("frame")
    groups = lax.axis_size("head")
    index = lax.axis_index("frame")
    heads, rows, _ = query_proj.shape
    half = rows // 2
    frames = lengths.shape[0]
    weight = lax.all_gather(out_weight, "head", axis=0, tiled=True)

    wanted = jnp.stack([2 * index + within - stride for within in range(2) for stride in STRIDES])
    table = jnp.arange(frames, dtype=jnp.int32)
    meta = jnp.sum(jnp.where(wanted[:, None] == table[None, :], lengths[None, :], 0), axis=1, dtype=jnp.int32)
    meta = jnp.concatenate((jnp.minimum(meta, rows), (index % 2).astype(jnp.int32)[None]))

    size = heads // 2 if heads % 2 == 0 else heads
    starts = range(0, heads, size)
    last = jnp.stack((key_proj[:, half:], value_proj[:, half:]))
    by_two = [(i, i + 2) for i in range(devices - 2)]
    near_last = shifted(last, by_two)
    prev_odd = shifted(last, [(i, i + 1) for i in range(0, devices - 1, 2)])
    near_first, prev_even = [], []
    for start in starts:
        cut = slice(start, start + size)
        near_first.append(shifted(jnp.stack((key_proj[cut, :half], value_proj[cut, :half])), by_two))
    for start in starts:
        prev_even.append(shifted(near_last[:, start : start + size], [(i + 1, i) for i in range(2, devices - 1, 2)]))
    far = None
    if devices > 8:
        both = jnp.stack((key_proj, value_proj))
        far = shifted(both, [(i, i + 8) for i in range(devices - 8)])

    def own(slot, within):
        return slot, [(key_proj, None, within, 0)], [(value_proj, None, within, 0)]

    def moved(slot, *ways):
        return slot, [(array, 0, part, start) for array, part, start in ways], [
            (array, 1, part, start) for array, part, start in ways
        ]

    state_first = attend(meta, query_proj, 0, 0, heads, [own(0, 0)], None, None, None, "first_own")
    state_last = attend(meta, query_proj, 1, 0, heads, [own(4, 1), own(5, 0)], None, None, None, "last_own")
    dests = groups // 2
    outs = []
    for start in starts:
        sources = [moved(6, (near_last, 0, start))]
        if far is not None:
            sources.append(moved(7, (far, 1, start)))
        outs.append(attend(meta, query_proj, 1, start, size, sources, state_last, dests, None, "last_rest"))
    got = []
    for number, start in enumerate(starts):
        sources = [
            moved(1, (prev_odd, 0, start), (prev_even[number], 0, 0)),
            moved(2, (near_first[number], 0, 0)),
        ]
        if far is not None:
            sources.append(moved(3, (far, 0, start)))
        out = attend(meta, query_proj, 0, start, size, sources, state_first, dests, outs[number], "first_rest")
        got.append(lax.all_to_all(out, "head", split_axis=0, concat_axis=0, tiled=True))
    layout = tuple(
        (head % heads // size, head // heads, head % heads % size) for head in range(groups * heads)
    )
    return project(got, layout, weight)


def solution(mesh):
    return jax.shard_map(
        shards,
        mesh=mesh,
        in_specs=(
            P("head", "frame", None),
            P("head", "frame", None),
            P("head", "frame", None),
            P(),
            P("head", None),
        ),
        out_specs=P(("frame", "head"), None),
        check_vma=False,
    )
```

```python
import functools
import math

import jax
import jax.numpy as jnp
from jax import lax
from jax.experimental import pallas as pl
from jax.experimental.pallas import tpu as pltpu
from jax.sharding import PartitionSpec as P

LANES = 128
STRIDES = (0, 1, 4, 16)
VMEM = 40 * 1024 * 1024
LOW = -1e30
CHUNK = 768


def swapped(x):
    return pltpu.roll(x, LANES // 2, 1)


def left_half(rows):
    return lax.broadcasted_iota(jnp.int32, (rows, LANES), 1) < LANES // 2


def unpack_queries(queries, left_ref, right_ref):
    pairs = queries.shape[0]
    left = left_half(pairs)
    turned = swapped(queries)
    zero = jnp.zeros_like(queries)
    left_ref[:pairs] = jnp.where(left, queries, zero)
    left_ref[pairs:] = jnp.where(left, turned, zero)
    right_ref[:pairs] = jnp.where(left, zero, turned)
    right_ref[pairs:] = jnp.where(left, zero, queries)


def unpack_values(values, even_ref, odd_ref, at, count, half):
    pairs = values.shape[0]
    lane = lax.broadcasted_iota(jnp.int32, (pairs, LANES), 1)
    left = lane < LANES // 2
    ones = (lane < 3 * LANES // 4).astype(values.dtype)
    even_ref[at : at + pairs] = jnp.where(left, values, ones)
    odd_ref[at : at + pairs] = jnp.where(left, swapped(values), ones)

    @pl.when(count % (2 * half) != 0)
    def _():
        start = pl.multiple_of(count // (2 * half) * half, half)
        token = 2 * (start + lax.broadcasted_iota(jnp.int32, (half, LANES), 0))
        rows = pl.ds(at + start, half)
        for ref, later in ((even_ref, 0), (odd_ref, 1)):
            block = ref[rows, :].astype(jnp.float32)
            ref[rows, :] = jnp.where(token + later < count, block, 0.0).astype(ref.dtype)


def scores_of(queries, keys):
    return lax.dot_general(queries, keys, (((1,), (1,)), ((), ())), preferred_element_type=jnp.float32)


def attend_kernel(sources, scale, half, chunk, has_state, final, meta_ref, q_ref, *refs):
    refs = list(refs)
    key_refs = [refs.pop(0) for _ in sources]
    value_refs = [refs.pop(0) for _ in sources]
    if has_state:
        state_ref, marks_ref = refs.pop(0), refs.pop(0)
    if final:
        if len(refs) > 8:
            refs.pop(0)
        out_ref = refs.pop(0)
    else:
        out_ref, mark_ref = refs.pop(0), refs.pop(0)
    left_ref, right_ref, k_ref, even_ref, odd_ref, p_ref, acc_ref = refs
    if not final:
        acc_ref = out_ref
    pairs = q_ref.shape[0]
    tokens = 2 * pairs
    block = 2 * half
    spare = len(sources) * pairs
    counts = [meta_ref[slot] for slot in sources]

    queries = q_ref[...]
    unpack_queries(queries, left_ref, right_ref)
    largest = None
    for at, key_ref in enumerate(key_refs):
        keys = key_ref[...]
        k_ref[at * pairs : (at + 1) * pairs] = keys
        top = jnp.max(jnp.abs(keys), axis=0, keepdims=True).astype(jnp.float32)
        largest = top if largest is None else jnp.maximum(largest, top)
    k_ref[spare:] = jnp.zeros((half, LANES), k_ref.dtype)
    even_ref[spare:] = jnp.zeros((half, LANES), even_ref.dtype)
    odd_ref[spare:] = jnp.zeros((half, LANES), odd_ref.dtype)
    acc_ref[...] = jnp.zeros(acc_ref.shape, acc_ref.dtype)

    largest = jnp.broadcast_to(largest, (8, LANES))
    largest = jnp.maximum(largest, swapped(largest))
    key_square = jnp.sum(jnp.where(left_half(8), largest * largest, 0.0)) * 0.125
    row = lax.broadcasted_iota(jnp.int32, (LANES, LANES), 0) < LANES // 2
    col = lax.broadcasted_iota(jnp.int32, (LANES, LANES), 1) < LANES // 2
    same = (row == col).astype(jnp.bfloat16)
    query_square = jnp.max(jnp.dot(queries * queries, same, preferred_element_type=jnp.float32))
    safe = query_square * key_square * (1.03 * scale * scale) < 1e4
    if has_state:
        safe = safe & (jnp.max(marks_ref[...]) == 0.0)
    for at, (value_ref, count) in enumerate(zip(value_refs, counts)):
        unpack_values(value_ref[...], even_ref, odd_ref, at * pairs, count, half)

    blocks = [(count + block - 1) // block for count in counts]

    def rows_of(index):
        place, rest = spare, index
        for at, number in enumerate(blocks):
            place = jnp.where((rest >= 0) & (rest < number), at * pairs + rest * half, place)
            rest = rest - number
        return pl.ds(pl.multiple_of(place, half), half)

    def keys_of(index):
        return jnp.concatenate([k_ref[rows_of(2 * index), :], k_ref[rows_of(2 * index + 1), :]], axis=0)

    def values_of(index):
        first, second = rows_of(2 * index), rows_of(2 * index + 1)
        return jnp.concatenate(
            [even_ref[first, :], even_ref[second, :], odd_ref[first, :], odd_ref[second, :]], axis=0
        )

    tiles = (sum(blocks) + 1) // 2

    @pl.when(safe & (tiles > 0))
    def _():
        def weigh(at, keys):
            for side, ref in enumerate((left_ref, right_ref)):
                scores = scores_of(ref[at : at + chunk], keys) * scale
                p_ref[at : at + chunk, side * block : (side + 1) * block] = jnp.exp2(scores).astype(jnp.bfloat16)

        def add(at, values):
            acc_ref[at : at + chunk] += jnp.dot(
                p_ref[at : at + chunk], values, preferred_element_type=jnp.float32
            )

        first = keys_of(0)
        for at in range(0, tokens, chunk):
            weigh(at, first)

        def one(index, carry):
            values, keys = values_of(index - 1), keys_of(index)
            for at in range(0, tokens, chunk):
                add(at, values)
                weigh(at, keys)
            return carry

        lax.fori_loop(1, tiles, one, 0)
        last = values_of(tiles - 1)
        for at in range(0, tokens, chunk):
            add(at, last)

    if not final:
        mark_ref[...] = jnp.broadcast_to(jnp.where(safe, 0.0, 1.0), mark_ref.shape)

    @pl.when(jnp.logical_not(safe))
    def _():
        if has_state:
            acc_ref[...] = state_ref[...]
        else:
            acc_ref[...] = jnp.where(
                lax.broadcasted_iota(jnp.int32, acc_ref.shape, 1) >= 3 * LANES // 4, LOW, 0.0
            )
        rows = min(256, tokens)
        lane = lax.broadcasted_iota(jnp.int32, (rows, LANES), 1)
        col = lax.broadcasted_iota(jnp.int32, (rows, block), 1)
        token = jnp.where(col < half, 2 * col, 2 * (col - half) + 1)
        for at_source, (count, number) in enumerate(zip(counts, blocks)):

            def one(index, carry, at_source=at_source, count=count):
                place = pl.ds(pl.multiple_of(at_source * pairs + index * half, half), half)
                keys = k_ref[place, :]
                values = jnp.concatenate([even_ref[place, :], odd_ref[place, :]], axis=0)

                def part(i, carry):
                    at = pl.ds(pl.multiple_of(i * rows, rows), rows)
                    scores = [scores_of(ref[at, :], keys) for ref in (left_ref, right_ref)]
                    scores = jnp.concatenate(scores, axis=1) * scale
                    scores = jnp.where(token < count - index * block, scores, LOW)
                    old = acc_ref[at, :]
                    before = old[:, LANES - 1 :]
                    top = jnp.maximum(before, jnp.max(scores, axis=1, keepdims=True))
                    weights = jnp.exp2(scores - top).astype(jnp.bfloat16)
                    added = jnp.dot(weights, values, preferred_element_type=jnp.float32)
                    acc_ref[at, :] = jnp.where(
                        lane >= 3 * LANES // 4, top, old * jnp.exp2(before - top) + added
                    )
                    return carry

                return lax.fori_loop(0, tokens // rows, part, carry)

            lax.fori_loop(0, number, one, 0)

    if final:
        lane = lax.broadcasted_iota(jnp.int32, (pairs, LANES), 1)
        left = lane < LANES // 2
        kept = jnp.where(safe, 1.0, 0.0) if has_state else None

        def total(start):
            rows = acc_ref[start : start + pairs]
            return rows + state_ref[start : start + pairs] * kept if has_state else rows

        even, odd = total(0), total(pairs)
        own_sums = jnp.where(lane < 3 * LANES // 4, odd, pltpu.roll(odd, LANES // 4, 1))
        far_sums = swapped(jnp.where(lane < 3 * LANES // 4, even, pltpu.roll(even, LANES // 4, 1)))
        result = jnp.where(left, even, swapped(odd)) / jnp.where(left, far_sums, own_sums)
        out_ref[...] = result.astype(out_ref.dtype).reshape(out_ref.shape)


def attend(meta, queries, within, first_head, heads, sources, state, dests, out, name):
    pairs = queries.shape[1] // 2
    head_size = LANES // 2
    scale = math.log2(math.e) / math.sqrt(head_size)
    half = min(128, pairs)
    chunk = min(CHUNK, 2 * pairs)

    def spec(lead, part, start):
        if lead is None:
            return pl.BlockSpec((None, pairs, LANES), lambda h, m: (h + start, part, 0))
        return pl.BlockSpec((None, None, pairs, LANES), lambda h, m: (lead, h + start, part, 0))

    in_specs, arrays = [spec(None, within, first_head)], [queries]
    for part in (1, 2):
        for source in sources:
            array, lead, part_of, start = source[part]
            in_specs.append(spec(lead, part_of, start))
            arrays.append(array)
    shapes = [(2 * pairs, LANES), (8, LANES)]
    if state is not None:
        sums, marks, start = state
        in_specs += [pl.BlockSpec((None, *shape), lambda h, m: (h + start, 0, 0)) for shape in shapes]
        arrays += [sums, marks]
    aliases = {}
    if dests is None:
        out_shape = [jax.ShapeDtypeStruct((heads, *shape), jnp.float32) for shape in shapes]
        out_spec = [pl.BlockSpec((None, *shape), lambda h, m: (h, 0, 0)) for shape in shapes]
    else:
        out_shape = jax.ShapeDtypeStruct((2 * dests, heads, pairs // dests, LANES), jnp.bfloat16)
        out_spec = pl.BlockSpec((dests, 1, pairs // dests, LANES), lambda h, m: (within, h, 0, 0))
        if out is not None:
            in_specs.append(pl.BlockSpec(memory_space=pl.ANY))
            aliases = {1 + len(arrays): 0}
            arrays.append(out)
    unpacked = len(sources) * pairs + half
    work = heads * len(sources) * (2 * pairs) ** 2
    return pl.pallas_call(
        functools.partial(
            attend_kernel,
            tuple(source[0] for source in sources),
            scale,
            half,
            chunk,
            state is not None,
            dests is not None,
        ),
        out_shape=out_shape,
        grid_spec=pltpu.PrefetchScalarGridSpec(
            num_scalar_prefetch=1,
            grid=(heads,),
            in_specs=in_specs,
            out_specs=out_spec,
            scratch_shapes=[
                pltpu.VMEM((2 * pairs, LANES), jnp.bfloat16),
                pltpu.VMEM((2 * pairs, LANES), jnp.bfloat16),
                pltpu.VMEM((unpacked, LANES), jnp.bfloat16),
                pltpu.VMEM((unpacked, LANES), jnp.bfloat16),
                pltpu.VMEM((unpacked, LANES), jnp.bfloat16),
                pltpu.VMEM((2 * pairs, 4 * half), jnp.bfloat16),
                pltpu.VMEM((2 * pairs, LANES), jnp.float32),
            ],
        ),
        input_output_aliases=aliases,
        compiler_params=pltpu.CompilerParams(vmem_limit_bytes=VMEM),
        cost_estimate=pl.CostEstimate(
            flops=work * 4 * head_size * 4, bytes_accessed=8 * heads * pairs * LANES * 2, transcendentals=work
        ),
        name=name,
    )(meta, *arrays)


def project_kernel(layout, rows, weight_ref, *refs):
    parts, out_ref = refs[:-1], refs[-1]
    lane = lax.broadcasted_iota(jnp.int32, (rows, LANES), 1) < LANES // 2
    even, odd = [], []
    for first in range(0, len(layout), 2):
        (p, s, k), (p2, s2, k2) = layout[first], layout[first + 1]
        a = parts[p][s, k].astype(jnp.float32)
        b = parts[p2][s2, k2].astype(jnp.float32)
        even.append(jnp.where(lane, a, swapped(b)).astype(jnp.bfloat16))
        odd.append(jnp.where(lane, swapped(a), b).astype(jnp.bfloat16))
    stacked = jnp.concatenate([jnp.concatenate(even, axis=1), jnp.concatenate(odd, axis=1)], axis=0)
    token = lax.broadcasted_iota(jnp.int32, (2 * rows, 2 * rows), 0)
    place = lax.broadcasted_iota(jnp.int32, (2 * rows, 2 * rows), 1)
    order = (place == token // 2 + (token % 2) * rows).astype(jnp.bfloat16)
    tokens = jnp.dot(order, stacked, preferred_element_type=jnp.float32).astype(jnp.bfloat16)
    out_ref[...] = jnp.dot(tokens, weight_ref[...], preferred_element_type=jnp.float32).astype(out_ref.dtype)


def project(parts, layout, weight):
    pairs = parts[0].shape[2]
    rows = LANES if pairs % LANES == 0 else pairs
    return pl.pallas_call(
        functools.partial(project_kernel, layout, rows),
        out_shape=jax.ShapeDtypeStruct((2 * pairs, weight.shape[1]), jnp.bfloat16),
        grid=(pairs // rows,),
        in_specs=[pl.BlockSpec(weight.shape, lambda i: (0, 0))]
        + [pl.BlockSpec((*part.shape[:2], rows, LANES), lambda i: (0, 0, i, 0)) for part in parts],
        out_specs=pl.BlockSpec((2 * rows, weight.shape[1]), lambda i: (i, 0)),
        compiler_params=pltpu.CompilerParams(vmem_limit_bytes=VMEM + VMEM // 2),
        name="project",
    )(weight, *parts)


def shifted(x, pairs):
    return lax.ppermute(x, "frame", pairs)


def shards(query_proj, key_proj, value_proj, lengths, out_weight):
    devices = lax.axis_size("frame")
    groups = lax.axis_size("head")
    index = lax.axis_index("frame")
    heads, rows, _ = query_proj.shape
    half = rows // 2
    frames = lengths.shape[0]
    weight = lax.all_gather(out_weight, "head", axis=0, tiled=True)

    wanted = jnp.stack([2 * index + within - stride for within in range(2) for stride in STRIDES])
    table = jnp.arange(frames, dtype=jnp.int32)
    meta = jnp.sum(jnp.where(wanted[:, None] == table[None, :], lengths[None, :], 0), axis=1, dtype=jnp.int32)
    meta = jnp.minimum(meta, rows)

    size = heads // 2 if heads % 2 == 0 else heads
    starts = range(0, heads, size)
    last = jnp.stack((key_proj[:, half:], value_proj[:, half:]))
    first = jnp.stack((key_proj[:, :half], value_proj[:, :half]))
    by_two = [(i, i + 2) for i in range(devices - 2)]
    near_last = shifted(last, by_two)
    near_first = shifted(first, by_two)
    far = None
    if devices > 8:
        both = jnp.stack((key_proj, value_proj))
        far = shifted(both, [(i, i + 8) for i in range(devices - 8)])

    def own(slot, within):
        return slot, (key_proj, None, within, 0), (value_proj, None, within, 0)

    def moved(slot, array, part, start):
        return slot, (array, 0, part, start), (array, 1, part, start)

    sums_first, marks_first = attend(meta, query_proj, 0, 0, heads, [own(0, 0)], None, None, None, "first_own")
    state_last = []
    for start in starts:
        sources = [
            (4, (key_proj, None, 1, start), (value_proj, None, 1, start)),
            (5, (key_proj, None, 0, start), (value_proj, None, 0, start)),
        ]
        if start != starts[-1]:
            sums, marks = attend(meta, query_proj, 1, start, size, sources, None, None, None, "last_own")
            state_last.append((sums, marks, 0))
        else:
            near_last, held = lax.optimization_barrier((near_last, query_proj))
            sums, marks = attend(meta, held, 1, start, size, sources, None, None, None, "last_own")
            state_last.append((sums, marks, 0))
    to_even = [(i + 1, i) for i in range(2, devices - 1, 2)]
    to_odd = [(i, i + 1) for i in range(0, devices - 1, 2)]
    prev = shifted(jnp.where(index % 2 == 0, last, near_last), to_even + to_odd)
    dests = groups // 2
    outs = []
    for number, start in enumerate(starts):
        sources = [moved(6, near_last, 0, start)]
        if far is not None:
            sources.append(moved(7, far, 1, start))
        outs.append(attend(meta, query_proj, 1, start, size, sources, state_last[number], dests, None, "last_rest"))
    got = []
    for number, start in enumerate(starts):
        sources = [moved(1, prev, 0, start), moved(2, near_first, 0, start)]
        if far is not None:
            sources.append(moved(3, far, 0, start))
        state = (sums_first, marks_first, start)
        out = attend(meta, query_proj, 0, start, size, sources, state, dests, outs[number], "first_rest")
        got.append(lax.all_to_all(out, "head", split_axis=0, concat_axis=0, tiled=True))
    layout = tuple(
        (head % heads // size, head // heads, head % heads % size) for head in range(groups * heads)
    )
    return project(got, layout, weight)


def solution(mesh):
    return jax.shard_map(
        shards,
        mesh=mesh,
        in_specs=(
            P("head", "frame", None),
            P("head", "frame", None),
            P("head", "frame", None),
            P(),
            P("head", None),
        ),
        out_specs=P(("frame", "head"), None),
        check_vma=False,
    )
```

```python
import functools
import math

import jax
import jax.numpy as jnp
from jax import lax
from jax.experimental import pallas as pl
from jax.experimental.pallas import tpu as pltpu
from jax.sharding import PartitionSpec as P

LANES = 128
STRIDES = (0, 1, 4, 16)
VMEM = 62 * 1024 * 1024
LOW = -1e30
CHUNK = 768


def swapped(x):
    return pltpu.roll(x, LANES // 2, 1)


def left_half(rows):
    return lax.broadcasted_iota(jnp.int32, (rows, LANES), 1) < LANES // 2


def unpack_queries(queries, left_ref, right_ref):
    pairs = queries.shape[0]
    left = left_half(pairs)
    turned = swapped(queries)
    zero = jnp.zeros_like(queries)
    left_ref[:pairs] = jnp.where(left, queries, zero)
    left_ref[pairs:] = jnp.where(left, turned, zero)
    right_ref[:pairs] = jnp.where(left, zero, turned)
    right_ref[pairs:] = jnp.where(left, zero, queries)


def unpack_values(values, even_ref, odd_ref, at, count, half):
    pairs = values.shape[0]
    lane = lax.broadcasted_iota(jnp.int32, (pairs, LANES), 1)
    left = lane < LANES // 2
    ones = (lane < 3 * LANES // 4).astype(values.dtype)
    even_ref[at : at + pairs] = jnp.where(left, values, ones)
    odd_ref[at : at + pairs] = jnp.where(left, swapped(values), ones)

    @pl.when(count % (2 * half) != 0)
    def _():
        start = pl.multiple_of(count // (2 * half) * half, half)
        token = 2 * (start + lax.broadcasted_iota(jnp.int32, (half, LANES), 0))
        rows = pl.ds(at + start, half)
        for ref, later in ((even_ref, 0), (odd_ref, 1)):
            block = ref[rows, :].astype(jnp.float32)
            ref[rows, :] = jnp.where(token + later < count, block, 0.0).astype(ref.dtype)


def scores_of(queries, keys):
    return lax.dot_general(queries, keys, (((1,), (1,)), ((), ())), preferred_element_type=jnp.float32)


def stats_out(out_ref, rows, at):
    pairs = rows[0].shape[0]
    lines = []
    for block in rows:
        turned = jnp.transpose(block)
        lines += [turned[:1], turned[LANES // 2 : LANES // 2 + 1]]
    whole = jnp.concatenate(lines, axis=0)
    parts = []
    for _ in range(3):
        part = whole.astype(jnp.bfloat16).astype(jnp.float32)
        parts.append(part)
        whole = whole - part
    parts.append(jnp.zeros_like(whole))
    packed = jnp.concatenate(parts, axis=0).astype(jnp.bfloat16)
    for place in range(0, pairs, LANES):
        row = at + place // LANES * 16
        out_ref[row : row + 16, :] = packed[:, place : place + LANES]


def stats_in(ref, pairs):
    packed = jnp.concatenate(
        [ref[pairs + at // LANES * 16 : pairs + at // LANES * 16 + 16, :] for at in range(0, pairs, LANES)], axis=1
    ).astype(jnp.float32)
    whole = packed[0:4] + packed[4:8] + packed[8:12]

    def spread(line):
        wide = [jnp.broadcast_to(whole[at : at + 1], (LANES // 2, pairs)) for at in (line, line + 1)]
        return jnp.transpose(jnp.concatenate(wide, axis=0))

    return spread(0), spread(2)


def attend_kernel(sources, scale, half, chunk, has_state, partials, mode, meta_ref, q_ref, *refs):
    refs = list(refs)
    key_refs = [refs.pop(0) for _ in sources]
    value_refs = [refs.pop(0) for _ in sources]
    if has_state:
        state_ref, marks_ref = refs.pop(0), refs.pop(0)
    partial_refs = [refs.pop(0) for _ in range(partials)]
    if len(refs) > (9 if mode == "state" else 8):
        refs.pop(0)
    out_ref = refs.pop(0)
    if mode == "state":
        mark_ref = refs.pop(0)
    left_ref, right_ref, k_ref, even_ref, odd_ref, p_ref, acc_ref = refs
    if mode == "state":
        acc_ref = out_ref
    pairs = q_ref.shape[0]
    tokens = 2 * pairs
    block = 2 * half
    spare = len(sources) * pairs
    counts = [meta_ref[slot] for slot in sources]

    queries = q_ref[...]
    unpack_queries(queries, left_ref, right_ref)
    largest = None
    for at, key_ref in enumerate(key_refs):
        keys = key_ref[...]
        k_ref[at * pairs : (at + 1) * pairs] = keys
        top = jnp.max(jnp.abs(keys), axis=0, keepdims=True).astype(jnp.float32)
        largest = top if largest is None else jnp.maximum(largest, top)
    k_ref[spare:] = jnp.zeros((half, LANES), k_ref.dtype)
    even_ref[spare:] = jnp.zeros((half, LANES), even_ref.dtype)
    odd_ref[spare:] = jnp.zeros((half, LANES), odd_ref.dtype)
    acc_ref[...] = jnp.zeros(acc_ref.shape, acc_ref.dtype)

    largest = jnp.broadcast_to(largest, (8, LANES))
    largest = jnp.maximum(largest, swapped(largest))
    key_square = jnp.sum(jnp.where(left_half(8), largest * largest, 0.0)) * 0.125
    row = lax.broadcasted_iota(jnp.int32, (LANES, LANES), 0) < LANES // 2
    col = lax.broadcasted_iota(jnp.int32, (LANES, LANES), 1) < LANES // 2
    same = (row == col).astype(jnp.bfloat16)
    query_square = jnp.max(jnp.dot(queries * queries, same, preferred_element_type=jnp.float32))
    safe = query_square * key_square * (1.03 * scale * scale) < 1e4
    if has_state:
        safe = safe & (jnp.max(marks_ref[...]) == 0.0)
    for at, (value_ref, count) in enumerate(zip(value_refs, counts)):
        unpack_values(value_ref[...], even_ref, odd_ref, at * pairs, count, half)

    blocks = [(count + block - 1) // block for count in counts]

    def rows_of(index):
        place, rest = spare, index
        for at, number in enumerate(blocks):
            place = jnp.where((rest >= 0) & (rest < number), at * pairs + rest * half, place)
            rest = rest - number
        return pl.ds(pl.multiple_of(place, half), half)

    def keys_of(index):
        return jnp.concatenate([k_ref[rows_of(2 * index), :], k_ref[rows_of(2 * index + 1), :]], axis=0)

    def values_of(index):
        first, second = rows_of(2 * index), rows_of(2 * index + 1)
        return jnp.concatenate(
            [even_ref[first, :], even_ref[second, :], odd_ref[first, :], odd_ref[second, :]], axis=0
        )

    tiles = (sum(blocks) + 1) // 2

    @pl.when(safe & (tiles > 0))
    def _():
        def weigh(at, keys):
            for side, ref in enumerate((left_ref, right_ref)):
                scores = scores_of(ref[at : at + chunk], keys) * scale
                p_ref[at : at + chunk, side * block : (side + 1) * block] = jnp.exp2(scores).astype(jnp.bfloat16)

        def add(at, values):
            acc_ref[at : at + chunk] += jnp.dot(
                p_ref[at : at + chunk], values, preferred_element_type=jnp.float32
            )

        first = keys_of(0)
        for at in range(0, tokens, chunk):
            weigh(at, first)

        def one(index, carry):
            values, keys = values_of(index - 1), keys_of(index)
            for at in range(0, tokens, chunk):
                add(at, values)
                weigh(at, keys)
            return carry

        lax.fori_loop(1, tiles, one, 0)
        last = values_of(tiles - 1)
        for at in range(0, tokens, chunk):
            add(at, last)

    if mode == "state":
        mark_ref[...] = jnp.broadcast_to(jnp.where(safe, 0.0, 1.0), mark_ref.shape)

    @pl.when(jnp.logical_not(safe))
    def _():
        if has_state:
            acc_ref[...] = state_ref[...]
        else:
            acc_ref[...] = jnp.where(
                lax.broadcasted_iota(jnp.int32, acc_ref.shape, 1) >= 3 * LANES // 4, LOW, 0.0
            )
        rows = min(256, tokens)
        lane = lax.broadcasted_iota(jnp.int32, (rows, LANES), 1)
        col = lax.broadcasted_iota(jnp.int32, (rows, block), 1)
        token = jnp.where(col < half, 2 * col, 2 * (col - half) + 1)
        for at_source, (count, number) in enumerate(zip(counts, blocks)):

            def one(index, carry, at_source=at_source, count=count):
                place = pl.ds(pl.multiple_of(at_source * pairs + index * half, half), half)
                keys = k_ref[place, :]
                values = jnp.concatenate([even_ref[place, :], odd_ref[place, :]], axis=0)

                def part(i, carry):
                    at = pl.ds(pl.multiple_of(i * rows, rows), rows)
                    scores = [scores_of(ref[at, :], keys) for ref in (left_ref, right_ref)]
                    scores = jnp.concatenate(scores, axis=1) * scale
                    scores = jnp.where(token < count - index * block, scores, LOW)
                    old = acc_ref[at, :]
                    before = old[:, LANES - 1 :]
                    top = jnp.maximum(before, jnp.max(scores, axis=1, keepdims=True))
                    weights = jnp.exp2(scores - top).astype(jnp.bfloat16)
                    added = jnp.dot(weights, values, preferred_element_type=jnp.float32)
                    acc_ref[at, :] = jnp.where(
                        lane >= 3 * LANES // 4, top, old * jnp.exp2(before - top) + added
                    )
                    return carry

                return lax.fori_loop(0, tokens // rows, part, carry)

            lax.fori_loop(0, number, one, 0)

    if mode == "state":
        return

    lane = lax.broadcasted_iota(jnp.int32, (pairs, LANES), 1)
    left = lane < LANES // 2
    sums_lane = lane < 3 * LANES // 4
    if has_state:
        kept = jnp.where(safe, 1.0, 0.0)
        even = acc_ref[:pairs] + state_ref[:pairs] * kept
        odd = acc_ref[pairs:] + state_ref[pairs:] * kept
    else:
        even, odd = acc_ref[:pairs], acc_ref[pairs:]
    even_turned, odd_turned = pltpu.roll(even, LANES // 4, 1), pltpu.roll(odd, LANES // 4, 1)
    sums = jnp.where(left, swapped(jnp.where(sums_lane, even, even_turned)), jnp.where(sums_lane, odd, odd_turned))
    result = jnp.where(left, even, swapped(odd))
    if mode == "partial" or partials:
        even_turned, odd_turned = pltpu.roll(even, 3 * LANES // 4, 1), pltpu.roll(odd, 3 * LANES // 4, 1)
        shifts = jnp.where(left, swapped(jnp.where(sums_lane, even_turned, even)), jnp.where(sums_lane, odd_turned, odd))
    if mode == "partial":
        present = sums > 0.0
        result = jnp.where(present, result / jnp.where(present, sums, 1.0), 0.0)
        out_ref[:pairs] = result.astype(out_ref.dtype)
        stats_out(out_ref, (sums, shifts), pairs)
        return
    if partials:
        others = []
        top = shifts
        for ref in partial_refs:
            other_sums, other_shifts = stats_in(ref, pairs)
            other_shifts = jnp.where(other_sums > 0.0, other_shifts, LOW)
            others.append((ref[:pairs].astype(jnp.float32), other_sums, other_shifts))
            top = jnp.maximum(top, other_shifts)
        factor = jnp.exp2(shifts - top)
        result, sums = result * factor, sums * factor
        for values, other_sums, other_shifts in others:
            share = other_sums * jnp.exp2(other_shifts - top)
            result, sums = result + values * share, sums + share
    out_ref[...] = (result / sums).astype(out_ref.dtype).reshape(out_ref.shape)


def attend(meta, queries, first_head, heads, sources, mode, name, state=None, partials=(), dests=None, within=0, out=None):
    pairs = queries[0].shape[1] // queries[2]
    head_size = LANES // 2
    scale = math.log2(math.e) / math.sqrt(head_size)
    half = min(128, pairs)
    chunk = min(CHUNK, 2 * pairs)
    extra = 16 * pairs // LANES

    def spec(lead, part, start, rows=pairs):
        if lead is None:
            return pl.BlockSpec((None, rows, LANES), lambda h, m: (h + start, part, 0))
        return pl.BlockSpec((None, None, rows, LANES), lambda h, m: (lead, h + start, part, 0))

    in_specs, arrays = [spec(None, queries[1], first_head)], [queries[0]]
    for part in (1, 2):
        for source in sources:
            array, lead, part_of, start = source[part]
            in_specs.append(spec(lead, part_of, start))
            arrays.append(array)
    shapes = [(2 * pairs, LANES), (8, LANES)]
    if state is not None:
        sums, marks, start = state
        in_specs += [pl.BlockSpec((None, *shape), lambda h, m: (h + start, 0, 0)) for shape in shapes]
        arrays += [sums, marks]
    for array in partials:
        in_specs.append(spec(None, 0, first_head, pairs + extra))
        arrays.append(array)
    aliases = {}
    if mode == "state":
        out_shape = [jax.ShapeDtypeStruct((heads, *shape), jnp.float32) for shape in shapes]
        out_spec = [pl.BlockSpec((None, *shape), lambda h, m: (h, 0, 0)) for shape in shapes]
    elif mode == "partial":
        out_shape = jax.ShapeDtypeStruct((heads, pairs + extra, LANES), jnp.bfloat16)
        out_spec = pl.BlockSpec((None, pairs + extra, LANES), lambda h, m: (h, 0, 0))
    else:
        out_shape = jax.ShapeDtypeStruct((2 * dests, heads, pairs // dests, LANES), jnp.bfloat16)
        out_spec = pl.BlockSpec((dests, 1, pairs // dests, LANES), lambda h, m: (within, h, 0, 0))
        if out is not None:
            in_specs.append(pl.BlockSpec(memory_space=pl.ANY))
            aliases = {1 + len(arrays): 0}
            arrays.append(out)
    unpacked = len(sources) * pairs + half
    work = heads * len(sources) * (2 * pairs) ** 2
    return pl.pallas_call(
        functools.partial(
            attend_kernel,
            tuple(source[0] for source in sources),
            scale,
            half,
            chunk,
            state is not None,
            len(partials),
            mode,
        ),
        out_shape=out_shape,
        grid_spec=pltpu.PrefetchScalarGridSpec(
            num_scalar_prefetch=1,
            grid=(heads,),
            in_specs=in_specs,
            out_specs=out_spec,
            scratch_shapes=[
                pltpu.VMEM((2 * pairs, LANES), jnp.bfloat16),
                pltpu.VMEM((2 * pairs, LANES), jnp.bfloat16),
                pltpu.VMEM((unpacked, LANES), jnp.bfloat16),
                pltpu.VMEM((unpacked, LANES), jnp.bfloat16),
                pltpu.VMEM((unpacked, LANES), jnp.bfloat16),
                pltpu.VMEM((2 * pairs, 4 * half), jnp.bfloat16),
                pltpu.VMEM((2 * pairs, LANES), jnp.float32),
            ],
        ),
        input_output_aliases=aliases,
        compiler_params=pltpu.CompilerParams(vmem_limit_bytes=VMEM),
        cost_estimate=pl.CostEstimate(
            flops=work * 4 * head_size * 4, bytes_accessed=8 * heads * pairs * LANES * 2, transcendentals=work
        ),
        name=name,
    )(meta, *arrays)


def project_kernel(layout, rows, weight_ref, *refs):
    parts, out_ref = refs[:-1], refs[-1]
    lane = lax.broadcasted_iota(jnp.int32, (rows, LANES), 1) < LANES // 2
    even, odd = [], []
    for first in range(0, len(layout), 2):
        (p, s, k), (p2, s2, k2) = layout[first], layout[first + 1]
        a = parts[p][s, k].astype(jnp.float32)
        b = parts[p2][s2, k2].astype(jnp.float32)
        even.append(jnp.where(lane, a, swapped(b)).astype(jnp.bfloat16))
        odd.append(jnp.where(lane, swapped(a), b).astype(jnp.bfloat16))
    stacked = jnp.concatenate([jnp.concatenate(even, axis=1), jnp.concatenate(odd, axis=1)], axis=0)
    token = lax.broadcasted_iota(jnp.int32, (2 * rows, 2 * rows), 0)
    place = lax.broadcasted_iota(jnp.int32, (2 * rows, 2 * rows), 1)
    order = (place == token // 2 + (token % 2) * rows).astype(jnp.bfloat16)
    tokens = jnp.dot(order, stacked, preferred_element_type=jnp.float32).astype(jnp.bfloat16)
    out_ref[...] = jnp.dot(tokens, weight_ref[...], preferred_element_type=jnp.float32).astype(out_ref.dtype)


def project(parts, layout, weight):
    pairs = parts[0].shape[2]
    rows = LANES if pairs % LANES == 0 else pairs
    return pl.pallas_call(
        functools.partial(project_kernel, layout, rows),
        out_shape=jax.ShapeDtypeStruct((2 * pairs, weight.shape[1]), jnp.bfloat16),
        grid=(pairs // rows,),
        in_specs=[pl.BlockSpec(weight.shape, lambda i: (0, 0))]
        + [pl.BlockSpec((*part.shape[:2], rows, LANES), lambda i: (0, 0, i, 0)) for part in parts],
        out_specs=pl.BlockSpec((2 * rows, weight.shape[1]), lambda i: (i, 0)),
        compiler_params=pltpu.CompilerParams(vmem_limit_bytes=VMEM),
        name="project",
    )(weight, *parts)


def shifted(x, pairs):
    return lax.ppermute(x, "frame", pairs)


def shards(query_proj, key_proj, value_proj, lengths, out_weight):
    devices = lax.axis_size("frame")
    groups = lax.axis_size("head")
    index = lax.axis_index("frame")
    heads, rows, _ = query_proj.shape
    half = rows // 2
    frames = lengths.shape[0]
    weight = lax.all_gather(out_weight, "head", axis=0, tiled=True)

    even = index % 2 == 0
    first_frame = 2 * index
    wanted = [first_frame, first_frame + 1]
    wanted += [first_frame + within - stride for stride in STRIDES[2:] for within in range(2)]
    wanted.append(jnp.where(first_frame + STRIDES[2] < frames, first_frame, -1))
    wanted.append(jnp.where(even, first_frame + 1, -1))
    wanted.append(jnp.where(even, -1, first_frame + 1 - STRIDES[2]))
    table = jnp.arange(frames, dtype=jnp.int32)
    meta = jnp.sum(jnp.where(jnp.stack(wanted)[:, None] == table[None, :], lengths[None, :], 0), axis=1, dtype=jnp.int32)
    meta = jnp.minimum(meta, rows)

    last = jnp.stack((key_proj[:, half:], value_proj[:, half:]))
    last, held = lax.optimization_barrier((last, query_proj))
    first_queries = held[:, :half]
    ahead = [(i, i + 2) for i in range(devices - 2)]
    back = [(i + 2, i) for i in range(devices - 2)]
    there = [(i + 1, i) for i in range(0, devices - 1, 2)] + [(i, i + 1) for i in range(2, devices - 1, 2)]
    home = [(to, start) for start, to in there]
    near_last = shifted(last, ahead)
    far_queries = shifted(first_queries, back)
    pair_queries = shifted(first_queries, there)
    far = None
    if devices > 8:
        both = jnp.stack((key_proj, value_proj))
        far = shifted(both, [(i, i + 8) for i in range(devices - 8)])

    def own(slot, part, start):
        return slot, (key_proj, None, part, start), (value_proj, None, part, start)

    def moved(slot, array, part, start):
        return slot, (array, 0, part, start), (array, 1, part, start)

    size = heads // 2 if heads % 2 == 0 else heads
    starts = list(range(0, heads, size))
    states = {}
    if len(starts) > 1:
        sums, marks = attend(
            meta, (query_proj, 1, 2), 0, size, [own(1, 1, 0), own(0, 0, 0)], "state", "last_own"
        )
        states[0] = (sums, marks, 0)
        far_queries, marks = lax.optimization_barrier((far_queries, marks))
        states[0] = (sums, marks, 0)
    far_part = attend(meta, (far_queries, 0, 1), 0, heads, [own(6, 0, 0)], "partial", "far_part")
    far_back = shifted(far_part, ahead)
    pair_queries, _ = lax.optimization_barrier((pair_queries, far_part))
    pair_part = attend(
        meta, (pair_queries, 0, 1), 0, heads, [own(7, 1, 0), moved(8, near_last, 0, 0)], "partial", "pair_part"
    )
    pair_back = shifted(pair_part, home)
    near_last, _ = lax.optimization_barrier((near_last, pair_part))
    dests = groups // 2
    outs = []
    for start in starts:
        sources = [moved(3, near_last, 0, start)]
        if start not in states:
            sources += [own(1, 1, start), own(0, 0, start)]
        if far is not None:
            sources.append(moved(5, far, 1, start))
        outs.append(
            attend(
                meta, (query_proj, 1, 2), start, size, sources, "final", "last_rest",
                state=states.get(start), dests=dests, within=1,
            )
        )
    held, *outs = lax.optimization_barrier((query_proj, *outs))
    got = []
    for number, start in enumerate(starts):
        sources = [own(0, 0, start)]
        if far is not None:
            sources.append(moved(4, far, 0, start))
        out = attend(
            meta, (held, 0, 2), start, size, sources, "final", "first_rest",
            partials=(far_back, pair_back), dests=dests, within=0, out=outs[number],
        )
        got.append(lax.all_to_all(out, "head", split_axis=0, concat_axis=0, tiled=True))
    layout = tuple(
        (head % heads // size, head // heads, head % heads % size) for head in range(groups * heads)
    )
    return project(got, layout, weight)


def solution(mesh):
    return jax.shard_map(
        shards,
        mesh=mesh,
        in_specs=(
            P("head", "frame", None),
            P("head", "frame", None),
            P("head", "frame", None),
            P(),
            P("head", None),
        ),
        out_specs=P(("frame", "head"), None),
        check_vma=False,
    )
```

```python
import functools
import math

import jax
import jax.numpy as jnp
from jax import lax
from jax.experimental import pallas as pl
from jax.experimental.pallas import tpu as pltpu
from jax.sharding import PartitionSpec as P

LANES = 128
STRIDES = (0, 1, 4, 16)
VMEM = 62 * 1024 * 1024
LOW = -1e30
CHUNK = 1536


def swapped(x):
    return pltpu.roll(x, LANES // 2, 1)


def left_half(rows):
    return lax.broadcasted_iota(jnp.int32, (rows, LANES), 1) < LANES // 2


def unpack_values(values, even_ref, odd_ref, at, count, half, mask):
    pairs = values.shape[0]
    even_ref[at : at + pairs] = values * mask + (1 - mask)
    odd_ref[at : at + pairs] = swapped(values) * mask + (1 - mask)

    @pl.when(count % (2 * half) != 0)
    def _():
        start = pl.multiple_of(count // (2 * half) * half, half)
        token = 2 * (start + lax.broadcasted_iota(jnp.int32, (half, LANES), 0))
        rows = pl.ds(at + start, half)
        for ref, later in ((even_ref, 0), (odd_ref, 1)):
            block = ref[rows, :].astype(jnp.float32)
            ref[rows, :] = jnp.where(token + later < count, block, 0.0).astype(ref.dtype)


def scores_of(queries, keys):
    return lax.dot_general(queries, keys, (((1,), (1,)), ((), ())), preferred_element_type=jnp.float32)


def attend_kernel(slots, places, outs, scale, half, chunk, has_state, final, meta_ref, *refs):
    refs = list(refs)
    arrays = [refs.pop(0) for _ in places]
    number_out = len(outs)
    scratch = refs[-(len(places) + number_out + 7) :]
    out_arrays = refs[: -(len(places) + number_out + 7)][-number_out:]
    buffers = scratch[: len(places)]
    out_buffers = scratch[len(places) : len(places) + number_out]
    q2_ref, even_ref, odd_ref, p_ref, acc_scratch, top_ref, sems = scratch[len(places) + number_out :]
    heads = out_buffers[0].shape[0]
    pairs = buffers[0].shape[1]
    tokens = 2 * pairs
    block = 2 * half
    sources = len(slots)
    counts = [meta_ref[slot] for slot in slots]
    blocks = [(count + block - 1) // block for count in counts]
    total = sum(blocks)
    tiles = total // 2

    def copy_in(i, h):
        return pltpu.make_async_copy(arrays[i].at[places[i](h)], buffers[i].at[h], sems.at[i, h])

    def copy_out(i, h):
        return pltpu.make_async_copy(out_buffers[i].at[h], out_arrays[i].at[outs[i](h)], sems.at[len(places) + i, h])

    def begin(h, carry):
        for i in range(len(places)):
            copy_in(i, h).start()
        return carry

    lax.fori_loop(0, heads, begin, 0)
    mask = (lax.broadcasted_iota(jnp.int32, (16, LANES), 1) < LANES // 2).astype(jnp.bfloat16)[:1]
    row = lax.broadcasted_iota(jnp.int32, (LANES, LANES), 0) < LANES // 2
    col = lax.broadcasted_iota(jnp.int32, (LANES, LANES), 1) < LANES // 2
    same = (row == col).astype(jnp.bfloat16)

    def rows_of(index):
        which, start, rest = 0, 0, index
        for at, number in enumerate(blocks):
            here = (rest >= 0) & (rest < number)
            which = jnp.where(here, at, which)
            start = jnp.where(here, rest * half, start)
            rest = rest - number
        return which, pl.multiple_of(start, half)

    def one_head(h, carry):
        for i in range(len(places)):
            copy_in(i, h).wait()
        q_ref = buffers[0].at[h]
        key_refs = [buffers[1 + at].at[h] for at in range(sources)]
        value_refs = [buffers[1 + sources + at].at[h] for at in range(sources)]
        if has_state:
            state_ref, marks_ref = buffers[-2].at[h], buffers[-1].at[h]
        acc_ref = acc_scratch if final else out_buffers[0].at[h]

        queries = q_ref[...]
        q2_ref[:pairs] = queries * mask
        q2_ref[pairs:] = swapped(queries) * mask
        largest = None
        for key_ref in key_refs:
            top = jnp.max(jnp.abs(key_ref[...]), axis=0, keepdims=True).astype(jnp.float32)
            largest = top if largest is None else jnp.maximum(largest, top)
        acc_ref[...] = jnp.zeros(acc_ref.shape, acc_ref.dtype)

        largest = jnp.broadcast_to(largest, (8, LANES))
        largest = jnp.maximum(largest, swapped(largest))
        key_square = jnp.sum(jnp.where(left_half(8), largest * largest, 0.0)) * 0.125
        query_square = jnp.max(jnp.dot(queries * queries, same, preferred_element_type=jnp.float32))
        safe = query_square * key_square * (1.03 * scale * scale) < 1e4
        if has_state:
            safe = safe & (jnp.max(marks_ref[...]) == 0.0)
        for at, (value_ref, count) in enumerate(zip(value_refs, counts)):
            unpack_values(value_ref[...], even_ref, odd_ref, at * pairs, count, half, mask)

        def keys_of(index):
            which, start = rows_of(index)
            rows = pl.ds(start, half)
            keys = key_refs[0][rows, :]
            for at in range(1, sources):
                keys = jnp.where(which == at, key_refs[at][rows, :], keys)
            return keys

        def tile_keys(index):
            first, second = keys_of(2 * index), keys_of(2 * index + 1)
            return jnp.concatenate([first, second, swapped(first), swapped(second)], axis=0)

        def value_rows(index):
            which, start = rows_of(index)
            return pl.ds(pl.multiple_of(which * pairs + start, half), half)

        def tile_values(index):
            first, second = value_rows(2 * index), value_rows(2 * index + 1)
            return jnp.concatenate(
                [even_ref[first, :], even_ref[second, :], odd_ref[first, :], odd_ref[second, :]], axis=0
            )

        def weigh(at, keys):
            scores = scores_of(q2_ref[at : at + chunk], keys) * scale
            p_ref[at : at + chunk, : keys.shape[0]] = jnp.exp2(scores).astype(jnp.bfloat16)

        def add(at, values):
            weights = p_ref[at : at + chunk, : values.shape[0]]
            acc_ref[at : at + chunk] += jnp.dot(weights, values, preferred_element_type=jnp.float32)

        @pl.when(safe & (tiles > 0))
        def _():
            first = tile_keys(0)
            for at in range(0, tokens, chunk):
                weigh(at, first)

            def one(index, carry):
                values, keys = tile_values(index - 1), tile_keys(index)
                for at in range(0, tokens, chunk):
                    add(at, values)
                    weigh(at, keys)
                return carry

            lax.fori_loop(1, tiles, one, 0)
            last = tile_values(tiles - 1)
            for at in range(0, tokens, chunk):
                add(at, last)

        @pl.when(safe & (total % 2 == 1))
        def _():
            keys = keys_of(total - 1)
            keys = jnp.concatenate([keys, swapped(keys)], axis=0)
            rows = value_rows(total - 1)
            values = jnp.concatenate([even_ref[rows, :], odd_ref[rows, :]], axis=0)
            for at in range(0, tokens, chunk):
                weigh(at, keys)
                add(at, values)

        @pl.when(jnp.logical_not(safe))
        def _():
            if has_state:
                shifted_before = jnp.max(marks_ref[...])
                rows = state_ref[...]
                lane = lax.broadcasted_iota(jnp.int32, rows.shape, 1)
                turned = jnp.where(lane < LANES // 2, swapped(rows), rows)
                acc_ref[...] = jnp.where((shifted_before > 0.0) & (lane >= LANES // 2), 1.0, rows)
                top_ref[...] = jnp.where(shifted_before > 0.0, turned, 0.0)
            else:
                top_ref[...] = jnp.full(top_ref.shape, LOW)
            step = min(256, tokens)
            col = lax.broadcasted_iota(jnp.int32, (step, block), 1)
            token = jnp.where(col < half, 2 * col, 2 * (col - half) + 1)
            for at_source, (key_ref, count, number) in enumerate(zip(key_refs, counts, blocks)):

                def one(index, carry, at_source=at_source, key_ref=key_ref, count=count):
                    start = pl.multiple_of(index * half, half)
                    keys = key_ref[pl.ds(start, half), :]
                    keys = jnp.concatenate([keys, swapped(keys)], axis=0)
                    rows = pl.ds(at_source * pairs + start, half)
                    values = jnp.concatenate([even_ref[rows, :], odd_ref[rows, :]], axis=0)

                    def part(i, carry):
                        at = pl.ds(pl.multiple_of(i * step, step), step)
                        scores = scores_of(q2_ref[at, :], keys) * scale
                        scores = jnp.where(token < count - index * block, scores, LOW)
                        before = top_ref[at, :]
                        top = jnp.maximum(before, jnp.max(scores, axis=1, keepdims=True))
                        weights = jnp.exp2(scores - top[:, :1]).astype(jnp.bfloat16)
                        added = jnp.dot(weights, values, preferred_element_type=jnp.float32)
                        acc_ref[at, :] = acc_ref[at, :] * jnp.exp2(before - top) + added
                        top_ref[at, :] = top
                        return carry

                    return lax.fori_loop(0, tokens // step, part, carry)

                lax.fori_loop(0, number, one, 0)

            if not final:
                rows = acc_ref[...]
                lane = lax.broadcasted_iota(jnp.int32, rows.shape, 1)
                acc_ref[...] = jnp.where(
                    lane < LANES // 2, rows / swapped(rows), top_ref[...] + jnp.log2(jnp.maximum(rows, 1e-30))
                )

        if final:
            left = left_half(pairs)
            even, odd = acc_ref[:pairs], acc_ref[pairs:]
            if has_state:
                kept = jnp.where(safe, 1.0, 0.0)
                even = even + state_ref[:pairs] * kept
                odd = odd + state_ref[pairs:] * kept
            result = jnp.where(left, even, swapped(odd)) / jnp.where(left, swapped(even), odd)
            out_buffers[0][h] = result.astype(jnp.bfloat16).reshape(out_buffers[0].shape[1:])
        else:
            out_buffers[1][h] = jnp.broadcast_to(jnp.where(safe, 0.0, 1.0), out_buffers[1].shape[1:])
        for i in range(number_out):
            copy_out(i, h).start()
        return carry

    lax.fori_loop(0, heads, one_head, 0)

    def end(h, carry):
        for i in range(number_out):
            copy_out(i, h).wait()
        return carry

    lax.fori_loop(0, heads, end, 0)


def attend(meta, queries, within, first_head, heads, sources, state, dests, out, name):
    pairs = queries.shape[1] // 2
    head_size = LANES // 2
    scale = math.log2(math.e) / math.sqrt(head_size)
    half = min(128, pairs)
    chunk = min(CHUNK, 2 * pairs)

    def place(lead, part, start):
        rows = pl.ds(part * pairs, pairs)
        if lead is None:
            return lambda h: (h + start, rows)
        return lambda h: (lead, h + start, rows)

    arrays, places = [queries], [place(None, within, first_head)]
    for part in (1, 2):
        for source in sources:
            array, lead, part_of, start = source[part]
            arrays.append(array)
            places.append(place(lead, part_of, start))
    shapes = [((pairs, LANES), jnp.bfloat16)] * len(arrays)
    state_shapes = [((2 * pairs, LANES), jnp.float32), ((8, LANES), jnp.float32)]
    if state is not None:
        sums, marks, begin = state
        arrays += [sums, marks]
        places += [lambda h: (h + begin,)] * 2
        shapes += state_shapes
    aliases, extra = {}, []
    if dests is None:
        out_shape = [jax.ShapeDtypeStruct((heads, *shape), dtype) for shape, dtype in state_shapes]
        out_places = [lambda h: (h,)] * 2
        out_shapes = state_shapes
    else:
        out_shape = [jax.ShapeDtypeStruct((2 * dests, heads, pairs // dests, LANES), jnp.bfloat16)]
        out_places = [lambda h: (pl.ds(within * dests, dests), h)]
        out_shapes = [((dests, pairs // dests, LANES), jnp.bfloat16)]
        if out is not None:
            aliases = {1 + len(arrays): 0}
            extra = [out]
    unpacked = len(sources) * pairs
    work = heads * len(sources) * (2 * pairs) ** 2
    got = pl.pallas_call(
        functools.partial(
            attend_kernel,
            tuple(source[0] for source in sources),
            tuple(places),
            tuple(out_places),
            scale,
            half,
            chunk,
            state is not None,
            dests is not None,
        ),
        out_shape=out_shape,
        in_specs=[pl.BlockSpec(memory_space=pltpu.SMEM)]
        + [pl.BlockSpec(memory_space=pl.ANY)] * (len(arrays) + len(extra)),
        out_specs=[pl.BlockSpec(memory_space=pl.ANY)] * len(out_shape),
        scratch_shapes=[pltpu.VMEM((heads, *shape), dtype) for shape, dtype in shapes + out_shapes]
        + [
            pltpu.VMEM((2 * pairs, LANES), jnp.bfloat16),
            pltpu.VMEM((unpacked, LANES), jnp.bfloat16),
            pltpu.VMEM((unpacked, LANES), jnp.bfloat16),
            pltpu.VMEM((2 * pairs, 4 * half), jnp.bfloat16),
            pltpu.VMEM((2 * pairs, LANES), jnp.float32),
            pltpu.VMEM((2 * pairs, LANES), jnp.float32),
            pltpu.SemaphoreType.DMA((len(shapes) + len(out_shapes), heads)),
        ],
        input_output_aliases=aliases,
        compiler_params=pltpu.CompilerParams(vmem_limit_bytes=VMEM),
        cost_estimate=pl.CostEstimate(
            flops=work * 4 * head_size * 4, bytes_accessed=8 * heads * pairs * LANES * 2, transcendentals=work
        ),
        name=name,
    )(meta, *arrays, *extra)
    return got if dests is None else got[0]


def project_kernel(layout, rows, weight_ref, *refs):
    parts, out_ref = refs[:-1], refs[-1]
    lane = lax.broadcasted_iota(jnp.int32, (rows, LANES), 1) < LANES // 2
    even, odd = [], []
    for first in range(0, len(layout), 2):
        (p, s, k), (p2, s2, k2) = layout[first], layout[first + 1]
        a = parts[p][s, k].astype(jnp.float32)
        b = parts[p2][s2, k2].astype(jnp.float32)
        even.append(jnp.where(lane, a, swapped(b)).astype(jnp.bfloat16))
        odd.append(jnp.where(lane, swapped(a), b).astype(jnp.bfloat16))
    stacked = jnp.concatenate([jnp.concatenate(even, axis=1), jnp.concatenate(odd, axis=1)], axis=0)
    token = lax.broadcasted_iota(jnp.int32, (2 * rows, 2 * rows), 0)
    place = lax.broadcasted_iota(jnp.int32, (2 * rows, 2 * rows), 1)
    order = (place == token // 2 + (token % 2) * rows).astype(jnp.bfloat16)
    tokens = jnp.dot(order, stacked, preferred_element_type=jnp.float32).astype(jnp.bfloat16)
    out_ref[...] = jnp.dot(tokens, weight_ref[...], preferred_element_type=jnp.float32).astype(out_ref.dtype)


def project(parts, layout, weight):
    pairs = parts[0].shape[2]
    rows = LANES if pairs % LANES == 0 else pairs
    return pl.pallas_call(
        functools.partial(project_kernel, layout, rows),
        out_shape=jax.ShapeDtypeStruct((2 * pairs, weight.shape[1]), jnp.bfloat16),
        grid=(pairs // rows,),
        in_specs=[pl.BlockSpec(weight.shape, lambda i: (0, 0))]
        + [pl.BlockSpec((*part.shape[:2], rows, LANES), lambda i: (0, 0, i, 0)) for part in parts],
        out_specs=pl.BlockSpec((2 * rows, weight.shape[1]), lambda i: (i, 0)),
        compiler_params=pltpu.CompilerParams(vmem_limit_bytes=VMEM),
        name="project",
    )(weight, *parts)


def shifted(x, pairs):
    return lax.ppermute(x, "frame", pairs)


def shards(query_proj, key_proj, value_proj, lengths, out_weight):
    devices = lax.axis_size("frame")
    groups = lax.axis_size("head")
    index = lax.axis_index("frame")
    heads, rows, _ = query_proj.shape
    half = rows // 2
    frames = lengths.shape[0]
    weight = lax.all_gather(out_weight, "head", axis=0, tiled=True)

    wanted = jnp.stack([2 * index + within - stride for within in range(2) for stride in STRIDES])
    table = jnp.arange(frames, dtype=jnp.int32)
    meta = jnp.sum(jnp.where(wanted[:, None] == table[None, :], lengths[None, :], 0), axis=1, dtype=jnp.int32)
    meta = jnp.minimum(meta, rows)

    size = heads // 2 if heads % 2 == 0 else heads
    starts = range(0, heads, size)
    last = jnp.stack((key_proj[:, half:], value_proj[:, half:]))
    first = jnp.stack((key_proj[:, :half], value_proj[:, :half]))
    by_two = [(i, i + 2) for i in range(devices - 2)]
    near_last = shifted(last, by_two)
    near_first = shifted(first, by_two)
    far = None
    if devices > 8:
        both = jnp.stack((key_proj, value_proj))
        far = shifted(both, [(i, i + 8) for i in range(devices - 8)])

    def own(slot, part, start):
        return slot, (key_proj, None, part, start), (value_proj, None, part, start)

    def moved(slot, array, part, start):
        return slot, (array, 0, part, start), (array, 1, part, start)

    sums_first, marks_first = attend(meta, query_proj, 0, 0, heads, [own(0, 0, 0)], None, None, None, "first_own")
    state_last = {}
    for start in starts[:-1]:
        sources = [own(4, 1, start), own(5, 0, start)]
        sums, marks = attend(meta, query_proj, 1, start, size, sources, None, None, None, "last_own")
        state_last[start] = (sums, marks, 0)
    to_even = [(i + 1, i) for i in range(2, devices - 1, 2)]
    to_odd = [(i, i + 1) for i in range(0, devices - 1, 2)]
    prev = shifted(jnp.where(index % 2 == 0, last, near_last), to_even + to_odd)
    dests = groups // 2
    outs = []
    for start in starts:
        sources = [moved(6, near_last, 0, start)]
        if far is not None:
            sources.append(moved(7, far, 1, start))
        state = state_last.get(start)
        if state is None:
            sources += [own(4, 1, start), own(5, 0, start)]
        outs.append(attend(meta, query_proj, 1, start, size, sources, state, dests, None, "last_rest"))
    got = []
    for number, start in enumerate(starts):
        sources = [moved(1, prev, 0, start), moved(2, near_first, 0, start)]
        if far is not None:
            sources.append(moved(3, far, 0, start))
        state = (sums_first, marks_first, start)
        out = attend(meta, query_proj, 0, start, size, sources, state, dests, outs[number], "first_rest")
        got.append(lax.all_to_all(out, "head", split_axis=0, concat_axis=0, tiled=True))
    layout = tuple(
        (head % heads // size, head // heads, head % heads % size) for head in range(groups * heads)
    )
    return project(got, layout, weight)


def solution(mesh):
    return jax.shard_map(
        shards,
        mesh=mesh,
        in_specs=(
            P("head", "frame", None),
            P("head", "frame", None),
            P("head", "frame", None),
            P(),
            P("head", None),
        ),
        out_specs=P(("frame", "head"), None),
        check_vma=False,
    )
```

```python
import functools
import math

import jax
import jax.numpy as jnp
from jax import lax
from jax.experimental import pallas as pl
from jax.experimental.pallas import tpu as pltpu
from jax.sharding import PartitionSpec as P

LANES = 128
STRIDES = (0, 1, 4, 16)
VMEM = 62 * 1024 * 1024
LOW = -1e30
CHUNK = 512
LN2 = math.log(2)


def swapped(x):
    return pltpu.roll(x, LANES // 2, 1)


def left_half(rows):
    return lax.broadcasted_iota(jnp.int32, (rows, LANES), 1) < LANES // 2


def unpack_values(values, even_ref, odd_ref, at, count, half, mask):
    pairs = values.shape[0]
    even_ref[at : at + pairs] = values * mask + (1 - mask)
    odd_ref[at : at + pairs] = swapped(values) * mask + (1 - mask)

    @pl.when(count % (2 * half) != 0)
    def _():
        start = pl.multiple_of(count // (2 * half) * half, half)
        token = 2 * (start + lax.broadcasted_iota(jnp.int32, (half, LANES), 0))
        rows = pl.ds(at + start, half)
        for ref, later in ((even_ref, 0), (odd_ref, 1)):
            block = ref[rows, :].astype(jnp.float32)
            ref[rows, :] = jnp.where(token + later < count, block, 0.0).astype(ref.dtype)


def scores_of(queries, keys):
    return lax.dot_general(queries, keys, (((1,), (1,)), ((), ())), preferred_element_type=jnp.float32)


def attend_kernel(slots, places, outs, scale, half, chunk, has_state, final, meta_ref, *refs):
    refs = list(refs)
    arrays = [refs.pop(0) for _ in places]
    number_out = len(outs)
    scratch = refs[-(len(places) + number_out + 6) :]
    out_arrays = refs[: -(len(places) + number_out + 6)][-number_out:]
    buffers = scratch[: len(places)]
    out_buffers = scratch[len(places) : len(places) + number_out]
    q2_ref, even_ref, odd_ref, acc_scratch, top_ref, sems = scratch[len(places) + number_out :]
    heads = out_buffers[0].shape[0]
    pairs = buffers[0].shape[1]
    tokens = 2 * pairs
    block = 2 * half
    sources = len(slots)
    counts = [meta_ref[slot] for slot in slots]
    blocks = [(count + block - 1) // block for count in counts]
    total = sum(blocks)

    def copy_in(i, h):
        return pltpu.make_async_copy(arrays[i].at[places[i](h)], buffers[i].at[h], sems.at[i, h])

    def copy_out(i, h):
        return pltpu.make_async_copy(out_buffers[i].at[h], out_arrays[i].at[outs[i](h)], sems.at[len(places) + i, h])

    def begin(h, carry):
        for i in range(len(places)):
            copy_in(i, h).start()
        return carry

    begin(0, 0)
    mask = (lax.broadcasted_iota(jnp.int32, (16, LANES), 1) < LANES // 2).astype(jnp.bfloat16)[:1]
    row = lax.broadcasted_iota(jnp.int32, (LANES, LANES), 0) < LANES // 2
    col = lax.broadcasted_iota(jnp.int32, (LANES, LANES), 1) < LANES // 2
    same = (row == col).astype(jnp.bfloat16)

    def rows_of(index):
        which, start, rest = 0, 0, index
        for at, number in enumerate(blocks):
            here = (rest >= 0) & (rest < number)
            which = jnp.where(here, at, which)
            start = jnp.where(here, rest * half, start)
            rest = rest - number
        return which, pl.multiple_of(start, half)

    def one_head(h, carry):
        @pl.when(h + 1 < heads)
        def _():
            begin(h + 1, 0)

        def wait_for(*numbers):
            for i in numbers:
                copy_in(i, h).wait()

        wait_for(0, *range(1, 1 + sources))
        q_ref = buffers[0].at[h]
        key_refs = [buffers[1 + at].at[h] for at in range(sources)]
        value_refs = [buffers[1 + sources + at].at[h] for at in range(sources)]
        if has_state:
            state_ref, marks_ref = buffers[-2].at[h], buffers[-1].at[h]
        acc_ref = acc_scratch if final else out_buffers[0].at[h]

        queries = q_ref[...]
        q2_ref[:pairs] = queries * mask
        q2_ref[pairs:] = swapped(queries) * mask
        largest = None
        for key_ref in key_refs:
            top = jnp.max(jnp.abs(key_ref[...]), axis=0, keepdims=True).astype(jnp.float32)
            largest = top if largest is None else jnp.maximum(largest, top)
        acc_ref[...] = jnp.zeros(acc_ref.shape, acc_ref.dtype)

        largest = jnp.broadcast_to(largest, (8, LANES))
        largest = jnp.maximum(largest, swapped(largest))
        key_square = jnp.sum(jnp.where(left_half(8), largest * largest, 0.0)) * 0.125
        query_square = jnp.max(jnp.dot(queries * queries, same, preferred_element_type=jnp.float32))
        safe = query_square * key_square * (1.03 * scale * scale) < 1e4
        if has_state:
            wait_for(len(places) - 1)
            safe = safe & (jnp.max(marks_ref[...]) == 0.0)
        wait_for(*range(1 + sources, 1 + 2 * sources))
        for at, (value_ref, count) in enumerate(zip(value_refs, counts)):
            unpack_values(value_ref[...], even_ref, odd_ref, at * pairs, count, half, mask)

        def keys_of(index):
            which, start = rows_of(index)
            rows = pl.ds(start, half)
            keys = key_refs[0][rows, :]
            for at in range(1, sources):
                keys = jnp.where(which == at, key_refs[at][rows, :], keys)
            return keys

        def value_rows(index):
            which, start = rows_of(index)
            return pl.ds(pl.multiple_of(which * pairs + start, half), half)

        def weigh(scores):
            exponent = scores * scale
            coarse = exponent.astype(jnp.bfloat16)
            rest = (exponent - coarse.astype(jnp.float32)).astype(jnp.bfloat16) * LN2
            power = jnp.exp2(coarse)
            return power + power * (rest + rest * rest * 0.5)

        def tile(first, number):
            keys = [keys_of(first + i) for i in range(number)]
            keys = jnp.concatenate(keys + [swapped(block) for block in keys], axis=0)
            places_of = [value_rows(first + i) for i in range(number)]
            values = jnp.concatenate([ref[rows, :] for ref in (even_ref, odd_ref) for rows in places_of], axis=0)
            scores = scores_of(q2_ref[:chunk], keys)
            for at in range(0, tokens, chunk):
                after = at + chunk
                later = scores_of(q2_ref[after : after + chunk], keys) if after < tokens else None
                acc_ref[at:after] += jnp.dot(weigh(scores), values, preferred_element_type=jnp.float32)
                scores = later

        @pl.when(safe)
        def _():
            def whole(index, carry):
                tile(index * 4, 4)
                return carry

            lax.fori_loop(0, total // 4, whole, 0)

            @pl.when(total % 4 >= 2)
            def _():
                tile(total // 4 * 4, 2)

            @pl.when(total % 2 == 1)
            def _():
                tile(total - 1, 1)

        if has_state:
            wait_for(len(places) - 2)

        @pl.when(jnp.logical_not(safe))
        def _():
            if has_state:
                shifted_before = jnp.max(marks_ref[...])
                rows = state_ref[...]
                lane = lax.broadcasted_iota(jnp.int32, rows.shape, 1)
                turned = jnp.where(lane < LANES // 2, swapped(rows), rows)
                acc_ref[...] = jnp.where((shifted_before > 0.0) & (lane >= LANES // 2), 1.0, rows)
                top_ref[...] = jnp.where(shifted_before > 0.0, turned, 0.0)
            else:
                top_ref[...] = jnp.full(top_ref.shape, LOW)
            step = min(256, tokens)
            col = lax.broadcasted_iota(jnp.int32, (step, block), 1)
            token = jnp.where(col < half, 2 * col, 2 * (col - half) + 1)
            for at_source, (key_ref, count, number) in enumerate(zip(key_refs, counts, blocks)):

                def one(index, carry, at_source=at_source, key_ref=key_ref, count=count):
                    start = pl.multiple_of(index * half, half)
                    keys = key_ref[pl.ds(start, half), :]
                    keys = jnp.concatenate([keys, swapped(keys)], axis=0)
                    rows = pl.ds(at_source * pairs + start, half)
                    values = jnp.concatenate([even_ref[rows, :], odd_ref[rows, :]], axis=0)

                    def part(i, carry):
                        at = pl.ds(pl.multiple_of(i * step, step), step)
                        scores = scores_of(q2_ref[at, :], keys) * scale
                        scores = jnp.where(token < count - index * block, scores, LOW)
                        before = top_ref[at, :]
                        top = jnp.maximum(before, jnp.max(scores, axis=1, keepdims=True))
                        weights = jnp.exp2(scores - top[:, :1]).astype(jnp.bfloat16)
                        added = jnp.dot(weights, values, preferred_element_type=jnp.float32)
                        acc_ref[at, :] = acc_ref[at, :] * jnp.exp2(before - top) + added
                        top_ref[at, :] = top
                        return carry

                    return lax.fori_loop(0, tokens // step, part, carry)

                lax.fori_loop(0, number, one, 0)

            if not final:
                rows = acc_ref[...]
                lane = lax.broadcasted_iota(jnp.int32, rows.shape, 1)
                acc_ref[...] = jnp.where(
                    lane < LANES // 2, rows / swapped(rows), top_ref[...] + jnp.log2(jnp.maximum(rows, 1e-30))
                )

        if final:
            left = left_half(pairs)
            even, odd = acc_ref[:pairs], acc_ref[pairs:]
            if has_state:
                kept = jnp.where(safe, 1.0, 0.0)
                even = even + state_ref[:pairs] * kept
                odd = odd + state_ref[pairs:] * kept
            result = jnp.where(left, even, swapped(odd)) / jnp.where(left, swapped(even), odd)
            out_buffers[0][h] = result.astype(jnp.bfloat16).reshape(out_buffers[0].shape[1:])
        else:
            out_buffers[1][h] = jnp.broadcast_to(jnp.where(safe, 0.0, 1.0), out_buffers[1].shape[1:])
        for i in range(number_out):
            copy_out(i, h).start()
        return carry

    lax.fori_loop(0, heads, one_head, 0)

    def end(h, carry):
        for i in range(number_out):
            copy_out(i, h).wait()
        return carry

    lax.fori_loop(0, heads, end, 0)


def attend(meta, queries, within, first_head, heads, sources, state, dests, out, name):
    pairs = queries.shape[1] // 2
    head_size = LANES // 2
    scale = math.log2(math.e) / math.sqrt(head_size)
    half = min(128, pairs)
    chunk = min(CHUNK, 2 * pairs)

    def place(lead, part, start):
        rows = pl.ds(part * pairs, pairs)
        if lead is None:
            return lambda h: (h + start, rows)
        return lambda h: (lead, h + start, rows)

    arrays, places = [queries], [place(None, within, first_head)]
    for part in (1, 2):
        for source in sources:
            array, lead, part_of, start = source[part]
            arrays.append(array)
            places.append(place(lead, part_of, start))
    shapes = [((pairs, LANES), jnp.bfloat16)] * len(arrays)
    state_shapes = [((2 * pairs, LANES), jnp.float32), ((8, LANES), jnp.float32)]
    if state is not None:
        sums, marks, begin = state
        arrays += [sums, marks]
        places += [lambda h: (h + begin,)] * 2
        shapes += state_shapes
    aliases, extra = {}, []
    if dests is None:
        out_shape = [jax.ShapeDtypeStruct((heads, *shape), dtype) for shape, dtype in state_shapes]
        out_places = [lambda h: (h,)] * 2
        out_shapes = state_shapes
    else:
        out_shape = [jax.ShapeDtypeStruct((2 * dests, heads, pairs // dests, LANES), jnp.bfloat16)]
        out_places = [lambda h: (pl.ds(within * dests, dests), h)]
        out_shapes = [((dests, pairs // dests, LANES), jnp.bfloat16)]
        if out is not None:
            aliases = {1 + len(arrays): 0}
            extra = [out]
    unpacked = len(sources) * pairs
    work = heads * len(sources) * (2 * pairs) ** 2
    got = pl.pallas_call(
        functools.partial(
            attend_kernel,
            tuple(source[0] for source in sources),
            tuple(places),
            tuple(out_places),
            scale,
            half,
            chunk,
            state is not None,
            dests is not None,
        ),
        out_shape=out_shape,
        in_specs=[pl.BlockSpec(memory_space=pltpu.SMEM)]
        + [pl.BlockSpec(memory_space=pl.ANY)] * (len(arrays) + len(extra)),
        out_specs=[pl.BlockSpec(memory_space=pl.ANY)] * len(out_shape),
        scratch_shapes=[pltpu.VMEM((heads, *shape), dtype) for shape, dtype in shapes + out_shapes]
        + [
            pltpu.VMEM((2 * pairs, LANES), jnp.bfloat16),
            pltpu.VMEM((unpacked, LANES), jnp.bfloat16),
            pltpu.VMEM((unpacked, LANES), jnp.bfloat16),
            pltpu.VMEM((2 * pairs, LANES), jnp.float32),
            pltpu.VMEM((2 * pairs, LANES), jnp.float32),
            pltpu.SemaphoreType.DMA((len(shapes) + len(out_shapes), heads)),
        ],
        input_output_aliases=aliases,
        compiler_params=pltpu.CompilerParams(vmem_limit_bytes=VMEM),
        cost_estimate=pl.CostEstimate(
            flops=work * 4 * head_size * 4, bytes_accessed=8 * heads * pairs * LANES * 2, transcendentals=work
        ),
        name=name,
    )(meta, *arrays, *extra)
    return got if dests is None else got[0]


def project_kernel(layout, rows, weight_ref, *refs):
    parts, out_ref = refs[:-1], refs[-1]
    lane = lax.broadcasted_iota(jnp.int32, (rows, LANES), 1) < LANES // 2
    even, odd = [], []
    for first in range(0, len(layout), 2):
        (p, s, k), (p2, s2, k2) = layout[first], layout[first + 1]
        a = parts[p][s, k].astype(jnp.float32)
        b = parts[p2][s2, k2].astype(jnp.float32)
        even.append(jnp.where(lane, a, swapped(b)).astype(jnp.bfloat16))
        odd.append(jnp.where(lane, swapped(a), b).astype(jnp.bfloat16))
    stacked = jnp.concatenate([jnp.concatenate(even, axis=1), jnp.concatenate(odd, axis=1)], axis=0)
    token = lax.broadcasted_iota(jnp.int32, (2 * rows, 2 * rows), 0)
    place = lax.broadcasted_iota(jnp.int32, (2 * rows, 2 * rows), 1)
    order = (place == token // 2 + (token % 2) * rows).astype(jnp.bfloat16)
    tokens = jnp.dot(order, stacked, preferred_element_type=jnp.float32).astype(jnp.bfloat16)
    out_ref[...] = jnp.dot(tokens, weight_ref[...], preferred_element_type=jnp.float32).astype(out_ref.dtype)


def project(parts, layout, weight):
    pairs = parts[0].shape[2]
    rows = LANES if pairs % LANES == 0 else pairs
    return pl.pallas_call(
        functools.partial(project_kernel, layout, rows),
        out_shape=jax.ShapeDtypeStruct((2 * pairs, weight.shape[1]), jnp.bfloat16),
        grid=(pairs // rows,),
        in_specs=[pl.BlockSpec(weight.shape, lambda i: (0, 0))]
        + [pl.BlockSpec((*part.shape[:2], rows, LANES), lambda i: (0, 0, i, 0)) for part in parts],
        out_specs=pl.BlockSpec((2 * rows, weight.shape[1]), lambda i: (i, 0)),
        compiler_params=pltpu.CompilerParams(vmem_limit_bytes=VMEM),
        name="project",
    )(weight, *parts)


def shifted(x, pairs):
    return lax.ppermute(x, "frame", pairs)


def shards(query_proj, key_proj, value_proj, lengths, out_weight):
    devices = lax.axis_size("frame")
    groups = lax.axis_size("head")
    index = lax.axis_index("frame")
    heads, rows, _ = query_proj.shape
    half = rows // 2
    frames = lengths.shape[0]
    weight = lax.all_gather(out_weight, "head", axis=0, tiled=True)

    wanted = jnp.stack([2 * index + within - stride for within in range(2) for stride in STRIDES])
    table = jnp.arange(frames, dtype=jnp.int32)
    meta = jnp.sum(jnp.where(wanted[:, None] == table[None, :], lengths[None, :], 0), axis=1, dtype=jnp.int32)
    meta = jnp.minimum(meta, rows)

    size = heads // 2 if heads % 2 == 0 else heads
    starts = range(0, heads, size)
    last = jnp.stack((key_proj[:, half:], value_proj[:, half:]))
    first = jnp.stack((key_proj[:, :half], value_proj[:, :half]))
    by_two = [(i, i + 2) for i in range(devices - 2)]
    near_last = shifted(last, by_two)
    near_first = shifted(first, by_two)
    far = None
    if devices > 8:
        both = jnp.stack((key_proj, value_proj))
        far = shifted(both, [(i, i + 8) for i in range(devices - 8)])

    def own(slot, part, start):
        return slot, (key_proj, None, part, start), (value_proj, None, part, start)

    def moved(slot, array, part, start):
        return slot, (array, 0, part, start), (array, 1, part, start)

    sums_first, marks_first = attend(meta, query_proj, 0, 0, heads, [own(0, 0, 0)], None, None, None, "first_own")
    state_last = {}
    for start in starts[:-1]:
        sources = [own(4, 1, start), own(5, 0, start)]
        sums, marks = attend(meta, query_proj, 1, start, size, sources, None, None, None, "last_own")
        state_last[start] = (sums, marks, 0)
    to_even = [(i + 1, i) for i in range(2, devices - 1, 2)]
    to_odd = [(i, i + 1) for i in range(0, devices - 1, 2)]
    prev = shifted(jnp.where(index % 2 == 0, last, near_last), to_even + to_odd)
    dests = groups // 2
    outs = []
    for start in starts:
        sources = [moved(6, near_last, 0, start)]
        if far is not None:
            sources.append(moved(7, far, 1, start))
        state = state_last.get(start)
        if state is None:
            sources += [own(4, 1, start), own(5, 0, start)]
        outs.append(attend(meta, query_proj, 1, start, size, sources, state, dests, None, "last_rest"))
    got = []
    for number, start in enumerate(starts):
        sources = [moved(1, prev, 0, start), moved(2, near_first, 0, start)]
        if far is not None:
            sources.append(moved(3, far, 0, start))
        state = (sums_first, marks_first, start)
        out = attend(meta, query_proj, 0, start, size, sources, state, dests, outs[number], "first_rest")
        got.append(lax.all_to_all(out, "head", split_axis=0, concat_axis=0, tiled=True))
    layout = tuple(
        (head % heads // size, head // heads, head % heads % size) for head in range(groups * heads)
    )
    return project(got, layout, weight)


def solution(mesh):
    return jax.shard_map(
        shards,
        mesh=mesh,
        in_specs=(
            P("head", "frame", None),
            P("head", "frame", None),
            P("head", "frame", None),
            P(),
            P("head", None),
        ),
        out_specs=P(("frame", "head"), None),
        check_vma=False,
    )
```

```python
import functools
import math

import jax
import jax.numpy as jnp
from jax import lax
from jax.experimental import pallas as pl
from jax.experimental.pallas import tpu as pltpu
from jax.sharding import PartitionSpec as P

LANES = 128
STRIDES = (0, 1, 4, 16)
VMEM = 63 * 1024 * 1024
LOW = -1e30
CHUNK = 512


def swapped(x):
    return pltpu.roll(x, LANES // 2, 1)


def left_half(rows):
    return lax.broadcasted_iota(jnp.int32, (rows, LANES), 1) < LANES // 2


def split_queries(scaled, q2_ref):
    pairs = scaled.shape[0]
    high = scaled.astype(jnp.bfloat16).astype(jnp.float32)
    low = scaled - high
    left = left_half(pairs)
    q2_ref[:pairs] = jnp.where(left, high, swapped(low)).astype(jnp.bfloat16)
    q2_ref[pairs:] = jnp.where(left, swapped(high), low).astype(jnp.bfloat16)


def doubled(blocks, mask):
    even = [block * mask for block in blocks]
    odd = [block - part for block, part in zip(blocks, even)]
    return jnp.concatenate([part + swapped(part) for part in even + odd], axis=0)


def unpack_values(values, even_ref, odd_ref, at, count, half, mask):
    pairs = values.shape[0]
    even_ref[at : at + pairs] = values * mask + (1 - mask)
    odd_ref[at : at + pairs] = swapped(values) * mask + (1 - mask)

    @pl.when(count % (2 * half) != 0)
    def _():
        start = pl.multiple_of(count // (2 * half) * half, half)
        token = 2 * (start + lax.broadcasted_iota(jnp.int32, (half, LANES), 0))
        rows = pl.ds(at + start, half)
        for ref, later in ((even_ref, 0), (odd_ref, 1)):
            block = ref[rows, :].astype(jnp.float32)
            ref[rows, :] = jnp.where(token + later < count, block, 0.0).astype(ref.dtype)


def scores_of(queries, keys):
    return lax.dot_general(queries, keys, (((1,), (1,)), ((), ())), preferred_element_type=jnp.float32)


def attend_kernel(slots, places, outs, scale, half, chunk, has_state, final, meta_ref, *refs):
    refs = list(refs)
    arrays = [refs.pop(0) for _ in places]
    number_out = len(outs)
    scratch = refs[-(len(places) + number_out + 7) :]
    out_arrays = refs[: -(len(places) + number_out + 7)][-number_out:]
    buffers = scratch[: len(places)]
    out_buffers = scratch[len(places) : len(places) + number_out]
    q2_ref, even_ref, odd_ref, s_ref, acc_scratch, top_ref, sems = scratch[len(places) + number_out :]
    heads = out_buffers[0].shape[0]
    pairs = buffers[0].shape[1]
    tokens = 2 * pairs
    block = 2 * half
    sources = len(slots)
    counts = [meta_ref[slot] for slot in slots]
    blocks = [(count + block - 1) // block for count in counts]
    total = sum(blocks)
    tiles = total // 2

    def copy_in(i, h):
        return pltpu.make_async_copy(arrays[i].at[places[i](h)], buffers[i].at[h], sems.at[i, h])

    def copy_out(i, h):
        return pltpu.make_async_copy(out_buffers[i].at[h], out_arrays[i].at[outs[i](h)], sems.at[len(places) + i, h])

    def begin(h, carry):
        for i in range(len(places)):
            copy_in(i, h).start()
        return carry

    begin(0, 0)
    mask = (lax.broadcasted_iota(jnp.int32, (16, LANES), 1) < LANES // 2).astype(jnp.bfloat16)[:1]
    row = lax.broadcasted_iota(jnp.int32, (LANES, LANES), 0) < LANES // 2
    col = lax.broadcasted_iota(jnp.int32, (LANES, LANES), 1) < LANES // 2
    same = (row == col).astype(jnp.bfloat16)

    def rows_of(index):
        which, start, rest = 0, 0, index
        for at, number in enumerate(blocks):
            here = (rest >= 0) & (rest < number)
            which = jnp.where(here, at, which)
            start = jnp.where(here, rest * half, start)
            rest = rest - number
        return which, pl.multiple_of(start, half)

    def one_head(h, carry):
        @pl.when(h + 1 < heads)
        def _():
            begin(h + 1, 0)

        def wait_for(*numbers):
            for i in numbers:
                copy_in(i, h).wait()

        wait_for(0, *range(1, 1 + sources))
        q_ref = buffers[0].at[h]
        key_refs = [buffers[1 + at].at[h] for at in range(sources)]
        value_refs = [buffers[1 + sources + at].at[h] for at in range(sources)]
        if has_state:
            state_ref, marks_ref = buffers[-2].at[h], buffers[-1].at[h]
        acc_ref = acc_scratch if final else out_buffers[0].at[h]

        queries = q_ref[...]
        split_queries(queries.astype(jnp.float32) * scale, q2_ref)
        largest = None
        for key_ref in key_refs:
            top = jnp.max(jnp.abs(key_ref[...]), axis=0, keepdims=True).astype(jnp.float32)
            largest = top if largest is None else jnp.maximum(largest, top)
        acc_ref[...] = jnp.zeros(acc_ref.shape, acc_ref.dtype)

        largest = jnp.broadcast_to(largest, (8, LANES))
        largest = jnp.maximum(largest, swapped(largest))
        key_square = jnp.sum(jnp.where(left_half(8), largest * largest, 0.0)) * 0.125
        query_square = jnp.max(jnp.dot(queries * queries, same, preferred_element_type=jnp.float32))
        safe = query_square * key_square * (1.03 * scale * scale) < 1e4
        if has_state:
            wait_for(len(places) - 1)
            safe = safe & (jnp.max(marks_ref[...]) == 0.0)
        wait_for(*range(1 + sources, 1 + 2 * sources))
        for at, (value_ref, count) in enumerate(zip(value_refs, counts)):
            unpack_values(value_ref[...], even_ref, odd_ref, at * pairs, count, half, mask)

        def keys_of(index):
            which, start = rows_of(index)
            rows = pl.ds(start, half)
            keys = key_refs[0][rows, :]
            for at in range(1, sources):
                keys = jnp.where(which == at, key_refs[at][rows, :], keys)
            return keys

        def value_rows(index):
            which, start = rows_of(index)
            return pl.ds(pl.multiple_of(which * pairs + start, half), half)

        def keys_at(first, number):
            return doubled([keys_of(first + i) for i in range(number)], mask)

        def values_at(first, number):
            rows = [value_rows(first + i) for i in range(number)]
            return jnp.concatenate([ref[at, :] for ref in (even_ref, odd_ref) for at in rows], axis=0)

        def add(at, scores, values):
            weights = jnp.exp2(scores).astype(jnp.bfloat16)
            acc_ref[at : at + chunk] += jnp.dot(weights, values, preferred_element_type=jnp.float32)

        @pl.when(safe & (tiles > 0))
        def _():
            s_ref[...] = scores_of(q2_ref[:chunk], keys_at(0, 2))

            def whole(index, carry):
                keys, values = keys_at(2 * index, 2), values_at(2 * index, 2)
                scores = s_ref[...]
                for at in range(0, tokens, chunk):
                    after = at + chunk
                    if after < tokens:
                        later = scores_of(q2_ref[after : after + chunk], keys)
                    else:
                        later = scores_of(q2_ref[:chunk], keys_at(2 * jnp.minimum(index + 1, tiles - 1), 2))
                    add(at, scores, values)
                    scores = later
                s_ref[...] = scores
                return carry

            lax.fori_loop(0, tiles, whole, 0)

        @pl.when(safe & (total % 2 == 1))
        def _():
            keys, values = keys_at(total - 1, 1), values_at(total - 1, 1)
            scores = scores_of(q2_ref[:chunk], keys)
            for at in range(0, tokens, chunk):
                after = at + chunk
                later = scores_of(q2_ref[after : after + chunk], keys) if after < tokens else None
                add(at, scores, values)
                scores = later

        if has_state:
            wait_for(len(places) - 2)

        @pl.when(jnp.logical_not(safe))
        def _():
            if has_state:
                shifted_before = jnp.max(marks_ref[...])
                rows = state_ref[...]
                lane = lax.broadcasted_iota(jnp.int32, rows.shape, 1)
                turned = jnp.where(lane < LANES // 2, swapped(rows), rows)
                acc_ref[...] = jnp.where((shifted_before > 0.0) & (lane >= LANES // 2), 1.0, rows)
                top_ref[...] = jnp.where(shifted_before > 0.0, turned, 0.0)
            else:
                top_ref[...] = jnp.full(top_ref.shape, LOW)
            step = min(256, tokens)
            col = lax.broadcasted_iota(jnp.int32, (step, block), 1)
            token = jnp.where(col < half, 2 * col, 2 * (col - half) + 1)
            for at_source, (key_ref, count, number) in enumerate(zip(key_refs, counts, blocks)):

                def one(index, carry, at_source=at_source, key_ref=key_ref, count=count):
                    start = pl.multiple_of(index * half, half)
                    keys = doubled([key_ref[pl.ds(start, half), :]], mask)
                    rows = pl.ds(at_source * pairs + start, half)
                    values = jnp.concatenate([even_ref[rows, :], odd_ref[rows, :]], axis=0)

                    def part(i, carry):
                        at = pl.ds(pl.multiple_of(i * step, step), step)
                        scores = scores_of(q2_ref[at, :], keys)
                        scores = jnp.where(token < count - index * block, scores, LOW)
                        before = top_ref[at, :]
                        top = jnp.maximum(before, jnp.max(scores, axis=1, keepdims=True))
                        weights = jnp.exp2(scores - top[:, :1]).astype(jnp.bfloat16)
                        added = jnp.dot(weights, values, preferred_element_type=jnp.float32)
                        acc_ref[at, :] = acc_ref[at, :] * jnp.exp2(before - top) + added
                        top_ref[at, :] = top
                        return carry

                    return lax.fori_loop(0, tokens // step, part, carry)

                lax.fori_loop(0, number, one, 0)

            if not final:
                rows = acc_ref[...]
                lane = lax.broadcasted_iota(jnp.int32, rows.shape, 1)
                acc_ref[...] = jnp.where(
                    lane < LANES // 2, rows / swapped(rows), top_ref[...] + jnp.log2(jnp.maximum(rows, 1e-30))
                )

        if final:
            left = left_half(pairs)
            even, odd = acc_ref[:pairs], acc_ref[pairs:]
            if has_state:
                kept = jnp.where(safe, 1.0, 0.0)
                even = even + state_ref[:pairs] * kept
                odd = odd + state_ref[pairs:] * kept
            sums = jnp.where(left, swapped(even), odd)
            inverse = pl.reciprocal(sums, approx=True)
            inverse = inverse * (2.0 - sums * inverse)
            result = jnp.where(left, even, swapped(odd)) * inverse
            out_buffers[0][h] = result.astype(jnp.bfloat16).reshape(out_buffers[0].shape[1:])
        else:
            out_buffers[1][h] = jnp.broadcast_to(jnp.where(safe, 0.0, 1.0), out_buffers[1].shape[1:])
        for i in range(number_out):
            copy_out(i, h).start()
        return carry

    lax.fori_loop(0, heads, one_head, 0)

    def end(h, carry):
        for i in range(number_out):
            copy_out(i, h).wait()
        return carry

    lax.fori_loop(0, heads, end, 0)


def attend(meta, queries, within, first_head, heads, sources, state, dests, out, name):
    pairs = queries.shape[1] // 2
    head_size = LANES // 2
    scale = math.log2(math.e) / math.sqrt(head_size)
    half = min(128, pairs)
    chunk = min(CHUNK, 2 * pairs)

    def place(lead, part, start):
        rows = pl.ds(part * pairs, pairs)
        if lead is None:
            return lambda h: (h + start, rows)
        return lambda h: (lead, h + start, rows)

    arrays, places = [queries], [place(None, within, first_head)]
    for part in (1, 2):
        for source in sources:
            array, lead, part_of, start = source[part]
            arrays.append(array)
            places.append(place(lead, part_of, start))
    shapes = [((pairs, LANES), jnp.bfloat16)] * len(arrays)
    state_shapes = [((2 * pairs, LANES), jnp.float32), ((8, LANES), jnp.float32)]
    if state is not None:
        sums, marks, begin = state
        arrays += [sums, marks]
        places += [lambda h: (h + begin,)] * 2
        shapes += state_shapes
    aliases, extra = {}, []
    if dests is None:
        out_shape = [jax.ShapeDtypeStruct((heads, *shape), dtype) for shape, dtype in state_shapes]
        out_places = [lambda h: (h,)] * 2
        out_shapes = state_shapes
    else:
        out_shape = [jax.ShapeDtypeStruct((2 * dests, heads, pairs // dests, LANES), jnp.bfloat16)]
        out_places = [lambda h: (pl.ds(within * dests, dests), h)]
        out_shapes = [((dests, pairs // dests, LANES), jnp.bfloat16)]
        if out is not None:
            aliases = {1 + len(arrays): 0}
            extra = [out]
    unpacked = len(sources) * pairs
    work = heads * len(sources) * (2 * pairs) ** 2
    got = pl.pallas_call(
        functools.partial(
            attend_kernel,
            tuple(source[0] for source in sources),
            tuple(places),
            tuple(out_places),
            scale,
            half,
            chunk,
            state is not None,
            dests is not None,
        ),
        out_shape=out_shape,
        in_specs=[pl.BlockSpec(memory_space=pltpu.SMEM)]
        + [pl.BlockSpec(memory_space=pl.ANY)] * (len(arrays) + len(extra)),
        out_specs=[pl.BlockSpec(memory_space=pl.ANY)] * len(out_shape),
        scratch_shapes=[pltpu.VMEM((heads, *shape), dtype) for shape, dtype in shapes + out_shapes]
        + [
            pltpu.VMEM((2 * pairs, LANES), jnp.bfloat16),
            pltpu.VMEM((unpacked, LANES), jnp.bfloat16),
            pltpu.VMEM((unpacked, LANES), jnp.bfloat16),
            pltpu.VMEM((chunk, 4 * half), jnp.float32),
            pltpu.VMEM((2 * pairs, LANES), jnp.float32),
            pltpu.VMEM((2 * pairs, LANES), jnp.float32),
            pltpu.SemaphoreType.DMA((len(shapes) + len(out_shapes), heads)),
        ],
        input_output_aliases=aliases,
        compiler_params=pltpu.CompilerParams(vmem_limit_bytes=VMEM),
        cost_estimate=pl.CostEstimate(
            flops=work * 4 * head_size * 4, bytes_accessed=8 * heads * pairs * LANES * 2, transcendentals=work
        ),
        name=name,
    )(meta, *arrays, *extra)
    return got if dests is None else got[0]


def project_kernel(layout, rows, weight_ref, *refs):
    parts, out_ref = refs[:-1], refs[-1]
    lane = lax.broadcasted_iota(jnp.int32, (rows, LANES), 1) < LANES // 2
    even, odd = [], []
    for first in range(0, len(layout), 2):
        (p, s, k), (p2, s2, k2) = layout[first], layout[first + 1]
        a = parts[p][s, k].astype(jnp.float32)
        b = parts[p2][s2, k2].astype(jnp.float32)
        even.append(jnp.where(lane, a, swapped(b)).astype(jnp.bfloat16))
        odd.append(jnp.where(lane, swapped(a), b).astype(jnp.bfloat16))
    stacked = jnp.concatenate([jnp.concatenate(even, axis=1), jnp.concatenate(odd, axis=1)], axis=0)
    token = lax.broadcasted_iota(jnp.int32, (2 * rows, 2 * rows), 0)
    place = lax.broadcasted_iota(jnp.int32, (2 * rows, 2 * rows), 1)
    order = (place == token // 2 + (token % 2) * rows).astype(jnp.bfloat16)
    tokens = jnp.dot(order, stacked, preferred_element_type=jnp.float32).astype(jnp.bfloat16)
    out_ref[...] = jnp.dot(tokens, weight_ref[...], preferred_element_type=jnp.float32).astype(out_ref.dtype)


def project(parts, layout, weight):
    pairs = parts[0].shape[2]
    rows = LANES if pairs % LANES == 0 else pairs
    return pl.pallas_call(
        functools.partial(project_kernel, layout, rows),
        out_shape=jax.ShapeDtypeStruct((2 * pairs, weight.shape[1]), jnp.bfloat16),
        grid=(pairs // rows,),
        in_specs=[pl.BlockSpec(weight.shape, lambda i: (0, 0))]
        + [pl.BlockSpec((*part.shape[:2], rows, LANES), lambda i: (0, 0, i, 0)) for part in parts],
        out_specs=pl.BlockSpec((2 * rows, weight.shape[1]), lambda i: (i, 0)),
        compiler_params=pltpu.CompilerParams(vmem_limit_bytes=VMEM // 3),
        name="project",
    )(weight, *parts)


def shifted(x, pairs):
    return lax.ppermute(x, "frame", pairs)


def shards(query_proj, key_proj, value_proj, lengths, out_weight):
    devices = lax.axis_size("frame")
    groups = lax.axis_size("head")
    index = lax.axis_index("frame")
    heads, rows, _ = query_proj.shape
    half = rows // 2
    frames = lengths.shape[0]
    weight = lax.all_gather(out_weight, "head", axis=0, tiled=True)

    wanted = jnp.stack([2 * index + within - stride for within in range(2) for stride in STRIDES])
    table = jnp.arange(frames, dtype=jnp.int32)
    meta = jnp.sum(jnp.where(wanted[:, None] == table[None, :], lengths[None, :], 0), axis=1, dtype=jnp.int32)
    meta = jnp.minimum(meta, rows)

    size = heads // 2 if heads % 2 == 0 else heads
    starts = range(0, heads, size)
    last = jnp.stack((key_proj[:, half:], value_proj[:, half:]))
    first = jnp.stack((key_proj[:, :half], value_proj[:, :half]))
    by_two = [(i, i + 2) for i in range(devices - 2)]
    near_last = shifted(last, by_two)
    near_first = shifted(first, by_two)
    far = None
    if devices > 8:
        both = jnp.stack((key_proj, value_proj))
        far = shifted(both, [(i, i + 8) for i in range(devices - 8)])

    def own(slot, part, start):
        return slot, (key_proj, None, part, start), (value_proj, None, part, start)

    def moved(slot, array, part, start):
        return slot, (array, 0, part, start), (array, 1, part, start)

    sums_first, marks_first = attend(meta, query_proj, 0, 0, heads, [own(0, 0, 0)], None, None, None, "first_own")
    state_last = {}
    for start in starts[:-1]:
        sources = [own(4, 1, start), own(5, 0, start)]
        sums, marks = attend(meta, query_proj, 1, start, size, sources, None, None, None, "last_own")
        state_last[start] = (sums, marks, 0)
    to_even = [(i + 1, i) for i in range(2, devices - 1, 2)]
    to_odd = [(i, i + 1) for i in range(0, devices - 1, 2)]
    prev = shifted(jnp.where(index % 2 == 0, last, near_last), to_even + to_odd)
    dests = groups // 2
    outs = []
    for start in starts:
        sources = [moved(6, near_last, 0, start)]
        if far is not None:
            sources.append(moved(7, far, 1, start))
        state = state_last.get(start)
        if state is None:
            sources += [own(4, 1, start), own(5, 0, start)]
        outs.append(attend(meta, query_proj, 1, start, size, sources, state, dests, None, "last_rest"))
    weight, *outs = lax.optimization_barrier((weight, *outs))
    got = []
    for number, start in enumerate(starts):
        sources = [moved(1, prev, 0, start), moved(2, near_first, 0, start)]
        if far is not None:
            sources.append(moved(3, far, 0, start))
        state = (sums_first, marks_first, start)
        out = attend(meta, query_proj, 0, start, size, sources, state, dests, outs[number], "first_rest")
        got.append(lax.all_to_all(out, "head", split_axis=0, concat_axis=0, tiled=True))
    layout = tuple(
        (head % heads // size, head // heads, head % heads % size) for head in range(groups * heads)
    )
    return project(got, layout, weight)


def solution(mesh):
    return jax.shard_map(
        shards,
        mesh=mesh,
        in_specs=(
            P("head", "frame", None),
            P("head", "frame", None),
            P("head", "frame", None),
            P(),
            P("head", None),
        ),
        out_specs=P(("frame", "head"), None),
        check_vma=False,
    )
```

```python
import functools
import math

import jax
import jax.numpy as jnp
from jax import lax
from jax.experimental import pallas as pl
from jax.experimental.pallas import tpu as pltpu
from jax.sharding import PartitionSpec as P

LANES = 128
STRIDES = (0, 1, 4, 16)
VMEM = 63 * 1024 * 1024
LOW = -1e30
WIDTH = 256


def swapped(x):
    return pltpu.roll(x, LANES // 2, 1)


def doubled(blocks):
    mask = (lax.broadcasted_iota(jnp.int32, (16, LANES), 1) < LANES // 2).astype(blocks[0].dtype)[:1]
    even = [block * mask for block in blocks]
    odd = [block - part for block, part in zip(blocks, even)]
    return jnp.concatenate([part + swapped(part) for part in even + odd], axis=0)


def matmul(a, b):
    return jnp.dot(a, b, preferred_element_type=jnp.float32)


def attend_kernel(slots, scale, half, width, has_state, final, meta_ref, q_ref, *refs):
    refs = list(refs)
    key_refs = [refs.pop(0) for _ in slots]
    value_refs = [refs.pop(0) for _ in slots]
    if has_state:
        state_ref, marks_ref = refs.pop(0), refs.pop(0)
    if final:
        if len(refs) > 6:
            refs.pop(0)
        out_ref = refs.pop(0)
    else:
        out_ref, mark_ref = refs.pop(0), refs.pop(0)
    q2_ref, even_ref, odd_ref, acc_ref, top_ref = refs
    if not final:
        acc_ref = out_ref
    pairs = q_ref.shape[0]
    size = LANES // 2
    depth = acc_ref.shape[0]
    tokens = 2 * pairs
    block = 2 * half
    counts = [meta_ref[slot] for slot in slots]
    blocks = [(count + block - 1) // block for count in counts]
    total = sum(blocks)

    scaled = jnp.transpose(q_ref[...].astype(jnp.float32) * scale)
    high = scaled.astype(jnp.bfloat16)
    low = (scaled - high.astype(jnp.float32)).astype(jnp.bfloat16)
    q2_ref[:size, :pairs] = high[:size]
    q2_ref[size:, :pairs] = low[:size]
    q2_ref[:size, pairs:] = high[size:]
    q2_ref[size:, pairs:] = low[size:]
    acc_ref[...] = jnp.zeros(acc_ref.shape, acc_ref.dtype)

    largest = None
    for key_ref in key_refs:
        top = jnp.max(jnp.abs(key_ref[...]), axis=0, keepdims=True).astype(jnp.float32)
        largest = top if largest is None else jnp.maximum(largest, top)
    largest = jnp.broadcast_to(largest, (8, LANES))
    largest = jnp.maximum(largest, swapped(largest))
    key_square = jnp.sum(largest * largest) * 0.0625
    square = scaled * scaled
    query_square = jnp.max(
        jnp.maximum(
            jnp.sum(square[:size], axis=0, keepdims=True), jnp.sum(square[size:], axis=0, keepdims=True)
        )
    )
    safe = query_square * key_square * 1.01 < 1e4
    if has_state:
        safe = safe & (jnp.max(marks_ref[...]) == 0.0)

    for at, (value_ref, count) in enumerate(zip(value_refs, counts)):
        turned = jnp.transpose(value_ref[...].astype(jnp.float32)).astype(jnp.bfloat16)
        cols = slice(at * pairs, (at + 1) * pairs)
        for ref, part in ((even_ref, turned[:size]), (odd_ref, turned[size:])):
            ref[:size, cols] = part
            ref[size:, cols] = jnp.ones((depth - size, pairs), ref.dtype)

        @pl.when(count % block != 0)
        def _(at=at, count=count):
            start = pl.multiple_of(count // block * half, half)
            token = 2 * (start + lax.broadcasted_iota(jnp.int32, (depth, half), 1))
            cols = pl.ds(pl.multiple_of(at * pairs + start, half), half)
            for ref, later in ((even_ref, 0), (odd_ref, 1)):
                kept = jnp.where(token + later < count, ref[:, cols].astype(jnp.float32), 0.0)
                ref[:, cols] = kept.astype(ref.dtype)

    def place_of(index):
        which, start, rest = 0, 0, index
        for at, number in enumerate(blocks):
            here = (rest >= 0) & (rest < number)
            which = jnp.where(here, at, which)
            start = jnp.where(here, rest * half, start)
            rest = rest - number
        return which, pl.multiple_of(start, half)

    def keys_of(index):
        which, start = place_of(index)
        rows = pl.ds(start, half)
        keys = key_refs[0][rows, :]
        for at in range(1, len(slots)):
            keys = jnp.where(which == at, key_refs[at][rows, :], keys)
        return keys

    def values_at(first, number):
        cols = []
        for i in range(number):
            which, start = place_of(first + i)
            cols.append(pl.ds(pl.multiple_of(which * pairs + start, half), half))
        return jnp.concatenate([ref[:, at] for ref in (even_ref, odd_ref) for at in cols], axis=1)

    def tile(first, number):
        keys = doubled([keys_of(first + i) for i in range(number)])
        values = values_at(first, number)
        scores = matmul(keys, q2_ref[:, :width])
        for at in range(0, tokens, width):
            after = at + width
            later = matmul(keys, q2_ref[:, after : after + width]) if after < tokens else None
            weights = jnp.exp2(scores).astype(jnp.bfloat16)
            acc_ref[:, at:after] += matmul(values, weights)
            scores = later

    @pl.when(safe)
    def _():
        def whole(index, carry):
            tile(index * 4, 4)
            return carry

        lax.fori_loop(0, total // 4, whole, 0)

        @pl.when(total % 4 >= 2)
        def _():
            tile(total // 4 * 4, 2)

        @pl.when(total % 2 == 1)
        def _():
            tile(total - 1, 1)

    @pl.when(jnp.logical_not(safe))
    def _():
        if has_state:
            marked = jnp.max(marks_ref[...]) > 0.0
            rows = state_ref[...]
            row = lax.broadcasted_iota(jnp.int32, rows.shape, 0)
            acc_ref[...] = jnp.where(marked & (row >= size), 1.0, rows)
            top_ref[...] = jnp.where(marked, rows[size : size + 8], 0.0)
        else:
            top_ref[...] = jnp.full(top_ref.shape, LOW)
        step = 2 * half
        row = lax.broadcasted_iota(jnp.int32, (block, step), 0)
        token = jnp.where(row < half, 2 * row, 2 * (row - half) + 1)
        for at_source, (key_ref, count, number) in enumerate(zip(key_refs, counts, blocks)):

            def one(index, carry, at_source=at_source, key_ref=key_ref, count=count):
                start = pl.multiple_of(index * half, half)
                keys = doubled([key_ref[pl.ds(start, half), :]])
                cols = pl.ds(pl.multiple_of(at_source * pairs + start, half), half)
                values = jnp.concatenate([even_ref[:, cols], odd_ref[:, cols]], axis=1)

                def part(i, carry):
                    at = pl.ds(pl.multiple_of(i * step, step), step)
                    scores = jnp.where(token < count - index * block, matmul(keys, q2_ref[:, at]), LOW)
                    before = top_ref[:, at]
                    top = jnp.maximum(before, jnp.max(scores, axis=0, keepdims=True))
                    weights = jnp.exp2(scores - top[:1]).astype(jnp.bfloat16)
                    acc_ref[:, at] = acc_ref[:, at] * jnp.exp2(before - top)[:1] + matmul(values, weights)
                    top_ref[:, at] = top
                    return carry

                return lax.fori_loop(0, tokens // step, part, carry)

            lax.fori_loop(0, number, one, 0)

        if not final:
            rows = acc_ref[...]
            sums = rows[size : size + 1]
            row = lax.broadcasted_iota(jnp.int32, rows.shape, 0)
            acc_ref[...] = jnp.where(row < size, rows / sums, top_ref[:1, :] + jnp.log2(sums))

    if not final:
        mark_ref[...] = jnp.broadcast_to(jnp.where(safe, 0.0, 1.0), mark_ref.shape)
        return
    rows = acc_ref[...]
    if has_state:
        rows = rows + state_ref[...] * jnp.where(safe, 1.0, 0.0)
    result = rows[:size] / rows[size : size + 1]
    result = jnp.transpose(jnp.concatenate([result[:, :pairs], result[:, pairs:]], axis=0))
    out_ref[...] = result.astype(out_ref.dtype).reshape(out_ref.shape)


def attend(meta, queries, within, first_head, heads, sources, state, dests, out, name):
    pairs = queries.shape[1] // 2
    head_size = LANES // 2
    scale = math.log2(math.e) / math.sqrt(head_size)
    half = min(128, pairs)
    width = min(WIDTH, 2 * pairs)
    depth = head_size + 16

    def spec(lead, part, start):
        if lead is None:
            return pl.BlockSpec((None, pairs, LANES), lambda h, m: (h + start, part, 0))
        return pl.BlockSpec((None, None, pairs, LANES), lambda h, m: (lead, h + start, part, 0))

    in_specs, arrays = [spec(None, within, first_head)], [queries]
    for part in (1, 2):
        for source in sources:
            array, lead, part_of, start = source[part]
            in_specs.append(spec(lead, part_of, start))
            arrays.append(array)
    shapes = [(depth, 2 * pairs), (8, LANES)]
    if state is not None:
        sums, marks, start = state
        in_specs += [pl.BlockSpec((None, *shape), lambda h, m: (h + start, 0, 0)) for shape in shapes]
        arrays += [sums, marks]
    aliases = {}
    if dests is None:
        out_shape = [jax.ShapeDtypeStruct((heads, *shape), jnp.float32) for shape in shapes]
        out_spec = [pl.BlockSpec((None, *shape), lambda h, m: (h, 0, 0)) for shape in shapes]
    else:
        out_shape = jax.ShapeDtypeStruct((2 * dests, heads, pairs // dests, LANES), jnp.bfloat16)
        out_spec = pl.BlockSpec((dests, 1, pairs // dests, LANES), lambda h, m: (within, h, 0, 0))
        if out is not None:
            in_specs.append(pl.BlockSpec(memory_space=pl.ANY))
            aliases = {1 + len(arrays): 0}
            arrays.append(out)
    unpacked = len(sources) * pairs
    work = heads * len(sources) * (2 * pairs) ** 2
    return pl.pallas_call(
        functools.partial(
            attend_kernel,
            tuple(source[0] for source in sources),
            scale,
            half,
            width,
            state is not None,
            dests is not None,
        ),
        out_shape=out_shape,
        grid_spec=pltpu.PrefetchScalarGridSpec(
            num_scalar_prefetch=1,
            grid=(heads,),
            in_specs=in_specs,
            out_specs=out_spec,
            scratch_shapes=[
                pltpu.VMEM((LANES, 2 * pairs), jnp.bfloat16),
                pltpu.VMEM((depth, unpacked), jnp.bfloat16),
                pltpu.VMEM((depth, unpacked), jnp.bfloat16),
                pltpu.VMEM((depth, 2 * pairs), jnp.float32),
                pltpu.VMEM((8, 2 * pairs), jnp.float32),
            ],
        ),
        input_output_aliases=aliases,
        compiler_params=pltpu.CompilerParams(vmem_limit_bytes=VMEM),
        cost_estimate=pl.CostEstimate(
            flops=work * 4 * head_size * 4, bytes_accessed=8 * heads * pairs * LANES * 2, transcendentals=work
        ),
        name=name,
    )(meta, *arrays)


def project_kernel(layout, rows, weight_ref, *refs):
    parts, out_ref = refs[:-1], refs[-1]
    lane = lax.broadcasted_iota(jnp.int32, (rows, LANES), 1) < LANES // 2
    even, odd = [], []
    for first in range(0, len(layout), 2):
        (p, s, k), (p2, s2, k2) = layout[first], layout[first + 1]
        a = parts[p][s, k].astype(jnp.float32)
        b = parts[p2][s2, k2].astype(jnp.float32)
        even.append(jnp.where(lane, a, swapped(b)).astype(jnp.bfloat16))
        odd.append(jnp.where(lane, swapped(a), b).astype(jnp.bfloat16))
    stacked = jnp.concatenate([jnp.concatenate(even, axis=1), jnp.concatenate(odd, axis=1)], axis=0)
    token = lax.broadcasted_iota(jnp.int32, (2 * rows, 2 * rows), 0)
    place = lax.broadcasted_iota(jnp.int32, (2 * rows, 2 * rows), 1)
    order = (place == token // 2 + (token % 2) * rows).astype(jnp.bfloat16)
    tokens = jnp.dot(order, stacked, preferred_element_type=jnp.float32).astype(jnp.bfloat16)
    out_ref[...] = jnp.dot(tokens, weight_ref[...], preferred_element_type=jnp.float32).astype(out_ref.dtype)


def project(parts, layout, weight):
    pairs = parts[0].shape[2]
    rows = LANES if pairs % LANES == 0 else pairs
    return pl.pallas_call(
        functools.partial(project_kernel, layout, rows),
        out_shape=jax.ShapeDtypeStruct((2 * pairs, weight.shape[1]), jnp.bfloat16),
        grid=(pairs // rows,),
        in_specs=[pl.BlockSpec(weight.shape, lambda i: (0, 0))]
        + [pl.BlockSpec((*part.shape[:2], rows, LANES), lambda i: (0, 0, i, 0)) for part in parts],
        out_specs=pl.BlockSpec((2 * rows, weight.shape[1]), lambda i: (i, 0)),
        compiler_params=pltpu.CompilerParams(vmem_limit_bytes=VMEM // 3),
        name="project",
    )(weight, *parts)


def shifted(x, pairs):
    return lax.ppermute(x, "frame", pairs)


def shards(query_proj, key_proj, value_proj, lengths, out_weight):
    devices = lax.axis_size("frame")
    groups = lax.axis_size("head")
    index = lax.axis_index("frame")
    heads, rows, _ = query_proj.shape
    half = rows // 2
    frames = lengths.shape[0]
    weight = lax.all_gather(out_weight, "head", axis=0, tiled=True)

    wanted = jnp.stack([2 * index + within - stride for within in range(2) for stride in STRIDES])
    table = jnp.arange(frames, dtype=jnp.int32)
    meta = jnp.sum(jnp.where(wanted[:, None] == table[None, :], lengths[None, :], 0), axis=1, dtype=jnp.int32)
    meta = jnp.minimum(meta, rows)

    size = heads // 2 if heads % 2 == 0 else heads
    starts = range(0, heads, size)
    last = jnp.stack((key_proj[:, half:], value_proj[:, half:]))
    first = jnp.stack((key_proj[:, :half], value_proj[:, :half]))
    by_two = [(i, i + 2) for i in range(devices - 2)]
    near_last = shifted(last, by_two)
    near_first = shifted(first, by_two)
    far = None
    if devices > 8:
        both = jnp.stack((key_proj, value_proj))
        far = shifted(both, [(i, i + 8) for i in range(devices - 8)])

    def own(slot, part, start):
        return slot, (key_proj, None, part, start), (value_proj, None, part, start)

    def moved(slot, array, part, start):
        return slot, (array, 0, part, start), (array, 1, part, start)

    sums_first, marks_first = attend(meta, query_proj, 0, 0, heads, [own(0, 0, 0)], None, None, None, "first_own")
    state_last = {}
    for start in starts[:-1]:
        sources = [own(4, 1, start), own(5, 0, start)]
        sums, marks = attend(meta, query_proj, 1, start, size, sources, None, None, None, "last_own")
        state_last[start] = (sums, marks, 0)
    to_even = [(i + 1, i) for i in range(2, devices - 1, 2)]
    to_odd = [(i, i + 1) for i in range(0, devices - 1, 2)]
    prev = shifted(jnp.where(index % 2 == 0, last, near_last), to_even + to_odd)
    dests = groups // 2
    outs = []
    for start in starts:
        sources = [moved(6, near_last, 0, start)]
        if far is not None:
            sources.append(moved(7, far, 1, start))
        state = state_last.get(start)
        if state is None:
            sources += [own(4, 1, start), own(5, 0, start)]
        outs.append(attend(meta, query_proj, 1, start, size, sources, state, dests, None, "last_rest"))
    weight, *outs = lax.optimization_barrier((weight, *outs))
    got = []
    for number, start in enumerate(starts):
        sources = [moved(1, prev, 0, start), moved(2, near_first, 0, start)]
        if far is not None:
            sources.append(moved(3, far, 0, start))
        state = (sums_first, marks_first, start)
        out = attend(meta, query_proj, 0, start, size, sources, state, dests, outs[number], "first_rest")
        got.append(lax.all_to_all(out, "head", split_axis=0, concat_axis=0, tiled=True))
    layout = tuple(
        (head % heads // size, head // heads, head % heads % size) for head in range(groups * heads)
    )
    return project(got, layout, weight)


def solution(mesh):
    return jax.shard_map(
        shards,
        mesh=mesh,
        in_specs=(
            P("head", "frame", None),
            P("head", "frame", None),
            P("head", "frame", None),
            P(),
            P("head", None),
        ),
        out_specs=P(("frame", "head"), None),
        check_vma=False,
    )
```

```python
import functools
import math

import jax
import jax.numpy as jnp
from jax import lax
from jax.experimental import pallas as pl
from jax.experimental.pallas import tpu as pltpu
from jax.sharding import PartitionSpec as P

LANES = 128
STRIDES = (0, 1, 4, 16)
VMEM = 63 * 1024 * 1024
LOW = -1e30
WIDTH = 256


def swapped(x):
    return pltpu.roll(x, LANES // 2, 1)


def doubled(blocks):
    mask = (lax.broadcasted_iota(jnp.int32, (16, LANES), 1) < LANES // 2).astype(blocks[0].dtype)[:1]
    even = [block * mask for block in blocks]
    odd = [block - part for block, part in zip(blocks, even)]
    return jnp.concatenate([part + swapped(part) for part in even + odd], axis=0)


def matmul(a, b):
    return jnp.dot(a, b, preferred_element_type=jnp.float32)


def attend_kernel(slots, scale, half, width, has_state, final, meta_ref, q_ref, *refs):
    refs = list(refs)
    key_refs = [refs.pop(0) for _ in slots]
    value_refs = [refs.pop(0) for _ in slots]
    if has_state:
        state_ref, marks_ref = refs.pop(0), refs.pop(0)
    if final:
        if len(refs) > 6:
            refs.pop(0)
        out_ref = refs.pop(0)
    else:
        out_ref, mark_ref = refs.pop(0), refs.pop(0)
    q2_ref, even_ref, odd_ref, acc_ref, top_ref = refs
    if not final:
        acc_ref = out_ref
    pairs = q_ref.shape[0]
    size = LANES // 2
    depth = acc_ref.shape[0]
    tokens = 2 * pairs
    block = 2 * half
    counts = [meta_ref[slot] for slot in slots]
    blocks = [(count + block - 1) // block for count in counts]
    total = sum(blocks)

    scaled = jnp.transpose(q_ref[...]).astype(jnp.float32) * scale
    high = scaled.astype(jnp.bfloat16)
    low = (scaled - high.astype(jnp.float32)).astype(jnp.bfloat16)
    q2_ref[:size, :pairs] = high[:size]
    q2_ref[size:, :pairs] = low[:size]
    q2_ref[:size, pairs:] = high[size:]
    q2_ref[size:, pairs:] = low[size:]
    acc_ref[...] = jnp.zeros(acc_ref.shape, acc_ref.dtype)

    largest = None
    for key_ref in key_refs:
        top = jnp.max(jnp.abs(key_ref[...]), axis=0, keepdims=True).astype(jnp.float32)
        largest = top if largest is None else jnp.maximum(largest, top)
    largest = jnp.broadcast_to(largest, (8, LANES))
    largest = jnp.maximum(largest, swapped(largest))
    key_square = jnp.sum(largest * largest) * 0.0625
    square = scaled * scaled
    query_square = jnp.max(
        jnp.maximum(
            jnp.sum(square[:size], axis=0, keepdims=True), jnp.sum(square[size:], axis=0, keepdims=True)
        )
    )
    safe = query_square * key_square * 1.01 < 1e4
    if has_state:
        safe = safe & (jnp.max(marks_ref[...]) == 0.0)

    for at, (value_ref, count) in enumerate(zip(value_refs, counts)):
        turned = jnp.transpose(value_ref[...])
        cols = slice(at * pairs, (at + 1) * pairs)
        for ref, part in ((even_ref, turned[:size]), (odd_ref, turned[size:])):
            ref[:size, cols] = part
            ref[size:, cols] = jnp.ones((depth - size, pairs), ref.dtype)

        @pl.when(count % block != 0)
        def _(at=at, count=count):
            start = pl.multiple_of(count // block * half, half)
            token = 2 * (start + lax.broadcasted_iota(jnp.int32, (depth, half), 1))
            cols = pl.ds(pl.multiple_of(at * pairs + start, half), half)
            for ref, later in ((even_ref, 0), (odd_ref, 1)):
                kept = jnp.where(token + later < count, ref[:, cols].astype(jnp.float32), 0.0)
                ref[:, cols] = kept.astype(ref.dtype)

    def place_of(index):
        which, start, rest = 0, 0, index
        for at, number in enumerate(blocks):
            here = (rest >= 0) & (rest < number)
            which = jnp.where(here, at, which)
            start = jnp.where(here, rest * half, start)
            rest = rest - number
        return which, pl.multiple_of(start, half)

    def keys_of(index):
        which, start = place_of(index)
        rows = pl.ds(start, half)
        keys = key_refs[0][rows, :]
        for at in range(1, len(slots)):
            keys = jnp.where(which == at, key_refs[at][rows, :], keys)
        return keys

    def values_at(first, number):
        cols = []
        for i in range(number):
            which, start = place_of(first + i)
            cols.append(pl.ds(pl.multiple_of(which * pairs + start, half), half))
        return jnp.concatenate([ref[:, at] for ref in (even_ref, odd_ref) for at in cols], axis=1)

    def tiles(parts):
        steps = []
        for first, number in parts:
            keys = doubled([keys_of(first + i) for i in range(number)])
            values = values_at(first, number)
            steps += [(keys, values, at) for at in range(0, tokens, width)]

        def scores_at(step):
            keys, _, at = step
            return matmul(keys, q2_ref[:, at : at + width])

        scores = scores_at(steps[0])
        for step, after in zip(steps, steps[1:] + [None]):
            _, values, at = step
            later = scores_at(after) if after is not None else None
            acc_ref[:, at : at + width] += matmul(values, jnp.exp2(scores).astype(jnp.bfloat16))
            scores = later

    @pl.when(safe)
    def _():
        def whole(index, carry):
            tiles([(index * 4, 2), (index * 4 + 2, 2)])
            return carry

        lax.fori_loop(0, total // 4, whole, 0)

        @pl.when(total % 4 >= 2)
        def _():
            tiles([(total // 4 * 4, 2)])

        @pl.when(total % 2 == 1)
        def _():
            tiles([(total - 1, 1)])

    @pl.when(jnp.logical_not(safe))
    def _():
        if has_state:
            marked = jnp.max(marks_ref[...]) > 0.0
            rows = state_ref[...]
            row = lax.broadcasted_iota(jnp.int32, rows.shape, 0)
            acc_ref[...] = jnp.where(marked & (row >= size), 1.0, rows)
            top_ref[...] = jnp.where(marked, rows[size : size + 8], 0.0)
        else:
            top_ref[...] = jnp.full(top_ref.shape, LOW)
        step = 2 * half
        row = lax.broadcasted_iota(jnp.int32, (block, step), 0)
        token = jnp.where(row < half, 2 * row, 2 * (row - half) + 1)
        for at_source, (key_ref, count, number) in enumerate(zip(key_refs, counts, blocks)):

            def one(index, carry, at_source=at_source, key_ref=key_ref, count=count):
                start = pl.multiple_of(index * half, half)
                keys = doubled([key_ref[pl.ds(start, half), :]])
                cols = pl.ds(pl.multiple_of(at_source * pairs + start, half), half)
                values = jnp.concatenate([even_ref[:, cols], odd_ref[:, cols]], axis=1)

                def part(i, carry):
                    at = pl.ds(pl.multiple_of(i * step, step), step)
                    scores = jnp.where(token < count - index * block, matmul(keys, q2_ref[:, at]), LOW)
                    before = top_ref[:, at]
                    top = jnp.maximum(before, jnp.max(scores, axis=0, keepdims=True))
                    weights = jnp.exp2(scores - top[:1]).astype(jnp.bfloat16)
                    acc_ref[:, at] = acc_ref[:, at] * jnp.exp2(before - top)[:1] + matmul(values, weights)
                    top_ref[:, at] = top
                    return carry

                return lax.fori_loop(0, tokens // step, part, carry)

            lax.fori_loop(0, number, one, 0)

        if not final:
            rows = acc_ref[...]
            sums = rows[size : size + 1]
            row = lax.broadcasted_iota(jnp.int32, rows.shape, 0)
            acc_ref[...] = jnp.where(row < size, rows / sums, top_ref[:1, :] + jnp.log2(sums))

    if not final:
        mark_ref[...] = jnp.broadcast_to(jnp.where(safe, 0.0, 1.0), mark_ref.shape)
        return
    rows = acc_ref[...]
    if has_state:
        rows = rows + state_ref[...] * jnp.where(safe, 1.0, 0.0)
    result = (rows[:size] * (1.0 / rows[size : size + 1])).astype(out_ref.dtype)
    result = jnp.transpose(jnp.concatenate([result[:, :pairs], result[:, pairs:]], axis=0))
    out_ref[...] = result.reshape(out_ref.shape)


def attend(meta, queries, within, first_head, heads, sources, state, dests, out, name):
    pairs = queries.shape[1] // 2
    head_size = LANES // 2
    scale = math.log2(math.e) / math.sqrt(head_size)
    half = min(128, pairs)
    width = min(WIDTH, 2 * pairs)
    depth = head_size + 16

    def spec(lead, part, start):
        if lead is None:
            return pl.BlockSpec((None, pairs, LANES), lambda h, m: (h + start, part, 0))
        return pl.BlockSpec((None, None, pairs, LANES), lambda h, m: (lead, h + start, part, 0))

    in_specs, arrays = [spec(None, within, first_head)], [queries]
    for part in (1, 2):
        for source in sources:
            array, lead, part_of, start = source[part]
            in_specs.append(spec(lead, part_of, start))
            arrays.append(array)
    shapes = [(depth, 2 * pairs), (8, LANES)]
    if state is not None:
        sums, marks, start = state
        in_specs += [pl.BlockSpec((None, *shape), lambda h, m: (h + start, 0, 0)) for shape in shapes]
        arrays += [sums, marks]
    aliases = {}
    if dests is None:
        out_shape = [jax.ShapeDtypeStruct((heads, *shape), jnp.float32) for shape in shapes]
        out_spec = [pl.BlockSpec((None, *shape), lambda h, m: (h, 0, 0)) for shape in shapes]
    else:
        out_shape = jax.ShapeDtypeStruct((2 * dests, heads, pairs // dests, LANES), jnp.bfloat16)
        out_spec = pl.BlockSpec((dests, 1, pairs // dests, LANES), lambda h, m: (within, h, 0, 0))
        if out is not None:
            in_specs.append(pl.BlockSpec(memory_space=pl.ANY))
            aliases = {1 + len(arrays): 0}
            arrays.append(out)
    unpacked = len(sources) * pairs
    work = heads * len(sources) * (2 * pairs) ** 2
    return pl.pallas_call(
        functools.partial(
            attend_kernel,
            tuple(source[0] for source in sources),
            scale,
            half,
            width,
            state is not None,
            dests is not None,
        ),
        out_shape=out_shape,
        grid_spec=pltpu.PrefetchScalarGridSpec(
            num_scalar_prefetch=1,
            grid=(heads,),
            in_specs=in_specs,
            out_specs=out_spec,
            scratch_shapes=[
                pltpu.VMEM((LANES, 2 * pairs), jnp.bfloat16),
                pltpu.VMEM((depth, unpacked), jnp.bfloat16),
                pltpu.VMEM((depth, unpacked), jnp.bfloat16),
                pltpu.VMEM((depth, 2 * pairs), jnp.float32),
                pltpu.VMEM((8, 2 * pairs), jnp.float32),
            ],
        ),
        input_output_aliases=aliases,
        compiler_params=pltpu.CompilerParams(vmem_limit_bytes=VMEM),
        cost_estimate=pl.CostEstimate(
            flops=work * head_size * (16 if dests is None else 4), bytes_accessed=8 * heads * pairs * LANES * 2, transcendentals=work
        ),
        name=name,
    )(meta, *arrays)


def project_kernel(layout, rows, size, weight_ref, part_ref, *refs):
    out_ref = refs[-1]
    lane = lax.broadcasted_iota(jnp.int32, (rows, LANES), 1) < LANES // 2
    even, odd, weights = [], [], []
    for first in range(0, len(layout), 2):
        (s, k, head), (s2, k2, head2) = layout[first], layout[first + 1]
        a = part_ref[s, k].astype(jnp.float32)
        b = part_ref[s2, k2].astype(jnp.float32)
        even.append(jnp.where(lane, a, swapped(b)).astype(jnp.bfloat16))
        odd.append(jnp.where(lane, swapped(a), b).astype(jnp.bfloat16))
        weights += [weight_ref[h * size : (h + 1) * size, :] for h in (head, head2)]
    stacked = jnp.concatenate([jnp.concatenate(even, axis=1), jnp.concatenate(odd, axis=1)], axis=0)
    token = lax.broadcasted_iota(jnp.int32, (2 * rows, 2 * rows), 0)
    place = lax.broadcasted_iota(jnp.int32, (2 * rows, 2 * rows), 1)
    order = (place == token // 2 + (token % 2) * rows).astype(jnp.bfloat16)
    tokens = matmul(order, stacked).astype(jnp.bfloat16)
    result = matmul(tokens, jnp.concatenate(weights, axis=0))
    if len(refs) > 1:
        result = result + refs[0][...]
    out_ref[...] = result.astype(out_ref.dtype)


def project(part, layout, weight, before, last):
    pairs = part.shape[2]
    rows = LANES if pairs % LANES == 0 else pairs
    out = pl.BlockSpec((2 * rows, weight.shape[1]), lambda i: (i, 0))
    return pl.pallas_call(
        functools.partial(project_kernel, layout, rows, LANES // 2),
        out_shape=jax.ShapeDtypeStruct((2 * pairs, weight.shape[1]), jnp.bfloat16 if last else jnp.float32),
        grid=(pairs // rows,),
        in_specs=[
            pl.BlockSpec(weight.shape, lambda i: (0, 0)),
            pl.BlockSpec((*part.shape[:2], rows, LANES), lambda i: (0, 0, i, 0)),
        ]
        + [out] * (before is not None),
        out_specs=out,
        compiler_params=pltpu.CompilerParams(vmem_limit_bytes=VMEM // 3),
        cost_estimate=pl.CostEstimate(
            flops=4 * pairs * LANES // 2 * len(layout) * weight.shape[1], bytes_accessed=8 * 2**20, transcendentals=0
        ),
        name="project",
    )(weight, part, *([] if before is None else [before]))


def shifted(x, pairs):
    return lax.ppermute(x, "frame", pairs)


def shards(query_proj, key_proj, value_proj, lengths, out_weight):
    devices = lax.axis_size("frame")
    groups = lax.axis_size("head")
    index = lax.axis_index("frame")
    heads, rows, _ = query_proj.shape
    half = rows // 2
    frames = lengths.shape[0]
    weight = lax.all_gather(out_weight, "head", axis=0, tiled=True)

    wanted = jnp.stack([2 * index + within - stride for within in range(2) for stride in STRIDES])
    table = jnp.arange(frames, dtype=jnp.int32)
    meta = jnp.sum(jnp.where(wanted[:, None] == table[None, :], lengths[None, :], 0), axis=1, dtype=jnp.int32)
    meta = jnp.minimum(meta, rows)

    size = heads // 2 if heads % 2 == 0 else heads
    starts = range(0, heads, size)
    by_two = [(i, i + 2) for i in range(devices - 2)]
    first = jnp.stack((key_proj[:, :half], value_proj[:, :half]))
    lasts = [
        jnp.stack((key_proj[start : start + size, half:], value_proj[start : start + size, half:]))
        for start in starts
    ]
    near_lasts = [shifted(last, by_two) for last in lasts]
    far = None
    if devices > 8:
        both = jnp.stack((key_proj, value_proj))
        far = shifted(both, [(i, i + 8) for i in range(devices - 8)])

    def own(slot, part, start):
        return slot, (key_proj, None, part, start), (value_proj, None, part, start)

    def moved(slot, array, part, start):
        return slot, (array, 0, part, start), (array, 1, part, start)

    state_last = {}
    for start in starts[:-1]:
        sources = [own(4, 1, start), own(5, 0, start)]
        sums, marks = attend(meta, query_proj, 1, start, size, sources, None, None, None, "last_own")
        state_last[start] = (sums, marks, 0)
        first, near_lasts[0], sums = lax.optimization_barrier((first, near_lasts[0], sums))
        state_last[start] = (sums, marks, 0)
    near_first = shifted(first, by_two)
    near_lasts[0], held = lax.optimization_barrier((near_lasts[0], query_proj))
    sums_first, marks_first = attend(meta, held, 0, 0, heads, [own(0, 0, 0)], None, None, None, "first_own")
    if len(starts) > 1:
        near_lasts[1], sums_first = lax.optimization_barrier((near_lasts[1], sums_first))
    to_even = [(i + 1, i) for i in range(2, devices - 1, 2)]
    to_odd = [(i, i + 1) for i in range(0, devices - 1, 2)]
    prevs = [
        shifted(jnp.where(index % 2 == 0, last, near), to_even + to_odd) for last, near in zip(lasts, near_lasts)
    ]
    dests = groups // 2
    outs = []
    for number, start in enumerate(starts):
        sources = [moved(6, near_lasts[number], 0, 0)]
        if far is not None:
            sources.append(moved(7, far, 1, start))
        state = state_last.get(start)
        if state is None:
            sources += [own(4, 1, start), own(5, 0, start)]
        outs.append(attend(meta, query_proj, 1, start, size, sources, state, dests, None, "last_rest"))
    weight, *outs = lax.optimization_barrier((weight, *outs))
    result = None
    for number, start in enumerate(starts):
        sources = [moved(1, prevs[number], 0, 0), moved(2, near_first, 0, start)]
        if far is not None:
            sources.append(moved(3, far, 0, start))
        state = (sums_first, marks_first, start)
        out = attend(meta, query_proj, 0, start, size, sources, state, dests, outs[number], "first_rest")
        got = lax.all_to_all(out, "head", split_axis=0, concat_axis=0, tiled=True)
        layout = tuple(
            (head // heads, head % heads - start, head)
            for head in range(groups * heads)
            if start <= head % heads < start + size
        )
        result = project(got, layout, weight, result, start == starts[-1])
    return result


def solution(mesh):
    return jax.shard_map(
        shards,
        mesh=mesh,
        in_specs=(
            P("head", "frame", None),
            P("head", "frame", None),
            P("head", "frame", None),
            P(),
            P("head", None),
        ),
        out_specs=P(("frame", "head"), None),
        check_vma=False,
    )
```

```python
import functools
import math

import jax
import jax.numpy as jnp
from jax import lax
from jax.experimental import pallas as pl
from jax.experimental.pallas import tpu as pltpu
from jax.sharding import PartitionSpec as P

LANES = 128
STRIDES = (0, 1, 4, 16)
VMEM = 20 * 1024 * 1024
LOW = -1e30
WIDTH = 256


def swapped(x):
    return pltpu.roll(x, LANES // 2, 1)


def doubled(blocks):
    mask = (lax.broadcasted_iota(jnp.int32, (16, LANES), 1) < LANES // 2).astype(blocks[0].dtype)[:1]
    even = [block * mask for block in blocks]
    odd = [block - part for block, part in zip(blocks, even)]
    return jnp.concatenate([part + swapped(part) for part in even + odd], axis=0)


def matmul(a, b):
    return jnp.dot(a, b, preferred_element_type=jnp.float32)


def attend_kernel(slots, scale, half, width, has_state, final, meta_ref, q_ref, *refs):
    refs = list(refs)
    key_refs = [refs.pop(0) for _ in slots]
    value_refs = [refs.pop(0) for _ in slots]
    if has_state:
        state_ref, marks_ref = refs.pop(0), refs.pop(0)
    if final:
        if len(refs) > 6:
            refs.pop(0)
        out_ref = refs.pop(0)
    else:
        out_ref, mark_ref = refs.pop(0), refs.pop(0)
    q2_ref, even_ref, odd_ref, acc_ref, top_ref = refs
    if not final:
        acc_ref = out_ref
    pairs = q_ref.shape[0]
    size = LANES // 2
    depth = acc_ref.shape[0]
    tokens = 2 * pairs
    block = 2 * half
    counts = [meta_ref[slot] for slot in slots]
    blocks = [(count + block - 1) // block for count in counts]
    total = sum(blocks)

    scaled = jnp.transpose(q_ref[...]).astype(jnp.float32) * scale
    high = scaled.astype(jnp.bfloat16)
    low = (scaled - high.astype(jnp.float32)).astype(jnp.bfloat16)
    q2_ref[:size, :pairs] = high[:size]
    q2_ref[size:, :pairs] = low[:size]
    q2_ref[:size, pairs:] = high[size:]
    q2_ref[size:, pairs:] = low[size:]
    acc_ref[...] = jnp.zeros(acc_ref.shape, acc_ref.dtype)

    largest = None
    for key_ref in key_refs:
        top = jnp.max(jnp.abs(key_ref[...]), axis=0, keepdims=True).astype(jnp.float32)
        largest = top if largest is None else jnp.maximum(largest, top)
    largest = jnp.broadcast_to(largest, (8, LANES))
    largest = jnp.maximum(largest, swapped(largest))
    key_square = jnp.sum(largest * largest, axis=1, keepdims=True) * 0.5
    square = scaled * scaled
    longest = jnp.maximum(
        jnp.sum(square[:size], axis=0, keepdims=True), jnp.sum(square[size:], axis=0, keepdims=True)
    )
    product = jnp.max(longest, axis=1, keepdims=True) * key_square[:1]
    if has_state:
        product = jnp.where(marks_ref[:1, :1] > 0.0, 1e30, product)
    safe = jnp.max(product) * 1.01 < 1e4

    token = 2 * lax.broadcasted_iota(jnp.int32, (8, pairs), 1)
    for at, (value_ref, count) in enumerate(zip(value_refs, counts)):
        turned = jnp.transpose(value_ref[...])
        cols = slice(at * pairs, (at + 1) * pairs)
        for ref, part, later in ((even_ref, turned[:size], 0), (odd_ref, turned[size:], 1)):
            valid = (token + later < count).astype(jnp.float32)[:1].astype(ref.dtype)
            ref[:size, cols] = part * valid
            ref[size:, cols] = jnp.broadcast_to(valid, (depth - size, pairs))

    def place_of(index):
        which, start, rest = 0, 0, index
        for at, number in enumerate(blocks):
            here = (rest >= 0) & (rest < number)
            which = jnp.where(here, at, which)
            start = jnp.where(here, rest * half, start)
            rest = rest - number
        return which, pl.multiple_of(start, half)

    def keys_of(index):
        which, start = place_of(index)
        rows = pl.ds(start, half)
        keys = key_refs[0][rows, :]
        for at in range(1, len(slots)):
            keys = jnp.where(which == at, key_refs[at][rows, :], keys)
        return keys

    def values_at(first, number):
        cols = []
        for i in range(number):
            which, start = place_of(first + i)
            cols.append(pl.ds(pl.multiple_of(which * pairs + start, half), half))
        return jnp.concatenate([ref[:, at] for ref in (even_ref, odd_ref) for at in cols], axis=1)

    def tiles(parts):
        steps = []
        for first, number in parts:
            keys = doubled([keys_of(first + i) for i in range(number)])
            values = values_at(first, number)
            steps += [(keys, values, at) for at in range(0, tokens, width)]

        def scores_at(step):
            keys, _, at = step
            return matmul(keys, q2_ref[:, at : at + width])

        scores = scores_at(steps[0])
        for step, after in zip(steps, steps[1:] + [None]):
            _, values, at = step
            later = scores_at(after) if after is not None else None
            acc_ref[:, at : at + width] += matmul(values, jnp.exp2(scores).astype(jnp.bfloat16))
            scores = later

    @pl.when(safe)
    def _():
        def whole(index, carry):
            tiles([(index * 4, 2), (index * 4 + 2, 2)])
            return carry

        lax.fori_loop(0, total // 4, whole, 0)

        @pl.when(total % 4 >= 2)
        def _():
            tiles([(total // 4 * 4, 2)])

        @pl.when(total % 2 == 1)
        def _():
            tiles([(total - 1, 1)])

    @pl.when(jnp.logical_not(safe))
    def _():
        if has_state:
            marked = jnp.max(marks_ref[...]) > 0.0
            rows = state_ref[...]
            row = lax.broadcasted_iota(jnp.int32, rows.shape, 0)
            acc_ref[...] = jnp.where(marked & (row >= size), 1.0, rows)
            top_ref[...] = jnp.where(marked, rows[size : size + 8], 0.0)
        else:
            top_ref[...] = jnp.full(top_ref.shape, LOW)
        step = 2 * half
        row = lax.broadcasted_iota(jnp.int32, (block, step), 0)
        token = jnp.where(row < half, 2 * row, 2 * (row - half) + 1)
        for at_source, (key_ref, count, number) in enumerate(zip(key_refs, counts, blocks)):

            def one(index, carry, at_source=at_source, key_ref=key_ref, count=count):
                start = pl.multiple_of(index * half, half)
                keys = doubled([key_ref[pl.ds(start, half), :]])
                cols = pl.ds(pl.multiple_of(at_source * pairs + start, half), half)
                values = jnp.concatenate([even_ref[:, cols], odd_ref[:, cols]], axis=1)

                def part(i, carry):
                    at = pl.ds(pl.multiple_of(i * step, step), step)
                    scores = jnp.where(token < count - index * block, matmul(keys, q2_ref[:, at]), LOW)
                    before = top_ref[:, at]
                    top = jnp.maximum(before, jnp.max(scores, axis=0, keepdims=True))
                    weights = jnp.exp2(scores - top[:1]).astype(jnp.bfloat16)
                    acc_ref[:, at] = acc_ref[:, at] * jnp.exp2(before - top)[:1] + matmul(values, weights)
                    top_ref[:, at] = top
                    return carry

                return lax.fori_loop(0, tokens // step, part, carry)

            lax.fori_loop(0, number, one, 0)

        if not final:
            rows = acc_ref[...]
            sums = rows[size : size + 1]
            row = lax.broadcasted_iota(jnp.int32, rows.shape, 0)
            acc_ref[...] = jnp.where(row < size, rows / sums, top_ref[:1, :] + jnp.log2(sums))

    if not final:
        mark_ref[...] = jnp.broadcast_to(jnp.where(safe, 0.0, 1.0), mark_ref.shape)
        return
    rows = acc_ref[...]
    if has_state:
        rows = rows + state_ref[...] * jnp.where(safe, 1.0, 0.0)
    result = (rows[:size] * (1.0 / rows[size : size + 1])).astype(out_ref.dtype)
    result = jnp.transpose(jnp.concatenate([result[:, :pairs], result[:, pairs:]], axis=0))
    out_ref[...] = result.reshape(out_ref.shape)


def attend(meta, queries, within, first_head, heads, sources, state, dests, out, name):
    pairs = queries.shape[1] // 2
    head_size = LANES // 2
    scale = math.log2(math.e) / math.sqrt(head_size)
    half = min(128, pairs)
    width = min(WIDTH, 2 * pairs)
    depth = head_size + 16

    def spec(lead, part, start):
        if lead is None:
            return pl.BlockSpec((None, pairs, LANES), lambda h, m: (h + start, part, 0))
        return pl.BlockSpec((None, None, pairs, LANES), lambda h, m: (lead, h + start, part, 0))

    in_specs, arrays = [spec(None, within, first_head)], [queries]
    for part in (1, 2):
        for source in sources:
            array, lead, part_of, start = source[part]
            in_specs.append(spec(lead, part_of, start))
            arrays.append(array)
    shapes = [(depth, 2 * pairs), (8, LANES)]
    if state is not None:
        sums, marks, start = state
        in_specs += [pl.BlockSpec((None, *shape), lambda h, m: (h + start, 0, 0)) for shape in shapes]
        arrays += [sums, marks]
    aliases = {}
    if dests is None:
        out_shape = [jax.ShapeDtypeStruct((heads, *shape), jnp.float32) for shape in shapes]
        out_spec = [pl.BlockSpec((None, *shape), lambda h, m: (h, 0, 0)) for shape in shapes]
    else:
        out_shape = jax.ShapeDtypeStruct((2 * dests, heads, pairs // dests, LANES), jnp.bfloat16)
        out_spec = pl.BlockSpec((dests, 1, pairs // dests, LANES), lambda h, m: (within, h, 0, 0))
        if out is not None:
            in_specs.append(pl.BlockSpec(memory_space=pl.ANY))
            aliases = {1 + len(arrays): 0}
            arrays.append(out)
    unpacked = len(sources) * pairs
    work = heads * len(sources) * (2 * pairs) ** 2
    return pl.pallas_call(
        functools.partial(
            attend_kernel,
            tuple(source[0] for source in sources),
            scale,
            half,
            width,
            state is not None,
            dests is not None,
        ),
        out_shape=out_shape,
        grid_spec=pltpu.PrefetchScalarGridSpec(
            num_scalar_prefetch=1,
            grid=(heads,),
            in_specs=in_specs,
            out_specs=out_spec,
            scratch_shapes=[
                pltpu.VMEM((LANES, 2 * pairs), jnp.bfloat16),
                pltpu.VMEM((depth, unpacked), jnp.bfloat16),
                pltpu.VMEM((depth, unpacked), jnp.bfloat16),
                pltpu.VMEM((depth, 2 * pairs), jnp.float32),
                pltpu.VMEM((8, 2 * pairs), jnp.float32),
            ],
        ),
        input_output_aliases=aliases,
        compiler_params=pltpu.CompilerParams(vmem_limit_bytes=VMEM),
        cost_estimate=pl.CostEstimate(
            flops=work * head_size * (16 if dests is None else 4), bytes_accessed=8 * heads * pairs * LANES * 2, transcendentals=work
        ),
        name=name,
    )(meta, *arrays)


def project_kernel(layout, rows, size, weight_ref, part_ref, *refs):
    out_ref = refs[-1]
    lane = lax.broadcasted_iota(jnp.int32, (rows, LANES), 1) < LANES // 2
    even, odd, weights = [], [], []
    for first in range(0, len(layout), 2):
        (s, k, head), (s2, k2, head2) = layout[first], layout[first + 1]
        a = part_ref[s, k].astype(jnp.float32)
        b = part_ref[s2, k2].astype(jnp.float32)
        even.append(jnp.where(lane, a, swapped(b)).astype(jnp.bfloat16))
        odd.append(jnp.where(lane, swapped(a), b).astype(jnp.bfloat16))
        weights += [weight_ref[h * size : (h + 1) * size, :] for h in (head, head2)]
    stacked = jnp.concatenate([jnp.concatenate(even, axis=1), jnp.concatenate(odd, axis=1)], axis=0)
    token = lax.broadcasted_iota(jnp.int32, (2 * rows, 2 * rows), 0)
    place = lax.broadcasted_iota(jnp.int32, (2 * rows, 2 * rows), 1)
    order = (place == token // 2 + (token % 2) * rows).astype(jnp.bfloat16)
    tokens = matmul(order, stacked).astype(jnp.bfloat16)
    result = matmul(tokens, jnp.concatenate(weights, axis=0))
    if len(refs) > 1:
        result = result + refs[0][...]
    out_ref[...] = result.astype(out_ref.dtype)


def project(part, layout, weight, before, last):
    pairs = part.shape[2]
    rows = LANES if pairs % LANES == 0 else pairs
    out = pl.BlockSpec((2 * rows, weight.shape[1]), lambda i: (i, 0))
    return pl.pallas_call(
        functools.partial(project_kernel, layout, rows, LANES // 2),
        out_shape=jax.ShapeDtypeStruct((2 * pairs, weight.shape[1]), jnp.bfloat16 if last else jnp.float32),
        grid=(pairs // rows,),
        in_specs=[
            pl.BlockSpec(weight.shape, lambda i: (0, 0)),
            pl.BlockSpec((*part.shape[:2], rows, LANES), lambda i: (0, 0, i, 0)),
        ]
        + [out] * (before is not None),
        out_specs=out,
        compiler_params=pltpu.CompilerParams(vmem_limit_bytes=20 * 1024 * 1024),
        cost_estimate=pl.CostEstimate(
            flops=4 * pairs * LANES // 2 * len(layout) * weight.shape[1], bytes_accessed=8 * 2**20, transcendentals=0
        ),
        name="project",
    )(weight, part, *([] if before is None else [before]))


def shifted(x, pairs):
    return lax.ppermute(x, "frame", pairs)


def shards(query_proj, key_proj, value_proj, lengths, out_weight):
    devices = lax.axis_size("frame")
    groups = lax.axis_size("head")
    index = lax.axis_index("frame")
    heads, rows, _ = query_proj.shape
    half = rows // 2
    frames = lengths.shape[0]
    weight = lax.all_gather(out_weight, "head", axis=0, tiled=True)

    wanted = jnp.stack([2 * index + within - stride for within in range(2) for stride in STRIDES])
    table = jnp.arange(frames, dtype=jnp.int32)
    meta = jnp.sum(jnp.where(wanted[:, None] == table[None, :], lengths[None, :], 0), axis=1, dtype=jnp.int32)
    meta = jnp.minimum(meta, rows)

    size = heads // 2 if heads % 2 == 0 else heads
    starts = range(0, heads, size)
    by_two = [(i, i + 2) for i in range(devices - 2)]
    first = jnp.stack((key_proj[:, :half], value_proj[:, :half]))
    lasts = [
        jnp.stack((key_proj[start : start + size, half:], value_proj[start : start + size, half:]))
        for start in starts
    ]
    near_lasts = [shifted(last, by_two) for last in lasts]
    far = None
    if devices > 8:
        both = jnp.stack((key_proj, value_proj))
        far = shifted(both, [(i, i + 8) for i in range(devices - 8)])

    def own(slot, part, start):
        return slot, (key_proj, None, part, start), (value_proj, None, part, start)

    def moved(slot, array, part, start):
        return slot, (array, 0, part, start), (array, 1, part, start)

    state_last = {}
    for start in starts[:-1]:
        sources = [own(4, 1, start), own(5, 0, start)]
        sums, marks = attend(meta, query_proj, 1, start, size, sources, None, None, None, "last_own")
        state_last[start] = (sums, marks, 0)
        first, near_lasts[0], sums = lax.optimization_barrier((first, near_lasts[0], sums))
        state_last[start] = (sums, marks, 0)
    near_first = shifted(first, by_two)
    near_lasts[0], held = lax.optimization_barrier((near_lasts[0], query_proj))
    sums_first, marks_first = attend(meta, held, 0, 0, heads, [own(0, 0, 0)], None, None, None, "first_own")
    if len(starts) > 1:
        near_lasts[1], sums_first = lax.optimization_barrier((near_lasts[1], sums_first))
    to_even = [(i + 1, i) for i in range(2, devices - 1, 2)]
    to_odd = [(i, i + 1) for i in range(0, devices - 1, 2)]
    prevs = [
        shifted(jnp.where(index % 2 == 0, last, near), to_even + to_odd) for last, near in zip(lasts, near_lasts)
    ]
    dests = groups // 2
    outs = []
    for number, start in enumerate(starts):
        sources = [moved(6, near_lasts[number], 0, 0)]
        if far is not None:
            sources.append(moved(7, far, 1, start))
        state = state_last.get(start)
        if state is None:
            sources += [own(4, 1, start), own(5, 0, start)]
        outs.append(attend(meta, query_proj, 1, start, size, sources, state, dests, None, "last_rest"))
    weight, *outs = lax.optimization_barrier((weight, *outs))
    result = None
    for number, start in enumerate(starts):
        sources = [moved(1, prevs[number], 0, 0), moved(2, near_first, 0, start)]
        if far is not None:
            sources.append(moved(3, far, 0, start))
        state = (sums_first, marks_first, start)
        out = attend(meta, query_proj, 0, start, size, sources, state, dests, outs[number], "first_rest")
        got = lax.all_to_all(out, "head", split_axis=0, concat_axis=0, tiled=True)
        layout = tuple(
            (head // heads, head % heads - start, head)
            for head in range(groups * heads)
            if start <= head % heads < start + size
        )
        result = project(got, layout, weight, result, start == starts[-1])
    return result


def solution(mesh):
    return jax.shard_map(
        shards,
        mesh=mesh,
        in_specs=(
            P("head", "frame", None),
            P("head", "frame", None),
            P("head", "frame", None),
            P(),
            P("head", None),
        ),
        out_specs=P(("frame", "head"), None),
        check_vma=False,
    )
```

```python
import functools
import math

import jax
import jax.numpy as jnp
from jax import lax
from jax.experimental import pallas as pl
from jax.experimental.pallas import tpu as pltpu
from jax.sharding import PartitionSpec as P

LANES = 128
STRIDES = (0, 1, 4, 16)
VMEM = 20 * 1024 * 1024
WHOLE = 63 * 1024 * 1024
LOW = -1e30
WIDTH = 256


def swapped(x):
    return pltpu.roll(x, LANES // 2, 1)


def unpacked(blocks):
    return jnp.concatenate(blocks + [swapped(block) for block in blocks], axis=0)[:, : LANES // 2]


def matmul(a, b):
    return jnp.dot(a, b, preferred_element_type=jnp.float32)


def attend_kernel(slots, scale, half, width, has_state, final, meta_ref, q_ref, *refs):
    refs = list(refs)
    key_refs = [refs.pop(0) for _ in slots]
    value_refs = [refs.pop(0) for _ in slots]
    if has_state:
        state_ref, marks_ref = refs.pop(0), refs.pop(0)
    if final:
        if len(refs) > 6:
            refs.pop(0)
        out_ref = refs.pop(0)
    else:
        out_ref, mark_ref = refs.pop(0), refs.pop(0)
    q2_ref, even_ref, odd_ref, acc_ref, top_ref = refs
    if not final:
        acc_ref = out_ref
    pairs = q_ref.shape[0]
    size = LANES // 2
    depth = acc_ref.shape[0]
    tokens = 2 * pairs
    block = 2 * half
    counts = [meta_ref[slot] for slot in slots]
    blocks = [(count + block - 1) // block for count in counts]
    total = sum(blocks)

    turned = jnp.transpose(q_ref[...])
    q2_ref[:, :pairs] = turned[:size]
    q2_ref[:, pairs:] = turned[size:]
    acc_ref[...] = jnp.zeros(acc_ref.shape, acc_ref.dtype)

    largest = None
    for key_ref in key_refs:
        top = jnp.max(jnp.abs(key_ref[...]), axis=0, keepdims=True).astype(jnp.float32)
        largest = top if largest is None else jnp.maximum(largest, top)
    largest = jnp.broadcast_to(largest, (8, LANES))
    largest = jnp.maximum(largest, swapped(largest))
    key_square = jnp.sum(largest * largest, axis=1, keepdims=True) * 0.5
    square = turned.astype(jnp.float32)
    square = square * square
    longest = jnp.maximum(
        jnp.sum(square[:size], axis=0, keepdims=True), jnp.sum(square[size:], axis=0, keepdims=True)
    )
    product = jnp.max(longest, axis=1, keepdims=True) * key_square[:1]
    if has_state:
        product = jnp.where(marks_ref[:1, :1] > 0.0, 1e30, product)
    safe = jnp.max(product) * (1.01 * scale * scale) < 1e4

    token = 2 * lax.broadcasted_iota(jnp.int32, (8, pairs), 1)
    for at, (value_ref, count) in enumerate(zip(value_refs, counts)):
        turned = jnp.transpose(value_ref[...])
        cols = slice(at * pairs, (at + 1) * pairs)
        for ref, part, later in ((even_ref, turned[:size], 0), (odd_ref, turned[size:], 1)):
            valid = (token + later < count).astype(jnp.float32)[:1].astype(ref.dtype)
            ref[:size, cols] = part * valid
            ref[size:, cols] = jnp.broadcast_to(valid, (depth - size, pairs))

    def place_of(index):
        which, start, rest = 0, 0, index
        for at, number in enumerate(blocks):
            here = (rest >= 0) & (rest < number)
            which = jnp.where(here, at, which)
            start = jnp.where(here, rest * half, start)
            rest = rest - number
        return which, pl.multiple_of(start, half)

    def keys_of(index):
        which, start = place_of(index)
        rows = pl.ds(start, half)
        keys = key_refs[0][rows, :]
        for at in range(1, len(slots)):
            keys = jnp.where(which == at, key_refs[at][rows, :], keys)
        return keys

    def values_at(first, number):
        cols = []
        for i in range(number):
            which, start = place_of(first + i)
            cols.append(pl.ds(pl.multiple_of(which * pairs + start, half), half))
        return jnp.concatenate([ref[:, at] for ref in (even_ref, odd_ref) for at in cols], axis=1)

    def tiles(parts):
        steps = []
        for first, number in parts:
            keys = unpacked([keys_of(first + i) for i in range(number)])
            values = values_at(first, number)
            steps += [(keys, values, at) for at in range(0, tokens, width)]

        def scores_at(step):
            keys, _, at = step
            return matmul(keys, q2_ref[:, at : at + width])

        scores = scores_at(steps[0])
        for step, after in zip(steps, steps[1:] + [None]):
            _, values, at = step
            later = scores_at(after) if after is not None else None
            acc_ref[:, at : at + width] += matmul(values, jnp.exp2(scores * scale).astype(jnp.bfloat16))
            scores = later

    @pl.when(safe)
    def _():
        def whole(index, carry):
            tiles([(index * 4, 2), (index * 4 + 2, 2)])
            return carry

        lax.fori_loop(0, total // 4, whole, 0)

        @pl.when(total % 4 >= 2)
        def _():
            tiles([(total // 4 * 4, 2)])

        @pl.when(total % 2 == 1)
        def _():
            tiles([(total - 1, 1)])

    @pl.when(jnp.logical_not(safe))
    def _():
        if has_state:
            marked = jnp.max(marks_ref[...]) > 0.0
            rows = state_ref[...]
            row = lax.broadcasted_iota(jnp.int32, rows.shape, 0)
            acc_ref[...] = jnp.where(marked & (row >= size), 1.0, rows)
            top_ref[...] = jnp.where(marked, rows[size : size + 8], 0.0)
        else:
            top_ref[...] = jnp.full(top_ref.shape, LOW)
        step = 2 * half
        row = lax.broadcasted_iota(jnp.int32, (block, step), 0)
        token = jnp.where(row < half, 2 * row, 2 * (row - half) + 1)
        for at_source, (key_ref, count, number) in enumerate(zip(key_refs, counts, blocks)):

            def one(index, carry, at_source=at_source, key_ref=key_ref, count=count):
                start = pl.multiple_of(index * half, half)
                keys = unpacked([key_ref[pl.ds(start, half), :]])
                cols = pl.ds(pl.multiple_of(at_source * pairs + start, half), half)
                values = jnp.concatenate([even_ref[:, cols], odd_ref[:, cols]], axis=1)

                def part(i, carry):
                    at = pl.ds(pl.multiple_of(i * step, step), step)
                    scores = jnp.where(token < count - index * block, matmul(keys, q2_ref[:, at]) * scale, LOW)
                    before = top_ref[:, at]
                    top = jnp.maximum(before, jnp.max(scores, axis=0, keepdims=True))
                    weights = jnp.exp2(scores - top[:1]).astype(jnp.bfloat16)
                    acc_ref[:, at] = acc_ref[:, at] * jnp.exp2(before - top)[:1] + matmul(values, weights)
                    top_ref[:, at] = top
                    return carry

                return lax.fori_loop(0, tokens // step, part, carry)

            lax.fori_loop(0, number, one, 0)

        if not final:
            rows = acc_ref[...]
            sums = rows[size : size + 1]
            row = lax.broadcasted_iota(jnp.int32, rows.shape, 0)
            acc_ref[...] = jnp.where(row < size, rows / sums, top_ref[:1, :] + jnp.log2(sums))

    if not final:
        mark_ref[...] = jnp.broadcast_to(jnp.where(safe, 0.0, 1.0), mark_ref.shape)
        return
    rows = acc_ref[...]
    if has_state:
        rows = rows + state_ref[...] * jnp.where(safe, 1.0, 0.0)
    result = (rows[:size] * (1.0 / rows[size : size + 1])).astype(out_ref.dtype)
    result = jnp.transpose(jnp.concatenate([result[:, :pairs], result[:, pairs:]], axis=0))
    out_ref[...] = result.reshape(out_ref.shape)


def attend(meta, queries, within, first_head, heads, sources, state, dests, out, name):
    pairs = queries.shape[1] // 2
    head_size = LANES // 2
    scale = math.log2(math.e) / math.sqrt(head_size)
    half = min(128, pairs)
    width = min(WIDTH, 2 * pairs)
    depth = head_size + 16

    def spec(lead, part, start):
        if lead is None:
            return pl.BlockSpec((None, pairs, LANES), lambda h, m: (h + start, part, 0))
        return pl.BlockSpec((None, None, pairs, LANES), lambda h, m: (lead, h + start, part, 0))

    in_specs, arrays = [spec(None, within, first_head)], [queries]
    for part in (1, 2):
        for source in sources:
            array, lead, part_of, start = source[part]
            in_specs.append(spec(lead, part_of, start))
            arrays.append(array)
    shapes = [(depth, 2 * pairs), (8, LANES)]
    if state is not None:
        sums, marks, start = state
        in_specs += [pl.BlockSpec((None, *shape), lambda h, m: (h + start, 0, 0)) for shape in shapes]
        arrays += [sums, marks]
    aliases = {}
    if dests is None:
        out_shape = [jax.ShapeDtypeStruct((heads, *shape), jnp.float32) for shape in shapes]
        out_spec = [pl.BlockSpec((None, *shape), lambda h, m: (h, 0, 0)) for shape in shapes]
    else:
        out_shape = jax.ShapeDtypeStruct((2 * dests, heads, pairs // dests, LANES), jnp.bfloat16)
        out_spec = pl.BlockSpec((dests, 1, pairs // dests, LANES), lambda h, m: (within, h, 0, 0))
        if out is not None:
            in_specs.append(pl.BlockSpec(memory_space=pl.ANY))
            aliases = {1 + len(arrays): 0}
            arrays.append(out)
    unpacked = len(sources) * pairs
    work = heads * len(sources) * (2 * pairs) ** 2
    return pl.pallas_call(
        functools.partial(
            attend_kernel,
            tuple(source[0] for source in sources),
            scale,
            half,
            width,
            state is not None,
            dests is not None,
        ),
        out_shape=out_shape,
        grid_spec=pltpu.PrefetchScalarGridSpec(
            num_scalar_prefetch=1,
            grid=(heads,),
            in_specs=in_specs,
            out_specs=out_spec,
            scratch_shapes=[
                pltpu.VMEM((head_size, 2 * pairs), jnp.bfloat16),
                pltpu.VMEM((depth, unpacked), jnp.bfloat16),
                pltpu.VMEM((depth, unpacked), jnp.bfloat16),
                pltpu.VMEM((depth, 2 * pairs), jnp.float32),
                pltpu.VMEM((8, 2 * pairs), jnp.float32),
            ],
        ),
        input_output_aliases=aliases,
        compiler_params=pltpu.CompilerParams(vmem_limit_bytes=VMEM),
        cost_estimate=pl.CostEstimate(
            flops=work * head_size * (16 if dests is None else 4), bytes_accessed=8 * heads * pairs * LANES * 2, transcendentals=work
        ),
        name=name,
    )(meta, *arrays)


def project_kernel(rows, weight_ref, part_ref, *refs):
    out_ref = refs[-1]
    lane = lax.broadcasted_iota(jnp.int32, (rows, LANES), 1) < LANES // 2
    heads = [part_ref[s, k].astype(jnp.float32) for s in range(part_ref.shape[0]) for k in range(part_ref.shape[1])]
    even, odd = [], []
    for a, b in zip(heads[::2], heads[1::2]):
        even.append(jnp.where(lane, a, swapped(b)).astype(jnp.bfloat16))
        odd.append(jnp.where(lane, swapped(a), b).astype(jnp.bfloat16))
    stacked = jnp.concatenate([jnp.concatenate(even, axis=1), jnp.concatenate(odd, axis=1)], axis=0)
    token = lax.broadcasted_iota(jnp.int32, (2 * rows, 2 * rows), 0)
    place = lax.broadcasted_iota(jnp.int32, (2 * rows, 2 * rows), 1)
    order = (place == token // 2 + (token % 2) * rows).astype(jnp.bfloat16)
    tokens = matmul(order, stacked).astype(jnp.bfloat16)
    weight = weight_ref[...]
    result = matmul(tokens, weight.reshape(-1, weight.shape[-1]))
    if len(refs) > 1:
        result = result + refs[0][...].astype(jnp.float32)
    out_ref[...] = result.astype(out_ref.dtype)


def project(part, group, weight, before):
    pairs = part.shape[2]
    rows = LANES if pairs % LANES == 0 else pairs
    columns = weight.shape[3]
    out = pl.BlockSpec((2 * rows, columns), lambda i: (i, 0))
    return pl.pallas_call(
        functools.partial(project_kernel, rows),
        out_shape=jax.ShapeDtypeStruct((2 * pairs, columns), jnp.bfloat16),
        grid=(pairs // rows,),
        in_specs=[
            pl.BlockSpec((weight.shape[0], None, *weight.shape[2:]), lambda i: (0, group, 0, 0)),
            pl.BlockSpec((*part.shape[:2], rows, LANES), lambda i: (0, 0, i, 0)),
        ]
        + [out] * (before is not None),
        out_specs=out,
        compiler_params=pltpu.CompilerParams(vmem_limit_bytes=WHOLE),
        cost_estimate=pl.CostEstimate(
            flops=4 * pairs * weight.size // weight.shape[1], bytes_accessed=8 * 2**20, transcendentals=0
        ),
        name="project",
    )(weight, part, *([] if before is None else [before]))


def shifted(x, pairs):
    return lax.ppermute(x, "frame", pairs)


def shards(query_proj, key_proj, value_proj, lengths, out_weight):
    devices = lax.axis_size("frame")
    groups = lax.axis_size("head")
    index = lax.axis_index("frame")
    heads, rows, _ = query_proj.shape
    half = rows // 2
    frames = lengths.shape[0]
    weight = lax.all_gather(out_weight, "head", axis=0, tiled=True)

    wanted = jnp.stack([2 * index + within - stride for within in range(2) for stride in STRIDES])
    table = jnp.arange(frames, dtype=jnp.int32)
    meta = jnp.sum(jnp.where(wanted[:, None] == table[None, :], lengths[None, :], 0), axis=1, dtype=jnp.int32)
    meta = jnp.minimum(meta, rows)

    size = heads // 2 if heads % 2 == 0 else heads
    starts = range(0, heads, size)
    by_two = [(i, i + 2) for i in range(devices - 2)]
    first = jnp.stack((key_proj[:, :half], value_proj[:, :half]))
    lasts = [
        jnp.stack((key_proj[start : start + size, half:], value_proj[start : start + size, half:]))
        for start in starts
    ]
    near_lasts = [shifted(last, by_two) for last in lasts]
    near_first = shifted(first, by_two)
    far = None
    if devices > 8:
        both = jnp.stack((key_proj, value_proj))
        far = shifted(both, [(i, i + 8) for i in range(devices - 8)])

    def own(slot, part, start):
        return slot, (key_proj, None, part, start), (value_proj, None, part, start)

    def moved(slot, array, part, start):
        return slot, (array, 0, part, start), (array, 1, part, start)

    state_last = {}
    for start in starts[:-1]:
        sources = [own(4, 1, start), own(5, 0, start)]
        sums, marks = attend(meta, query_proj, 1, start, size, sources, None, None, None, "last_own")
        state_last[start] = (sums, marks, 0)
        near_lasts[0], sums = lax.optimization_barrier((near_lasts[0], sums))
        state_last[start] = (sums, marks, 0)
    near_lasts[0], held = lax.optimization_barrier((near_lasts[0], query_proj))
    sums_first, marks_first = attend(meta, held, 0, 0, heads, [own(0, 0, 0)], None, None, None, "first_own")
    if len(starts) > 1:
        near_lasts[1], sums_first = lax.optimization_barrier((near_lasts[1], sums_first))
    to_even = [(i + 1, i) for i in range(2, devices - 1, 2)]
    to_odd = [(i, i + 1) for i in range(0, devices - 1, 2)]
    prevs = [
        shifted(jnp.where(index % 2 == 0, last, near), to_even + to_odd) for last, near in zip(lasts, near_lasts)
    ]
    dests = groups // 2
    outs = []
    for number, start in enumerate(starts):
        sources = [moved(6, near_lasts[number], 0, 0)]
        if far is not None:
            sources.append(moved(7, far, 1, start))
        state = state_last.get(start)
        if state is None:
            sources += [own(4, 1, start), own(5, 0, start)]
        outs.append(attend(meta, query_proj, 1, start, size, sources, state, dests, None, "last_rest"))
    weight, *outs = lax.optimization_barrier((weight, *outs))
    weight = weight.reshape(groups, len(starts), size * LANES // 2, weight.shape[1])
    result = None
    for number, start in enumerate(starts):
        sources = [moved(1, prevs[number], 0, 0), moved(2, near_first, 0, start)]
        if far is not None:
            sources.append(moved(3, far, 0, start))
        state = (sums_first, marks_first, start)
        out = attend(meta, query_proj, 0, start, size, sources, state, dests, outs[number], "first_rest")
        got = lax.all_to_all(out, "head", split_axis=0, concat_axis=0, tiled=True)
        result = project(got, number, weight, result)
    return result


def solution(mesh):
    return jax.shard_map(
        shards,
        mesh=mesh,
        in_specs=(
            P("head", "frame", None),
            P("head", "frame", None),
            P("head", "frame", None),
            P(),
            P("head", None),
        ),
        out_specs=P(("frame", "head"), None),
        check_vma=False,
    )
```

```python
import functools
import math

import jax
import jax.numpy as jnp
from jax import lax
from jax.experimental import pallas as pl
from jax.experimental.pallas import tpu as pltpu
from jax.sharding import PartitionSpec as P

LANES = 128
STRIDES = (0, 1, 4, 16)
VMEM = 20 * 1024 * 1024
PROJECT = 63 * 1024 * 1024
LOW = -1e30
WIDTH = 256


def swapped(x):
    return pltpu.roll(x, LANES // 2, 1)


def unpacked(blocks):
    return jnp.concatenate(blocks + [swapped(block) for block in blocks], axis=0)[:, : LANES // 2]


def matmul(a, b):
    return jnp.dot(a, b, preferred_element_type=jnp.float32)


def attend_kernel(slots, scale, half, width, has_state, final, meta_ref, q_ref, *refs):
    refs = list(refs)
    key_refs = [refs.pop(0) for _ in slots]
    value_refs = [refs.pop(0) for _ in slots]
    if has_state:
        state_ref, marks_ref = refs.pop(0), refs.pop(0)
    if final:
        if len(refs) > 6:
            refs.pop(0)
        out_ref = refs.pop(0)
    else:
        out_ref, mark_ref = refs.pop(0), refs.pop(0)
    q2_ref, even_ref, odd_ref, acc_ref, top_ref = refs
    if not final:
        acc_ref = out_ref
    pairs = q_ref.shape[0]
    size = LANES // 2
    depth = acc_ref.shape[0]
    tokens = 2 * pairs
    block = 2 * half
    counts = [meta_ref[slot] for slot in slots]
    blocks = [(count + block - 1) // block for count in counts]
    total = sum(blocks)

    turned = jnp.transpose(q_ref[...])
    q2_ref[:, :pairs] = turned[:size]
    q2_ref[:, pairs:] = turned[size:]
    acc_ref[...] = jnp.zeros(acc_ref.shape, acc_ref.dtype)

    largest = None
    for key_ref in key_refs:
        top = jnp.max(jnp.abs(key_ref[...]), axis=0, keepdims=True).astype(jnp.float32)
        largest = top if largest is None else jnp.maximum(largest, top)
    largest = jnp.broadcast_to(largest, (8, LANES))
    largest = jnp.maximum(largest, swapped(largest))
    key_square = jnp.sum(largest * largest, axis=1, keepdims=True) * 0.5
    square = turned.astype(jnp.float32)
    square = square * square
    longest = jnp.maximum(
        jnp.sum(square[:size], axis=0, keepdims=True), jnp.sum(square[size:], axis=0, keepdims=True)
    )
    product = jnp.max(longest, axis=1, keepdims=True) * key_square[:1]
    if has_state:
        product = jnp.where(marks_ref[:1, :1] > 0.0, 1e30, product)
    safe = jnp.max(product) * (1.01 * scale * scale) < 1e4

    token = 2 * lax.broadcasted_iota(jnp.int32, (8, pairs), 1)
    for at, (value_ref, count) in enumerate(zip(value_refs, counts)):
        turned = jnp.transpose(value_ref[...])
        cols = slice(at * pairs, (at + 1) * pairs)
        for ref, part, later in ((even_ref, turned[:size], 0), (odd_ref, turned[size:], 1)):
            valid = (token + later < count).astype(jnp.float32)[:1].astype(ref.dtype)
            ref[:size, cols] = part * valid
            ref[size:, cols] = jnp.broadcast_to(valid, (depth - size, pairs))

    def place_of(index):
        which, start, rest = 0, 0, index
        for at, number in enumerate(blocks):
            here = (rest >= 0) & (rest < number)
            which = jnp.where(here, at, which)
            start = jnp.where(here, rest * half, start)
            rest = rest - number
        return which, pl.multiple_of(start, half)

    def keys_of(index):
        which, start = place_of(index)
        rows = pl.ds(start, half)
        keys = key_refs[0][rows, :]
        for at in range(1, len(slots)):
            keys = jnp.where(which == at, key_refs[at][rows, :], keys)
        return keys

    def values_at(first, number):
        cols = []
        for i in range(number):
            which, start = place_of(first + i)
            cols.append(pl.ds(pl.multiple_of(which * pairs + start, half), half))
        return jnp.concatenate([ref[:, at] for ref in (even_ref, odd_ref) for at in cols], axis=1)

    def tile(first, number):
        keys = unpacked([keys_of(first + i) for i in range(number)])
        values = values_at(first, number)
        scores = matmul(keys, q2_ref[:, :width])
        for at in range(0, tokens, width):
            after = at + width
            later = matmul(keys, q2_ref[:, after : after + width]) if after < tokens else None
            weights = jnp.exp2(scores * scale).astype(jnp.bfloat16)
            acc_ref[:, at:after] += matmul(values, weights)
            scores = later

    @pl.when(safe)
    def _():
        def whole(index, carry):
            tile(index * 2, 2)
            return carry

        lax.fori_loop(0, total // 2, whole, 0)

        @pl.when(total % 2 == 1)
        def _():
            tile(total - 1, 1)

    @pl.when(jnp.logical_not(safe))
    def _():
        if has_state:
            marked = jnp.max(marks_ref[...]) > 0.0
            rows = state_ref[...]
            row = lax.broadcasted_iota(jnp.int32, rows.shape, 0)
            acc_ref[...] = jnp.where(marked & (row >= size), 1.0, rows)
            top_ref[...] = jnp.where(marked, rows[size : size + 8], 0.0)
        else:
            top_ref[...] = jnp.full(top_ref.shape, LOW)
        step = 2 * half
        row = lax.broadcasted_iota(jnp.int32, (block, step), 0)
        token = jnp.where(row < half, 2 * row, 2 * (row - half) + 1)
        for at_source, (key_ref, count, number) in enumerate(zip(key_refs, counts, blocks)):

            def one(index, carry, at_source=at_source, key_ref=key_ref, count=count):
                start = pl.multiple_of(index * half, half)
                keys = unpacked([key_ref[pl.ds(start, half), :]])
                cols = pl.ds(pl.multiple_of(at_source * pairs + start, half), half)
                values = jnp.concatenate([even_ref[:, cols], odd_ref[:, cols]], axis=1)

                def part(i, carry):
                    at = pl.ds(pl.multiple_of(i * step, step), step)
                    scores = jnp.where(token < count - index * block, matmul(keys, q2_ref[:, at]) * scale, LOW)
                    before = top_ref[:, at]
                    top = jnp.maximum(before, jnp.max(scores, axis=0, keepdims=True))
                    weights = jnp.exp2(scores - top[:1]).astype(jnp.bfloat16)
                    acc_ref[:, at] = acc_ref[:, at] * jnp.exp2(before - top)[:1] + matmul(values, weights)
                    top_ref[:, at] = top
                    return carry

                return lax.fori_loop(0, tokens // step, part, carry)

            lax.fori_loop(0, number, one, 0)

        if not final:
            rows = acc_ref[...]
            sums = rows[size : size + 1]
            row = lax.broadcasted_iota(jnp.int32, rows.shape, 0)
            acc_ref[...] = jnp.where(row < size, rows / sums, top_ref[:1, :] + jnp.log2(sums))

    if not final:
        mark_ref[...] = jnp.broadcast_to(jnp.where(safe, 0.0, 1.0), mark_ref.shape)
        return
    rows = acc_ref[...]
    if has_state:
        rows = rows + state_ref[...] * jnp.where(safe, 1.0, 0.0)
    result = (rows[:size] * (1.0 / rows[size : size + 1])).astype(out_ref.dtype)
    result = jnp.transpose(jnp.concatenate([result[:, :pairs], result[:, pairs:]], axis=0))
    out_ref[...] = result.reshape(out_ref.shape)


def attend(meta, queries, within, first_head, heads, sources, state, dests, out, name):
    pairs = queries.shape[1] // 2
    head_size = LANES // 2
    scale = math.log2(math.e) / math.sqrt(head_size)
    half = min(128, pairs)
    width = min(WIDTH, 2 * pairs)
    depth = head_size + 16

    def spec(lead, part, start):
        if lead is None:
            return pl.BlockSpec((None, pairs, LANES), lambda h, m: (h + start, part, 0))
        return pl.BlockSpec((None, None, pairs, LANES), lambda h, m: (lead, h + start, part, 0))

    in_specs, arrays = [spec(None, within, first_head)], [queries]
    for part in (1, 2):
        for source in sources:
            array, lead, part_of, start = source[part]
            in_specs.append(spec(lead, part_of, start))
            arrays.append(array)
    shapes = [(depth, 2 * pairs), (8, LANES)]
    if state is not None:
        sums, marks, start = state
        in_specs += [pl.BlockSpec((None, *shape), lambda h, m: (h + start, 0, 0)) for shape in shapes]
        arrays += [sums, marks]
    aliases = {}
    if dests is None:
        out_shape = [jax.ShapeDtypeStruct((heads, *shape), jnp.float32) for shape in shapes]
        out_spec = [pl.BlockSpec((None, *shape), lambda h, m: (h, 0, 0)) for shape in shapes]
    else:
        out_shape = jax.ShapeDtypeStruct((2 * dests, heads, pairs // dests, LANES), jnp.bfloat16)
        out_spec = pl.BlockSpec((dests, 1, pairs // dests, LANES), lambda h, m: (within, h, 0, 0))
        if out is not None:
            in_specs.append(pl.BlockSpec(memory_space=pl.ANY))
            aliases = {1 + len(arrays): 0}
            arrays.append(out)
    unpacked = len(sources) * pairs
    work = heads * len(sources) * (2 * pairs) ** 2
    return pl.pallas_call(
        functools.partial(
            attend_kernel,
            tuple(source[0] for source in sources),
            scale,
            half,
            width,
            state is not None,
            dests is not None,
        ),
        out_shape=out_shape,
        grid_spec=pltpu.PrefetchScalarGridSpec(
            num_scalar_prefetch=1,
            grid=(heads,),
            in_specs=in_specs,
            out_specs=out_spec,
            scratch_shapes=[
                pltpu.VMEM((head_size, 2 * pairs), jnp.bfloat16),
                pltpu.VMEM((depth, unpacked), jnp.bfloat16),
                pltpu.VMEM((depth, unpacked), jnp.bfloat16),
                pltpu.VMEM((depth, 2 * pairs), jnp.float32),
                pltpu.VMEM((8, 2 * pairs), jnp.float32),
            ],
        ),
        input_output_aliases=aliases,
        compiler_params=pltpu.CompilerParams(vmem_limit_bytes=VMEM),
        cost_estimate=pl.CostEstimate(
            flops=work * head_size * (16 if dests is None else 4), bytes_accessed=8 * heads * pairs * LANES * 2, transcendentals=work
        ),
        name=name,
    )(meta, *arrays)


def project_kernel(rows, weight_ref, part_ref, *refs):
    out_ref, tokens_ref = refs[-2:]

    @pl.when(pl.program_id(0) == 0)
    def _():
        lane = lax.broadcasted_iota(jnp.int32, (rows, LANES), 1) < LANES // 2
        token = lax.broadcasted_iota(jnp.int32, (2 * rows, 2 * rows), 0)
        place = lax.broadcasted_iota(jnp.int32, (2 * rows, 2 * rows), 1)
        order = (place == token // 2 + (token % 2) * rows).astype(jnp.bfloat16)
        names = [(s, k) for s in range(part_ref.shape[0]) for k in range(part_ref.shape[1])]
        for start in range(0, part_ref.shape[2], rows):
            even, odd = [], []
            for first, second in zip(names[::2], names[1::2]):
                a = part_ref[(*first, pl.ds(start, rows))].astype(jnp.float32)
                b = part_ref[(*second, pl.ds(start, rows))].astype(jnp.float32)
                even.append(jnp.where(lane, a, swapped(b)).astype(jnp.bfloat16))
                odd.append(jnp.where(lane, swapped(a), b).astype(jnp.bfloat16))
            stacked = jnp.concatenate([jnp.concatenate(even, axis=1), jnp.concatenate(odd, axis=1)], axis=0)
            tokens_ref[2 * start : 2 * (start + rows)] = matmul(order, stacked).astype(jnp.bfloat16)

    weight = weight_ref[...]
    result = matmul(tokens_ref[...], weight.reshape(-1, weight.shape[-1]))
    if len(refs) > 2:
        result = result + refs[0][...].astype(jnp.float32)
    out_ref[...] = result.astype(out_ref.dtype)


def project(part, group, weight, before):
    pairs = part.shape[2]
    rows = LANES if pairs % LANES == 0 else pairs
    columns = weight.shape[3]
    width = min(2 * LANES, columns)
    out = pl.BlockSpec((2 * pairs, width), lambda i: (0, i))
    return pl.pallas_call(
        functools.partial(project_kernel, rows),
        out_shape=jax.ShapeDtypeStruct((2 * pairs, columns), jnp.bfloat16),
        grid=(columns // width,),
        in_specs=[
            pl.BlockSpec((weight.shape[0], None, weight.shape[2], width), lambda i: (0, group, 0, i)),
            pl.BlockSpec(part.shape, lambda i: (0, 0, 0, 0)),
        ]
        + [out] * (before is not None),
        out_specs=out,
        scratch_shapes=[pltpu.VMEM((2 * pairs, weight.size // weight.shape[1] // columns), jnp.bfloat16)],
        compiler_params=pltpu.CompilerParams(vmem_limit_bytes=PROJECT),
        cost_estimate=pl.CostEstimate(
            flops=4 * pairs * weight.size // weight.shape[1], bytes_accessed=8 * 2**20, transcendentals=0
        ),
        name="project",
    )(weight, part, *([] if before is None else [before]))


def shifted(x, pairs):
    return lax.ppermute(x, "frame", pairs)


def shards(query_proj, key_proj, value_proj, lengths, out_weight):
    devices = lax.axis_size("frame")
    groups = lax.axis_size("head")
    index = lax.axis_index("frame")
    heads, rows, _ = query_proj.shape
    half = rows // 2
    frames = lengths.shape[0]
    weight = lax.all_gather(out_weight, "head", axis=0, tiled=True)

    wanted = jnp.stack([2 * index + within - stride for within in range(2) for stride in STRIDES])
    table = jnp.arange(frames, dtype=jnp.int32)
    meta = jnp.sum(jnp.where(wanted[:, None] == table[None, :], lengths[None, :], 0), axis=1, dtype=jnp.int32)
    meta = jnp.minimum(meta, rows)

    size = heads // 2 if heads % 2 == 0 else heads
    starts = range(0, heads, size)
    by_two = [(i, i + 2) for i in range(devices - 2)]
    lasts, firsts = [
        [jnp.stack((key_proj[cut, rows], value_proj[cut, rows])) for cut in (slice(at, at + size) for at in starts)]
        for rows in (slice(half, None), slice(half))
    ]
    near_lasts = [shifted(last, by_two) for last in lasts]
    near_firsts = [shifted(firsts[0], by_two)]
    far = None
    if devices > 8:
        both = jnp.stack((key_proj, value_proj))
        far = shifted(both, [(i, i + 8) for i in range(devices - 8)])

    def own(slot, part, start):
        return slot, (key_proj, None, part, start), (value_proj, None, part, start)

    def moved(slot, array, part, start):
        return slot, (array, 0, part, start), (array, 1, part, start)

    state_last = {}
    for start in starts[:-1]:
        sources = [own(4, 1, start), own(5, 0, start)]
        sums, marks = attend(meta, query_proj, 1, start, size, sources, None, None, None, "last_own")
        state_last[start] = (sums, marks, 0)
        near_lasts[0], sums, marks, *firsts[1:] = lax.optimization_barrier((near_lasts[0], sums, marks, *firsts[1:]))
        state_last[start] = (sums, marks, 0)
    near_firsts += [shifted(first, by_two) for first in firsts[1:]]
    near_lasts[0], held = lax.optimization_barrier((near_lasts[0], query_proj))
    sums_first, marks_first = attend(meta, held, 0, 0, heads, [own(0, 0, 0)], None, None, None, "first_own")
    if len(starts) > 1:
        near_lasts[1], sums_first = lax.optimization_barrier((near_lasts[1], sums_first))
    to_even = [(i + 1, i) for i in range(2, devices - 1, 2)]
    to_odd = [(i, i + 1) for i in range(0, devices - 1, 2)]
    prevs = [
        shifted(jnp.where(index % 2 == 0, last, near), to_even + to_odd) for last, near in zip(lasts, near_lasts)
    ]
    dests = groups // 2
    outs = []
    for number, start in enumerate(starts):
        sources = [moved(6, near_lasts[number], 0, 0)]
        if far is not None:
            sources.append(moved(7, far, 1, start))
        state = state_last.get(start)
        if state is None:
            sources += [own(4, 1, start), own(5, 0, start)]
        outs.append(attend(meta, query_proj, 1, start, size, sources, state, dests, None, "last_rest"))
    weight, *outs = lax.optimization_barrier((weight, *outs))
    weight = weight.reshape(groups, len(starts), size * LANES // 2, weight.shape[1])
    result = None
    for number, start in enumerate(starts):
        sources = [moved(1, prevs[number], 0, 0), moved(2, near_firsts[number], 0, 0)]
        if far is not None:
            sources.append(moved(3, far, 0, start))
        state = (sums_first, marks_first, start)
        out = attend(meta, query_proj, 0, start, size, sources, state, dests, outs[number], "first_rest")
        got = lax.all_to_all(out, "head", split_axis=0, concat_axis=0, tiled=True)
        result = project(got, number, weight, result)
    return result


def solution(mesh):
    return jax.shard_map(
        shards,
        mesh=mesh,
        in_specs=(
            P("head", "frame", None),
            P("head", "frame", None),
            P("head", "frame", None),
            P(),
            P("head", None),
        ),
        out_specs=P(("frame", "head"), None),
        check_vma=False,
    )
```

```python
import functools
import math

import jax
import jax.numpy as jnp
from jax import lax
from jax.experimental import pallas as pl
from jax.experimental.pallas import tpu as pltpu
from jax.sharding import PartitionSpec as P

LANES = 128
STRIDES = (0, 1, 4, 16)
VMEM = 20 * 1024 * 1024
LOW = -1e30
WIDTH = 256


def swapped(x):
    return pltpu.roll(x, LANES // 2, 1)


def unpacked(blocks):
    return jnp.concatenate(blocks + [swapped(block) for block in blocks], axis=0)[:, : LANES // 2]


def matmul(a, b):
    return jnp.dot(a, b, preferred_element_type=jnp.float32)


def attend_kernel(slots, scale, half, width, has_state, final, meta_ref, q_ref, *refs):
    refs = list(refs)
    key_refs = [refs.pop(0) for _ in slots]
    value_refs = [refs.pop(0) for _ in slots]
    if has_state:
        state_ref, marks_ref = refs.pop(0), refs.pop(0)
    if final:
        if len(refs) > 6:
            refs.pop(0)
        out_ref = refs.pop(0)
    else:
        out_ref, mark_ref = refs.pop(0), refs.pop(0)
    q2_ref, even_ref, odd_ref, acc_ref, top_ref = refs
    if not final:
        acc_ref = out_ref
    pairs = q_ref.shape[0]
    size = LANES // 2
    depth = acc_ref.shape[0]
    tokens = 2 * pairs
    block = 2 * half
    counts = [meta_ref[slot] for slot in slots]
    blocks = [(count + block - 1) // block for count in counts]
    total = sum(blocks)

    turned = jnp.transpose(q_ref[...])
    q2_ref[:, :pairs] = turned[:size]
    q2_ref[:, pairs:] = turned[size:]
    acc_ref[...] = jnp.zeros(acc_ref.shape, acc_ref.dtype)

    largest = None
    for key_ref in key_refs:
        top = jnp.max(jnp.abs(key_ref[...]), axis=0, keepdims=True).astype(jnp.float32)
        largest = top if largest is None else jnp.maximum(largest, top)
    largest = jnp.broadcast_to(largest, (8, LANES))
    largest = jnp.maximum(largest, swapped(largest))
    key_square = jnp.sum(largest * largest, axis=1, keepdims=True) * 0.5
    square = turned.astype(jnp.float32)
    square = square * square
    longest = jnp.maximum(
        jnp.sum(square[:size], axis=0, keepdims=True), jnp.sum(square[size:], axis=0, keepdims=True)
    )
    product = jnp.max(longest, axis=1, keepdims=True) * key_square[:1]
    if has_state:
        product = jnp.where(marks_ref[:1, :1] > 0.0, 1e30, product)
    safe = jnp.max(product) * (1.01 * scale * scale) < 1e4

    token = 2 * lax.broadcasted_iota(jnp.int32, (8, pairs), 1)
    for at, (value_ref, count) in enumerate(zip(value_refs, counts)):
        turned = jnp.transpose(value_ref[...])
        cols = slice(at * pairs, (at + 1) * pairs)
        for ref, part, later in ((even_ref, turned[:size], 0), (odd_ref, turned[size:], 1)):
            valid = (token + later < count).astype(jnp.float32)[:1].astype(ref.dtype)
            ref[:size, cols] = part * valid
            ref[size:, cols] = jnp.broadcast_to(valid, (depth - size, pairs))

    def place_of(index):
        which, start, rest = 0, 0, index
        for at, number in enumerate(blocks):
            here = (rest >= 0) & (rest < number)
            which = jnp.where(here, at, which)
            start = jnp.where(here, rest * half, start)
            rest = rest - number
        return which, pl.multiple_of(start, half)

    def keys_of(index):
        which, start = place_of(index)
        rows = pl.ds(start, half)
        keys = key_refs[0][rows, :]
        for at in range(1, len(slots)):
            keys = jnp.where(which == at, key_refs[at][rows, :], keys)
        return keys

    def values_at(first, number):
        cols = []
        for i in range(number):
            which, start = place_of(first + i)
            cols.append(pl.ds(pl.multiple_of(which * pairs + start, half), half))
        return jnp.concatenate([ref[:, at] for ref in (even_ref, odd_ref) for at in cols], axis=1)

    def tiles(parts):
        steps = []
        for first, number in parts:
            keys = unpacked([keys_of(first + i) for i in range(number)])
            values = values_at(first, number)
            steps += [(keys, values, at) for at in range(0, tokens, width)]

        def scores_at(step):
            keys, _, at = step
            return matmul(keys, q2_ref[:, at : at + width])

        scores = scores_at(steps[0])
        for step, after in zip(steps, steps[1:] + [None]):
            _, values, at = step
            later = scores_at(after) if after is not None else None
            acc_ref[:, at : at + width] += matmul(values, jnp.exp2(scores * scale).astype(jnp.bfloat16))
            scores = later

    @pl.when(safe)
    def _():
        def whole(index, carry):
            tiles([(index * 4, 2), (index * 4 + 2, 2)])
            return carry

        lax.fori_loop(0, total // 4, whole, 0)

        first = total // 4 * 4
        for rest in (1, 2, 3):

            @pl.when(total % 4 == rest)
            def _(rest=rest):
                tiles([(first, 2)] * (rest > 1) + [(total - 1, 1)] * (rest % 2))

    @pl.when(jnp.logical_not(safe))
    def _():
        if has_state:
            marked = jnp.max(marks_ref[...]) > 0.0
            rows = state_ref[...]
            row = lax.broadcasted_iota(jnp.int32, rows.shape, 0)
            acc_ref[...] = jnp.where(marked & (row >= size), 1.0, rows)
            top_ref[...] = jnp.where(marked, rows[size : size + 8], 0.0)
        else:
            top_ref[...] = jnp.full(top_ref.shape, LOW)
        step = 2 * half
        row = lax.broadcasted_iota(jnp.int32, (block, step), 0)
        token = jnp.where(row < half, 2 * row, 2 * (row - half) + 1)
        for at_source, (key_ref, count, number) in enumerate(zip(key_refs, counts, blocks)):

            def one(index, carry, at_source=at_source, key_ref=key_ref, count=count):
                start = pl.multiple_of(index * half, half)
                keys = unpacked([key_ref[pl.ds(start, half), :]])
                cols = pl.ds(pl.multiple_of(at_source * pairs + start, half), half)
                values = jnp.concatenate([even_ref[:, cols], odd_ref[:, cols]], axis=1)

                def part(i, carry):
                    at = pl.ds(pl.multiple_of(i * step, step), step)
                    scores = jnp.where(token < count - index * block, matmul(keys, q2_ref[:, at]) * scale, LOW)
                    before = top_ref[:, at]
                    top = jnp.maximum(before, jnp.max(scores, axis=0, keepdims=True))
                    weights = jnp.exp2(scores - top[:1]).astype(jnp.bfloat16)
                    acc_ref[:, at] = acc_ref[:, at] * jnp.exp2(before - top)[:1] + matmul(values, weights)
                    top_ref[:, at] = top
                    return carry

                return lax.fori_loop(0, tokens // step, part, carry)

            lax.fori_loop(0, number, one, 0)

        if not final:
            rows = acc_ref[...]
            sums = rows[size : size + 1]
            row = lax.broadcasted_iota(jnp.int32, rows.shape, 0)
            acc_ref[...] = jnp.where(row < size, rows / sums, top_ref[:1, :] + jnp.log2(sums))

    if not final:
        mark_ref[...] = jnp.broadcast_to(jnp.where(safe, 0.0, 1.0), mark_ref.shape)
        return
    rows = acc_ref[...]
    if has_state:
        rows = rows + state_ref[...] * jnp.where(safe, 1.0, 0.0)
    result = (rows[:size] * (1.0 / rows[size : size + 1])).astype(out_ref.dtype)
    result = jnp.transpose(jnp.concatenate([result[:, :pairs], result[:, pairs:]], axis=0))
    out_ref[...] = result.reshape(out_ref.shape)


def attend(meta, queries, within, first_head, heads, sources, state, dests, out, name):
    pairs = queries.shape[1] // 2
    head_size = LANES // 2
    scale = math.log2(math.e) / math.sqrt(head_size)
    half = min(128, pairs)
    width = min(WIDTH, 2 * pairs)
    depth = head_size + 16

    def spec(lead, part, start):
        if lead is None:
            return pl.BlockSpec((None, pairs, LANES), lambda h, m: (h + start, part, 0))
        return pl.BlockSpec((None, None, pairs, LANES), lambda h, m: (lead, h + start, part, 0))

    in_specs, arrays = [spec(None, within, first_head)], [queries]
    for part in (1, 2):
        for source in sources:
            array, lead, part_of, start = source[part]
            in_specs.append(spec(lead, part_of, start))
            arrays.append(array)
    shapes = [(depth, 2 * pairs), (8, LANES)]
    if state is not None:
        sums, marks, start = state
        in_specs += [pl.BlockSpec((None, *shape), lambda h, m: (h + start, 0, 0)) for shape in shapes]
        arrays += [sums, marks]
    aliases = {}
    if dests is None:
        out_shape = [jax.ShapeDtypeStruct((heads, *shape), jnp.float32) for shape in shapes]
        out_spec = [pl.BlockSpec((None, *shape), lambda h, m: (h, 0, 0)) for shape in shapes]
    else:
        out_shape = jax.ShapeDtypeStruct((2 * dests, heads, pairs // dests, LANES), jnp.bfloat16)
        out_spec = pl.BlockSpec((dests, 1, pairs // dests, LANES), lambda h, m: (within, h, 0, 0))
        if out is not None:
            in_specs.append(pl.BlockSpec(memory_space=pl.ANY))
            aliases = {1 + len(arrays): 0}
            arrays.append(out)
    unpacked = len(sources) * pairs
    work = heads * len(sources) * (2 * pairs) ** 2
    return pl.pallas_call(
        functools.partial(
            attend_kernel,
            tuple(source[0] for source in sources),
            scale,
            half,
            width,
            state is not None,
            dests is not None,
        ),
        out_shape=out_shape,
        grid_spec=pltpu.PrefetchScalarGridSpec(
            num_scalar_prefetch=1,
            grid=(heads,),
            in_specs=in_specs,
            out_specs=out_spec,
            scratch_shapes=[
                pltpu.VMEM((head_size, 2 * pairs), jnp.bfloat16),
                pltpu.VMEM((depth, unpacked), jnp.bfloat16),
                pltpu.VMEM((depth, unpacked), jnp.bfloat16),
                pltpu.VMEM((depth, 2 * pairs), jnp.float32),
                pltpu.VMEM((8, 2 * pairs), jnp.float32),
            ],
        ),
        input_output_aliases=aliases,
        compiler_params=pltpu.CompilerParams(vmem_limit_bytes=VMEM),
        cost_estimate=pl.CostEstimate(
            flops=work * head_size * (16 if dests is None else 4), bytes_accessed=8 * heads * pairs * LANES * 2, transcendentals=work
        ),
        name=name,
    )(meta, *arrays)


def project_kernel(rows, more, weight_ref, part_ref, *refs):
    refs = list(refs)
    tokens_ref = refs.pop()
    if more:
        refs.pop()[...] = refs.pop(0)[...]
    out_ref = refs.pop()

    @pl.when(pl.program_id(0) == 0)
    def _():
        lane = lax.broadcasted_iota(jnp.int32, (rows, LANES), 1) < LANES // 2
        token = lax.broadcasted_iota(jnp.int32, (2 * rows, 2 * rows), 0)
        place = lax.broadcasted_iota(jnp.int32, (2 * rows, 2 * rows), 1)
        order = (place == token // 2 + (token % 2) * rows).astype(jnp.bfloat16)
        names = [(s, k) for s in range(part_ref.shape[0]) for k in range(part_ref.shape[1])]
        for start in range(0, part_ref.shape[2], rows):
            even, odd = [], []
            for first, second in zip(names[::2], names[1::2]):
                a = part_ref[(*first, pl.ds(start, rows))].astype(jnp.float32)
                b = part_ref[(*second, pl.ds(start, rows))].astype(jnp.float32)
                even.append(jnp.where(lane, a, swapped(b)).astype(jnp.bfloat16))
                odd.append(jnp.where(lane, swapped(a), b).astype(jnp.bfloat16))
            stacked = jnp.concatenate([jnp.concatenate(even, axis=1), jnp.concatenate(odd, axis=1)], axis=0)
            tokens_ref[2 * start : 2 * (start + rows)] = matmul(order, stacked).astype(jnp.bfloat16)

    weight = weight_ref[...]
    result = matmul(tokens_ref[...], weight.reshape(-1, weight.shape[-1]))
    if refs:
        result = result + refs[0][...].astype(jnp.float32)
    out_ref[...] = result.astype(out_ref.dtype)


def project(part, weight, before, following):
    pairs = part.shape[2]
    rows = LANES if pairs % LANES == 0 else pairs
    devices, _, depth, columns = weight[0].shape
    width = min(2 * LANES, columns)

    def weights(group):
        return pl.BlockSpec((devices, None, depth, width), lambda i: (0, group, 0, i))

    out = pl.BlockSpec((2 * pairs, width), lambda i: (0, i))
    out_shape, out_specs = [jax.ShapeDtypeStruct((2 * pairs, columns), jnp.bfloat16)], [out]
    arrays, in_specs = [weight[0], part], [weights(weight[1]), pl.BlockSpec(part.shape, lambda i: (0, 0, 0, 0))]
    if following is not None:
        arrays.append(following[0])
        in_specs.append(weights(following[1]))
        out_shape.append(jax.ShapeDtypeStruct((devices, 1, depth, columns), jnp.bfloat16))
        out_specs.append(weights(0))
    if before is not None:
        arrays.append(before)
        in_specs.append(out)
    return pl.pallas_call(
        functools.partial(project_kernel, rows, following is not None),
        out_shape=out_shape,
        grid=(columns // width,),
        in_specs=in_specs,
        out_specs=out_specs,
        scratch_shapes=[pltpu.VMEM((2 * pairs, devices * depth), jnp.bfloat16)],
        compiler_params=pltpu.CompilerParams(vmem_limit_bytes=VMEM),
        cost_estimate=pl.CostEstimate(
            flops=4 * pairs * devices * depth * columns, bytes_accessed=8 * 2**20, transcendentals=0
        ),
        name="project",
    )(*arrays)


def pack_kernel(places, k_ref, v_ref, *refs):
    copies = [
        pltpu.make_async_copy(ref.at[place], out_ref.at[half], refs[-1].at[number, half])
        for number, (place, out_ref) in enumerate(zip(places, refs))
        for half, ref in enumerate((k_ref, v_ref))
    ]
    for copy in copies:
        copy.start()
    for copy in copies:
        copy.wait()


def pack(keys, values, places):
    return pl.pallas_call(
        functools.partial(
            pack_kernel, tuple((pl.ds(head, heads), pl.ds(row, rows)) for head, heads, row, rows in places)
        ),
        out_shape=[jax.ShapeDtypeStruct((2, heads, rows, LANES), keys.dtype) for _, heads, _, rows in places],
        in_specs=[pl.BlockSpec(memory_space=pl.ANY)] * 2,
        out_specs=[pl.BlockSpec(memory_space=pl.ANY)] * len(places),
        scratch_shapes=[pltpu.SemaphoreType.DMA((len(places), 2))],
        name="pack",
    )(keys, values)


def shifted(x, pairs):
    return lax.ppermute(x, "frame", pairs)


def shards(query_proj, key_proj, value_proj, lengths, out_weight):
    devices = lax.axis_size("frame")
    groups = lax.axis_size("head")
    index = lax.axis_index("frame")
    heads, rows, _ = query_proj.shape
    half = rows // 2
    frames = lengths.shape[0]
    weight = lax.all_gather(out_weight, "head", axis=0, tiled=True)

    wanted = jnp.stack([2 * index + within - stride for within in range(2) for stride in STRIDES])
    table = jnp.arange(frames, dtype=jnp.int32)
    meta = jnp.sum(jnp.where(wanted[:, None] == table[None, :], lengths[None, :], 0), axis=1, dtype=jnp.int32)
    meta = jnp.minimum(meta, rows)

    size = heads // 2 if heads % 2 == 0 else heads
    starts = range(0, heads, size)
    by_two = [(i, i + 2) for i in range(devices - 2)]
    places = [(start, size, row, half) for row in (half, 0) for start in starts]
    packed = list(pack(key_proj, value_proj, places))
    lasts, firsts = packed[: len(starts)], packed[len(starts) :]
    near_lasts = [shifted(last, by_two) for last in lasts]
    far = None
    if devices > 8:
        both = jnp.stack((key_proj, value_proj))
        far = shifted(both, [(i, i + 8) for i in range(devices - 8)])

    def own(slot, part, start):
        return slot, (key_proj, None, part, start), (value_proj, None, part, start)

    def moved(slot, array, part, start):
        return slot, (array, 0, part, start), (array, 1, part, start)

    state_last = {}
    for start in starts[:-1]:
        sources = [own(4, 1, start), own(5, 0, start)]
        sums, marks = attend(meta, query_proj, 1, start, size, sources, None, None, None, "last_own")
        state_last[start] = (sums, marks, 0)
        near_lasts[0], firsts[0], sums = lax.optimization_barrier((near_lasts[0], firsts[0], sums))
        state_last[start] = (sums, marks, 0)
    near_lasts[0], held = lax.optimization_barrier((near_lasts[0], query_proj))
    sums_first, marks_first = attend(meta, held, 0, 0, heads, [own(0, 0, 0)], None, None, None, "first_own")
    if len(starts) > 1:
        near_lasts[1], sums_first, *firsts[1:] = lax.optimization_barrier((near_lasts[1], sums_first, *firsts[1:]))
    near_firsts = [shifted(first, by_two) for first in firsts]
    to_even = [(i + 1, i) for i in range(2, devices - 1, 2)]
    to_odd = [(i, i + 1) for i in range(0, devices - 1, 2)]
    prevs = [
        shifted(jnp.where(index % 2 == 0, last, near), to_even + to_odd) for last, near in zip(lasts, near_lasts)
    ]
    dests = groups // 2
    outs = []
    for number, start in enumerate(starts):
        sources = [moved(6, near_lasts[number], 0, 0)]
        if far is not None:
            sources.append(moved(7, far, 1, start))
        state = state_last.get(start)
        if state is None:
            sources += [own(4, 1, start), own(5, 0, start)]
        outs.append(attend(meta, query_proj, 1, start, size, sources, state, dests, None, "last_rest"))
    weight, *outs = lax.optimization_barrier((weight, *outs))
    weight = weight.reshape(groups, len(starts), size * LANES // 2, weight.shape[1])
    result, weights = None, (weight, 0)
    for number, start in enumerate(starts):
        sources = [moved(1, prevs[number], 0, 0), moved(2, near_firsts[number], 0, 0)]
        if far is not None:
            sources.append(moved(3, far, 0, start))
        state = (sums_first, marks_first, start)
        out = attend(meta, query_proj, 0, start, size, sources, state, dests, outs[number], "first_rest")
        got = lax.all_to_all(out, "head", split_axis=0, concat_axis=0, tiled=True)
        following = (weight, number + 1) if number + 1 < len(starts) else None
        result, *handed = project(got, weights, result, following)
        weights = (handed[0], 0) if handed else None
    return result


def solution(mesh):
    return jax.shard_map(
        shards,
        mesh=mesh,
        in_specs=(
            P("head", "frame", None),
            P("head", "frame", None),
            P("head", "frame", None),
            P(),
            P("head", None),
        ),
        out_specs=P(("frame", "head"), None),
        check_vma=False,
    )
```

```python
import functools
import math

import jax
import jax.numpy as jnp
from jax import lax
from jax.experimental import pallas as pl
from jax.experimental.pallas import tpu as pltpu
from jax.sharding import PartitionSpec as P

LANES = 128
STRIDES = (0, 1, 4, 16)
VMEM = 20 * 1024 * 1024
WHOLE = 63 * 1024 * 1024
LOW = -1e30
WIDTH = 256


def swapped(x):
    return pltpu.roll(x, LANES // 2, 1)


def unpacked(blocks):
    return jnp.concatenate(blocks + [swapped(block) for block in blocks], axis=0)[:, : LANES // 2]


def matmul(a, b):
    return jnp.dot(a, b, preferred_element_type=jnp.float32)


def attend_kernel(slots, scale, half, width, has_state, final, meta_ref, q_ref, *refs):
    refs = list(refs)
    key_refs = [refs.pop(0) for _ in slots]
    value_refs = [refs.pop(0) for _ in slots]
    if has_state:
        state_ref, marks_ref = refs.pop(0), refs.pop(0)
    if final:
        if len(refs) > 6:
            refs.pop(0)
        out_ref = refs.pop(0)
    else:
        out_ref, mark_ref = refs.pop(0), refs.pop(0)
    q2_ref, even_ref, odd_ref, acc_ref, top_ref = refs
    if not final:
        acc_ref = out_ref
    pairs = q_ref.shape[0]
    size = LANES // 2
    depth = acc_ref.shape[0]
    tokens = 2 * pairs
    block = 2 * half
    counts = [meta_ref[slot] for slot in slots]
    blocks = [(count + block - 1) // block for count in counts]
    total = sum(blocks)

    turned = jnp.transpose(q_ref[...])
    q2_ref[:, :pairs] = turned[:size]
    q2_ref[:, pairs:] = turned[size:]
    acc_ref[...] = jnp.zeros(acc_ref.shape, acc_ref.dtype)

    largest = None
    for key_ref in key_refs:
        top = jnp.max(jnp.abs(key_ref[...]), axis=0, keepdims=True).astype(jnp.float32)
        largest = top if largest is None else jnp.maximum(largest, top)
    largest = jnp.broadcast_to(largest, (8, LANES))
    largest = jnp.maximum(largest, swapped(largest))
    key_square = jnp.sum(largest * largest, axis=1, keepdims=True) * 0.5
    square = turned.astype(jnp.float32)
    square = square * square
    longest = jnp.maximum(
        jnp.sum(square[:size], axis=0, keepdims=True), jnp.sum(square[size:], axis=0, keepdims=True)
    )
    product = jnp.max(longest, axis=1, keepdims=True) * key_square[:1]
    if has_state:
        product = jnp.where(marks_ref[:1, :1] > 0.0, 1e30, product)
    safe = jnp.max(product) * (1.01 * scale * scale) < 1e4

    token = 2 * lax.broadcasted_iota(jnp.int32, (8, pairs), 1)
    for at, (value_ref, count) in enumerate(zip(value_refs, counts)):
        turned = jnp.transpose(value_ref[...])
        cols = slice(at * pairs, (at + 1) * pairs)
        for ref, part, later in ((even_ref, turned[:size], 0), (odd_ref, turned[size:], 1)):
            valid = (token + later < count).astype(jnp.float32)[:1].astype(ref.dtype)
            ref[:size, cols] = part * valid
            ref[size:, cols] = jnp.broadcast_to(valid, (depth - size, pairs))

    def place_of(index):
        which, start, rest = 0, 0, index
        for at, number in enumerate(blocks):
            here = (rest >= 0) & (rest < number)
            which = jnp.where(here, at, which)
            start = jnp.where(here, rest * half, start)
            rest = rest - number
        return which, pl.multiple_of(start, half)

    def keys_of(index):
        which, start = place_of(index)
        rows = pl.ds(start, half)
        keys = key_refs[0][rows, :]
        for at in range(1, len(slots)):
            keys = jnp.where(which == at, key_refs[at][rows, :], keys)
        return keys

    def values_at(first, number):
        cols = []
        for i in range(number):
            which, start = place_of(first + i)
            cols.append(pl.ds(pl.multiple_of(which * pairs + start, half), half))
        return jnp.concatenate([ref[:, at] for ref in (even_ref, odd_ref) for at in cols], axis=1)

    def tiles(parts):
        steps = []
        for first, number in parts:
            keys = unpacked([keys_of(first + i) for i in range(number)])
            values = values_at(first, number)
            steps += [(keys, values, at) for at in range(0, tokens, width)]

        def scores_at(step):
            keys, _, at = step
            return matmul(keys, q2_ref[:, at : at + width])

        scores = scores_at(steps[0])
        for step, after in zip(steps, steps[1:] + [None]):
            _, values, at = step
            later = scores_at(after) if after is not None else None
            acc_ref[:, at : at + width] += matmul(values, jnp.exp2(scores * scale).astype(jnp.bfloat16))
            scores = later

    @pl.when(safe)
    def _():
        def whole(index, carry):
            tiles([(index * 4, 2), (index * 4 + 2, 2)])
            return carry

        lax.fori_loop(0, total // 4, whole, 0)

        first = total // 4 * 4
        for rest in (1, 2, 3):

            @pl.when(total % 4 == rest)
            def _(rest=rest):
                tiles([(first, 2)] * (rest > 1) + [(total - 1, 1)] * (rest % 2))

    @pl.when(jnp.logical_not(safe))
    def _():
        if has_state:
            marked = jnp.max(marks_ref[...]) > 0.0
            rows = state_ref[...]
            row = lax.broadcasted_iota(jnp.int32, rows.shape, 0)
            acc_ref[...] = jnp.where(marked & (row >= size), 1.0, rows)
            top_ref[...] = jnp.where(marked, rows[size : size + 8], 0.0)
        else:
            top_ref[...] = jnp.full(top_ref.shape, LOW)
        step = 2 * half
        row = lax.broadcasted_iota(jnp.int32, (block, step), 0)
        token = jnp.where(row < half, 2 * row, 2 * (row - half) + 1)
        for at_source, (key_ref, count, number) in enumerate(zip(key_refs, counts, blocks)):

            def one(index, carry, at_source=at_source, key_ref=key_ref, count=count):
                start = pl.multiple_of(index * half, half)
                keys = unpacked([key_ref[pl.ds(start, half), :]])
                cols = pl.ds(pl.multiple_of(at_source * pairs + start, half), half)
                values = jnp.concatenate([even_ref[:, cols], odd_ref[:, cols]], axis=1)

                def part(i, carry):
                    at = pl.ds(pl.multiple_of(i * step, step), step)
                    scores = jnp.where(token < count - index * block, matmul(keys, q2_ref[:, at]) * scale, LOW)
                    before = top_ref[:, at]
                    top = jnp.maximum(before, jnp.max(scores, axis=0, keepdims=True))
                    weights = jnp.exp2(scores - top[:1]).astype(jnp.bfloat16)
                    acc_ref[:, at] = acc_ref[:, at] * jnp.exp2(before - top)[:1] + matmul(values, weights)
                    top_ref[:, at] = top
                    return carry

                return lax.fori_loop(0, tokens // step, part, carry)

            lax.fori_loop(0, number, one, 0)

        if not final:
            rows = acc_ref[...]
            sums = rows[size : size + 1]
            row = lax.broadcasted_iota(jnp.int32, rows.shape, 0)
            acc_ref[...] = jnp.where(row < size, rows / sums, top_ref[:1, :] + jnp.log2(sums))

    if not final:
        mark_ref[...] = jnp.broadcast_to(jnp.where(safe, 0.0, 1.0), mark_ref.shape)
        return
    rows = acc_ref[...]
    if has_state:
        rows = rows + state_ref[...] * jnp.where(safe, 1.0, 0.0)
    result = (rows[:size] * (1.0 / rows[size : size + 1])).astype(out_ref.dtype)
    result = jnp.transpose(jnp.concatenate([result[:, :pairs], result[:, pairs:]], axis=0))
    out_ref[...] = result.reshape(out_ref.shape)


def attend(meta, queries, within, first_head, heads, sources, state, dests, out, name):
    pairs = queries.shape[1] // 2
    head_size = LANES // 2
    scale = math.log2(math.e) / math.sqrt(head_size)
    half = min(128, pairs)
    width = min(WIDTH, 2 * pairs)
    depth = head_size + 16

    def spec(lead, part, start):
        if lead is None:
            return pl.BlockSpec((None, pairs, LANES), lambda h, m: (h + start, part, 0))
        return pl.BlockSpec((None, None, pairs, LANES), lambda h, m: (lead, h + start, part, 0))

    in_specs, arrays = [spec(None, within, first_head)], [queries]
    for part in (1, 2):
        for source in sources:
            array, lead, part_of, start = source[part]
            in_specs.append(spec(lead, part_of, start))
            arrays.append(array)
    shapes = [(depth, 2 * pairs), (8, LANES)]
    if state is not None:
        sums, marks, start = state
        in_specs += [pl.BlockSpec((None, *shape), lambda h, m: (h + start, 0, 0)) for shape in shapes]
        arrays += [sums, marks]
    aliases = {}
    if dests is None:
        out_shape = [jax.ShapeDtypeStruct((heads, *shape), jnp.float32) for shape in shapes]
        out_spec = [pl.BlockSpec((None, *shape), lambda h, m: (h, 0, 0)) for shape in shapes]
    else:
        out_shape = jax.ShapeDtypeStruct((2 * dests, heads, pairs // dests, LANES), jnp.bfloat16)
        out_spec = pl.BlockSpec((dests, 1, pairs // dests, LANES), lambda h, m: (within, h, 0, 0))
        if out is not None:
            in_specs.append(pl.BlockSpec(memory_space=pl.ANY))
            aliases = {1 + len(arrays): 0}
            arrays.append(out)
    unpacked = len(sources) * pairs
    work = heads * len(sources) * (2 * pairs) ** 2
    return pl.pallas_call(
        functools.partial(
            attend_kernel,
            tuple(source[0] for source in sources),
            scale,
            half,
            width,
            state is not None,
            dests is not None,
        ),
        out_shape=out_shape,
        grid_spec=pltpu.PrefetchScalarGridSpec(
            num_scalar_prefetch=1,
            grid=(heads,),
            in_specs=in_specs,
            out_specs=out_spec,
            scratch_shapes=[
                pltpu.VMEM((head_size, 2 * pairs), jnp.bfloat16),
                pltpu.VMEM((depth, unpacked), jnp.bfloat16),
                pltpu.VMEM((depth, unpacked), jnp.bfloat16),
                pltpu.VMEM((depth, 2 * pairs), jnp.float32),
                pltpu.VMEM((8, 2 * pairs), jnp.float32),
            ],
        ),
        input_output_aliases=aliases,
        compiler_params=pltpu.CompilerParams(vmem_limit_bytes=VMEM),
        cost_estimate=pl.CostEstimate(
            flops=work * head_size * (16 if dests is None else 4), bytes_accessed=8 * heads * pairs * LANES * 2, transcendentals=work
        ),
        name=name,
    )(meta, *arrays)


def project_kernel(rows, weight_ref, part_ref, *refs):
    out_ref = refs[-1]
    lane = lax.broadcasted_iota(jnp.int32, (rows, LANES), 1) < LANES // 2
    heads = [part_ref[s, k].astype(jnp.float32) for s in range(part_ref.shape[0]) for k in range(part_ref.shape[1])]
    even, odd = [], []
    for a, b in zip(heads[::2], heads[1::2]):
        even.append(jnp.where(lane, a, swapped(b)).astype(jnp.bfloat16))
        odd.append(jnp.where(lane, swapped(a), b).astype(jnp.bfloat16))
    stacked = jnp.concatenate([jnp.concatenate(even, axis=1), jnp.concatenate(odd, axis=1)], axis=0)
    token = lax.broadcasted_iota(jnp.int32, (2 * rows, 2 * rows), 0)
    place = lax.broadcasted_iota(jnp.int32, (2 * rows, 2 * rows), 1)
    order = (place == token // 2 + (token % 2) * rows).astype(jnp.bfloat16)
    tokens = matmul(order, stacked).astype(jnp.bfloat16)
    weight = weight_ref[...]
    result = matmul(tokens, weight.reshape(-1, weight.shape[-1]))
    if len(refs) > 1:
        result = result + refs[0][...].astype(jnp.float32)
    out_ref[...] = result.astype(out_ref.dtype)


def project(part, group, weight, before):
    pairs = part.shape[2]
    rows = LANES if pairs % LANES == 0 else pairs
    columns = weight.shape[3]
    out = pl.BlockSpec((2 * rows, columns), lambda i: (i, 0))
    return pl.pallas_call(
        functools.partial(project_kernel, rows),
        out_shape=jax.ShapeDtypeStruct((2 * pairs, columns), jnp.bfloat16),
        grid=(pairs // rows,),
        in_specs=[
            pl.BlockSpec((weight.shape[0], None, *weight.shape[2:]), lambda i: (0, group, 0, 0)),
            pl.BlockSpec((*part.shape[:2], rows, LANES), lambda i: (0, 0, i, 0)),
        ]
        + [out] * (before is not None),
        out_specs=out,
        compiler_params=pltpu.CompilerParams(vmem_limit_bytes=WHOLE),
        cost_estimate=pl.CostEstimate(
            flops=4 * pairs * weight.size // weight.shape[1], bytes_accessed=8 * 2**20, transcendentals=0
        ),
        name="project",
    )(weight, part, *([] if before is None else [before]))


def shifted(x, pairs):
    return lax.ppermute(x, "frame", pairs)


def shards(query_proj, key_proj, value_proj, lengths, out_weight):
    devices = lax.axis_size("frame")
    groups = lax.axis_size("head")
    index = lax.axis_index("frame")
    heads, rows, _ = query_proj.shape
    half = rows // 2
    frames = lengths.shape[0]
    weight = lax.all_gather(out_weight, "head", axis=0, tiled=True)

    wanted = jnp.stack([2 * index + within - stride for within in range(2) for stride in STRIDES])
    table = jnp.arange(frames, dtype=jnp.int32)
    meta = jnp.sum(jnp.where(wanted[:, None] == table[None, :], lengths[None, :], 0), axis=1, dtype=jnp.int32)
    meta = jnp.minimum(meta, rows)

    size = heads // 2 if heads % 2 == 0 else heads
    starts = range(0, heads, size)
    by_two = [(i, i + 2) for i in range(devices - 2)]
    cuts = [slice(start, start + size) for start in starts]
    lasts = [jnp.stack((key_proj[cut, half:], value_proj[cut, half:])) for cut in cuts]
    near_lasts = [shifted(last, by_two) for last in lasts]
    far = None
    if devices > 8:
        both = jnp.stack((key_proj, value_proj))
        far = shifted(both, [(i, i + 8) for i in range(devices - 8)])

    def own(slot, part, start):
        return slot, (key_proj, None, part, start), (value_proj, None, part, start)

    def moved(slot, array, part, start):
        return slot, (array, 0, part, start), (array, 1, part, start)

    state_last = {}
    held_keys, held_values = key_proj, value_proj
    for start in starts[:-1]:
        sources = [own(4, 1, start), own(5, 0, start)]
        sums, marks = attend(meta, query_proj, 1, start, size, sources, None, None, None, "last_own")
        state_last[start] = (sums, marks, 0)
        held_keys, held_values, sums = lax.optimization_barrier((held_keys, held_values, sums))
        near_lasts[0], sums = lax.optimization_barrier((near_lasts[0], sums))
        state_last[start] = (sums, marks, 0)
    firsts = [jnp.stack((held_keys[cut, :half], held_values[cut, :half])) for cut in cuts]
    near_lasts[0], firsts[0] = lax.optimization_barrier((near_lasts[0], firsts[0]))
    near_lasts[0], held = lax.optimization_barrier((near_lasts[0], query_proj))
    sums_first, marks_first = attend(meta, held, 0, 0, heads, [own(0, 0, 0)], None, None, None, "first_own")
    if len(starts) > 1:
        near_lasts[1], sums_first, *firsts[1:] = lax.optimization_barrier((near_lasts[1], sums_first, *firsts[1:]))
    near_firsts = [shifted(first, by_two) for first in firsts]
    to_even = [(i + 1, i) for i in range(2, devices - 1, 2)]
    to_odd = [(i, i + 1) for i in range(0, devices - 1, 2)]
    prevs = [
        shifted(jnp.where(index % 2 == 0, last, near), to_even + to_odd) for last, near in zip(lasts, near_lasts)
    ]
    dests = groups // 2
    outs = []
    for number, start in enumerate(starts):
        sources = [moved(6, near_lasts[number], 0, 0)]
        if far is not None:
            sources.append(moved(7, far, 1, start))
        state = state_last.get(start)
        if state is None:
            sources += [own(4, 1, start), own(5, 0, start)]
        outs.append(attend(meta, query_proj, 1, start, size, sources, state, dests, None, "last_rest"))
    weight, *outs = lax.optimization_barrier((weight, *outs))
    weight = weight.reshape(groups, len(starts), size * LANES // 2, weight.shape[1])
    result = None
    for number, start in enumerate(starts):
        sources = [moved(1, prevs[number], 0, 0), moved(2, near_firsts[number], 0, 0)]
        if far is not None:
            sources.append(moved(3, far, 0, start))
        state = (sums_first, marks_first, start)
        out = attend(meta, query_proj, 0, start, size, sources, state, dests, outs[number], "first_rest")
        got = lax.all_to_all(out, "head", split_axis=0, concat_axis=0, tiled=True)
        result = project(got, number, weight, result)
    return result


def solution(mesh):
    return jax.shard_map(
        shards,
        mesh=mesh,
        in_specs=(
            P("head", "frame", None),
            P("head", "frame", None),
            P("head", "frame", None),
            P(),
            P("head", None),
        ),
        out_specs=P(("frame", "head"), None),
        check_vma=False,
    )
```

```python
import functools
import math

import jax
import jax.numpy as jnp
from jax import lax
from jax.experimental import pallas as pl
from jax.experimental.pallas import tpu as pltpu
from jax.sharding import PartitionSpec as P

LANES = 128
STRIDES = (0, 1, 4, 16)
VMEM = 20 * 1024 * 1024
WHOLE = 63 * 1024 * 1024
LOW = -1e30
WIDTH = 256


def swapped(x):
    return pltpu.roll(x, LANES // 2, 1)


def unpacked(blocks):
    return jnp.concatenate(blocks + [swapped(block) for block in blocks], axis=0)[:, : LANES // 2]


def matmul(a, b):
    return jnp.dot(a, b, preferred_element_type=jnp.float32)


def attend_kernel(slots, scale, half, width, has_state, first_head, final, meta_ref, q_ref, *refs):
    refs = list(refs)
    key_refs = [refs.pop(0) for _ in slots]
    value_refs = [refs.pop(0) for _ in slots]
    if has_state:
        sums_ref, marks_ref = refs.pop(0), refs.pop(0)
        sem, state_ref = refs.pop(), refs.pop()
    if final:
        if len(refs) > 6:
            refs.pop(0)
        out_ref = refs.pop(0)
    else:
        out_ref, mark_ref = refs.pop(0), refs.pop(0)
    q2_ref, even_ref, odd_ref, acc_ref, top_ref = refs
    if not final:
        acc_ref = out_ref
    pairs = q_ref.shape[0]
    size = LANES // 2
    depth = acc_ref.shape[0]
    tokens = 2 * pairs
    block = 2 * half
    if has_state:
        def state_copy():
            return pltpu.make_async_copy(sums_ref.at[first_head + pl.program_id(0)], state_ref, sem)

        state_copy().start()
    counts = [meta_ref[slot] for slot in slots]
    blocks = [(count + block - 1) // block for count in counts]
    total = sum(blocks)

    turned = jnp.transpose(q_ref[...])
    q2_ref[:, :pairs] = turned[:size]
    q2_ref[:, pairs:] = turned[size:]
    acc_ref[...] = jnp.zeros(acc_ref.shape, acc_ref.dtype)

    largest = None
    for key_ref in key_refs:
        top = jnp.max(jnp.abs(key_ref[...]), axis=0, keepdims=True).astype(jnp.float32)
        largest = top if largest is None else jnp.maximum(largest, top)
    largest = jnp.broadcast_to(largest, (8, LANES))
    largest = jnp.maximum(largest, swapped(largest))
    key_square = jnp.sum(largest * largest, axis=1, keepdims=True) * 0.5
    square = turned.astype(jnp.float32)
    square = square * square
    longest = jnp.maximum(
        jnp.sum(square[:size], axis=0, keepdims=True), jnp.sum(square[size:], axis=0, keepdims=True)
    )
    product = jnp.max(longest, axis=1, keepdims=True) * key_square[:1]
    if has_state:
        product = jnp.where(marks_ref[:1, :1] > 0.0, 1e30, product)
    safe = jnp.max(product) * (1.01 * scale * scale) < 1e4

    token = 2 * lax.broadcasted_iota(jnp.int32, (8, pairs), 1)
    for at, (value_ref, count) in enumerate(zip(value_refs, counts)):
        turned = jnp.transpose(value_ref[...])
        cols = slice(at * pairs, (at + 1) * pairs)
        for ref, part, later in ((even_ref, turned[:size], 0), (odd_ref, turned[size:], 1)):
            valid = (token + later < count).astype(jnp.float32)[:1].astype(ref.dtype)
            ref[:size, cols] = part * valid
            ref[size:, cols] = jnp.broadcast_to(valid, (depth - size, pairs))

    def place_of(index):
        which, start, rest = 0, 0, index
        for at, number in enumerate(blocks):
            here = (rest >= 0) & (rest < number)
            which = jnp.where(here, at, which)
            start = jnp.where(here, rest * half, start)
            rest = rest - number
        return which, pl.multiple_of(start, half)

    def keys_of(index):
        which, start = place_of(index)
        rows = pl.ds(start, half)
        keys = key_refs[0][rows, :]
        for at in range(1, len(slots)):
            keys = jnp.where(which == at, key_refs[at][rows, :], keys)
        return keys

    def values_at(first, number):
        cols = []
        for i in range(number):
            which, start = place_of(first + i)
            cols.append(pl.ds(pl.multiple_of(which * pairs + start, half), half))
        return jnp.concatenate([ref[:, at] for ref in (even_ref, odd_ref) for at in cols], axis=1)

    def tiles(parts):
        steps = []
        for first, number in parts:
            keys = unpacked([keys_of(first + i) for i in range(number)])
            values = values_at(first, number)
            steps += [(keys, values, at) for at in range(0, tokens, width)]

        def scores_at(step):
            keys, _, at = step
            return matmul(keys, q2_ref[:, at : at + width])

        scores = scores_at(steps[0])
        for step, after in zip(steps, steps[1:] + [None]):
            _, values, at = step
            later = scores_at(after) if after is not None else None
            acc_ref[:, at : at + width] += matmul(values, jnp.exp2(scores * scale).astype(jnp.bfloat16))
            scores = later

    @pl.when(safe)
    def _():
        def whole(index, carry):
            tiles([(index * 4, 2), (index * 4 + 2, 2)])
            return carry

        lax.fori_loop(0, total // 4, whole, 0)

        first = total // 4 * 4
        for rest in (1, 2, 3):

            @pl.when(total % 4 == rest)
            def _(rest=rest):
                tiles([(first, 2)] * (rest > 1) + [(total - 1, 1)] * (rest % 2))

    if has_state:
        state_copy().wait()

    @pl.when(jnp.logical_not(safe))
    def _():
        if has_state:
            marked = jnp.max(marks_ref[...]) > 0.0
            rows = state_ref[...]
            row = lax.broadcasted_iota(jnp.int32, rows.shape, 0)
            acc_ref[...] = jnp.where(marked & (row >= size), 1.0, rows)
            top_ref[...] = jnp.where(marked, rows[size : size + 8], 0.0)
        else:
            top_ref[...] = jnp.full(top_ref.shape, LOW)
        step = 2 * half
        row = lax.broadcasted_iota(jnp.int32, (block, step), 0)
        token = jnp.where(row < half, 2 * row, 2 * (row - half) + 1)
        for at_source, (key_ref, count, number) in enumerate(zip(key_refs, counts, blocks)):

            def one(index, carry, at_source=at_source, key_ref=key_ref, count=count):
                start = pl.multiple_of(index * half, half)
                keys = unpacked([key_ref[pl.ds(start, half), :]])
                cols = pl.ds(pl.multiple_of(at_source * pairs + start, half), half)
                values = jnp.concatenate([even_ref[:, cols], odd_ref[:, cols]], axis=1)

                def part(i, carry):
                    at = pl.ds(pl.multiple_of(i * step, step), step)
                    scores = jnp.where(token < count - index * block, matmul(keys, q2_ref[:, at]) * scale, LOW)
                    before = top_ref[:, at]
                    top = jnp.maximum(before, jnp.max(scores, axis=0, keepdims=True))
                    weights = jnp.exp2(scores - top[:1]).astype(jnp.bfloat16)
                    acc_ref[:, at] = acc_ref[:, at] * jnp.exp2(before - top)[:1] + matmul(values, weights)
                    top_ref[:, at] = top
                    return carry

                return lax.fori_loop(0, tokens // step, part, carry)

            lax.fori_loop(0, number, one, 0)

        if not final:
            rows = acc_ref[...]
            sums = rows[size : size + 1]
            row = lax.broadcasted_iota(jnp.int32, rows.shape, 0)
            acc_ref[...] = jnp.where(row < size, rows / sums, top_ref[:1, :] + jnp.log2(sums))

    if not final:
        mark_ref[...] = jnp.broadcast_to(jnp.where(safe, 0.0, 1.0), mark_ref.shape)
        return
    rows = acc_ref[...]
    if has_state:
        rows = rows + state_ref[...] * jnp.where(safe, 1.0, 0.0)
    result = (rows[:size] * (1.0 / rows[size : size + 1])).astype(out_ref.dtype)
    result = jnp.transpose(jnp.concatenate([result[:, :pairs], result[:, pairs:]], axis=0))
    out_ref[...] = result.reshape(out_ref.shape)


def attend(meta, queries, within, first_head, heads, sources, state, dests, out, name):
    pairs = queries.shape[1] // 2
    head_size = LANES // 2
    scale = math.log2(math.e) / math.sqrt(head_size)
    half = min(128, pairs)
    width = min(WIDTH, 2 * pairs)
    depth = head_size + 16

    def spec(lead, part, start):
        if lead is None:
            return pl.BlockSpec((None, pairs, LANES), lambda h, m: (h + start, part, 0))
        return pl.BlockSpec((None, None, pairs, LANES), lambda h, m: (lead, h + start, part, 0))

    in_specs, arrays = [spec(None, within, first_head)], [queries]
    for part in (1, 2):
        for source in sources:
            array, lead, part_of, start = source[part]
            in_specs.append(spec(lead, part_of, start))
            arrays.append(array)
    shapes = [(depth, 2 * pairs), (8, LANES)]
    if state is not None:
        sums, marks, start = state
        in_specs.append(pl.BlockSpec(memory_space=pltpu.HBM))
        in_specs.append(pl.BlockSpec((None, *shapes[1]), lambda h, m: (h + start, 0, 0)))
        arrays += [sums, marks]
    aliases = {}
    if dests is None:
        out_shape = [jax.ShapeDtypeStruct((heads, *shape), jnp.float32) for shape in shapes]
        out_spec = [pl.BlockSpec((None, *shape), lambda h, m: (h, 0, 0)) for shape in shapes]
    else:
        out_shape = jax.ShapeDtypeStruct((2 * dests, heads, pairs // dests, LANES), jnp.bfloat16)
        out_spec = pl.BlockSpec((dests, 1, pairs // dests, LANES), lambda h, m: (within, h, 0, 0))
        if out is not None:
            in_specs.append(pl.BlockSpec(memory_space=pl.ANY))
            aliases = {1 + len(arrays): 0}
            arrays.append(out)
    unpacked = len(sources) * pairs
    work = heads * len(sources) * (2 * pairs) ** 2
    return pl.pallas_call(
        functools.partial(
            attend_kernel,
            tuple(source[0] for source in sources),
            scale,
            half,
            width,
            state is not None,
            None if state is None else state[2],
            dests is not None,
        ),
        out_shape=out_shape,
        grid_spec=pltpu.PrefetchScalarGridSpec(
            num_scalar_prefetch=1,
            grid=(heads,),
            in_specs=in_specs,
            out_specs=out_spec,
            scratch_shapes=[
                pltpu.VMEM((head_size, 2 * pairs), jnp.bfloat16),
                pltpu.VMEM((depth, unpacked), jnp.bfloat16),
                pltpu.VMEM((depth, unpacked), jnp.bfloat16),
                pltpu.VMEM((depth, 2 * pairs), jnp.float32),
                pltpu.VMEM((8, 2 * pairs), jnp.float32),
            ]
            + [pltpu.VMEM(shapes[0], jnp.float32), pltpu.SemaphoreType.DMA] * (state is not None),
        ),
        input_output_aliases=aliases,
        compiler_params=pltpu.CompilerParams(vmem_limit_bytes=VMEM),
        cost_estimate=pl.CostEstimate(
            flops=work * head_size * (16 if dests is None else 4), bytes_accessed=8 * heads * pairs * LANES * 2, transcendentals=work
        ),
        name=name,
    )(meta, *arrays)


def project_kernel(rows, weight_ref, part_ref, *refs):
    out_ref = refs[-1]
    lane = lax.broadcasted_iota(jnp.int32, (rows, LANES), 1) < LANES // 2
    heads = [part_ref[s, k].astype(jnp.float32) for s in range(part_ref.shape[0]) for k in range(part_ref.shape[1])]
    even, odd = [], []
    for a, b in zip(heads[::2], heads[1::2]):
        even.append(jnp.where(lane, a, swapped(b)).astype(jnp.bfloat16))
        odd.append(jnp.where(lane, swapped(a), b).astype(jnp.bfloat16))
    stacked = jnp.concatenate([jnp.concatenate(even, axis=1), jnp.concatenate(odd, axis=1)], axis=0)
    token = lax.broadcasted_iota(jnp.int32, (2 * rows, 2 * rows), 0)
    place = lax.broadcasted_iota(jnp.int32, (2 * rows, 2 * rows), 1)
    order = (place == token // 2 + (token % 2) * rows).astype(jnp.bfloat16)
    tokens = matmul(order, stacked).astype(jnp.bfloat16)
    weight = weight_ref[...]
    result = matmul(tokens, weight.reshape(-1, weight.shape[-1]))
    if len(refs) > 1:
        result = result + refs[0][...].astype(jnp.float32)
    out_ref[...] = result.astype(out_ref.dtype)


def project(part, group, weight, before):
    pairs = part.shape[2]
    rows = LANES if pairs % LANES == 0 else pairs
    columns = weight.shape[3]
    out = pl.BlockSpec((2 * rows, columns), lambda i: (i, 0))
    return pl.pallas_call(
        functools.partial(project_kernel, rows),
        out_shape=jax.ShapeDtypeStruct((2 * pairs, columns), jnp.bfloat16),
        grid=(pairs // rows,),
        in_specs=[
            pl.BlockSpec((weight.shape[0], None, *weight.shape[2:]), lambda i: (0, group, 0, 0)),
            pl.BlockSpec((*part.shape[:2], rows, LANES), lambda i: (0, 0, i, 0)),
        ]
        + [out] * (before is not None),
        out_specs=out,
        compiler_params=pltpu.CompilerParams(vmem_limit_bytes=WHOLE),
        cost_estimate=pl.CostEstimate(
            flops=4 * pairs * weight.size // weight.shape[1], bytes_accessed=8 * 2**20, transcendentals=0
        ),
        name="project",
    )(weight, part, *([] if before is None else [before]))


def shifted(x, pairs):
    return lax.ppermute(x, "frame", pairs)


def shards(query_proj, key_proj, value_proj, lengths, out_weight):
    devices = lax.axis_size("frame")
    groups = lax.axis_size("head")
    index = lax.axis_index("frame")
    heads, rows, _ = query_proj.shape
    half = rows // 2
    frames = lengths.shape[0]
    weight = lax.all_gather(out_weight, "head", axis=0, tiled=True)

    wanted = jnp.stack([2 * index + within - stride for within in range(2) for stride in STRIDES])
    table = jnp.arange(frames, dtype=jnp.int32)
    meta = jnp.sum(jnp.where(wanted[:, None] == table[None, :], lengths[None, :], 0), axis=1, dtype=jnp.int32)
    meta = jnp.minimum(meta, rows)

    size = heads // 2 if heads % 2 == 0 else heads
    starts = range(0, heads, size)
    by_two = [(i, i + 2) for i in range(devices - 2)]
    first = jnp.stack((key_proj[:, :half], value_proj[:, :half]))
    lasts = [
        jnp.stack((key_proj[start : start + size, half:], value_proj[start : start + size, half:]))
        for start in starts
    ]
    near_lasts = [shifted(last, by_two) for last in lasts]
    near_first = shifted(first, by_two)
    far = None
    if devices > 8:
        both = jnp.stack((key_proj, value_proj))
        far = shifted(both, [(i, i + 8) for i in range(devices - 8)])

    def own(slot, part, start):
        return slot, (key_proj, None, part, start), (value_proj, None, part, start)

    def moved(slot, array, part, start):
        return slot, (array, 0, part, start), (array, 1, part, start)

    state_last = {}
    for start in starts[:-1]:
        sources = [own(4, 1, start), own(5, 0, start)]
        sums, marks = attend(meta, query_proj, 1, start, size, sources, None, None, None, "last_own")
        state_last[start] = (sums, marks, 0)
        near_lasts[0], sums = lax.optimization_barrier((near_lasts[0], sums))
        state_last[start] = (sums, marks, 0)
    near_lasts[0], held = lax.optimization_barrier((near_lasts[0], query_proj))
    sums_first, marks_first = attend(meta, held, 0, 0, heads, [own(0, 0, 0)], None, None, None, "first_own")
    if len(starts) > 1:
        near_lasts[1], sums_first = lax.optimization_barrier((near_lasts[1], sums_first))
    to_even = [(i + 1, i) for i in range(2, devices - 1, 2)]
    to_odd = [(i, i + 1) for i in range(0, devices - 1, 2)]
    prevs = [
        shifted(jnp.where(index % 2 == 0, last, near), to_even + to_odd) for last, near in zip(lasts, near_lasts)
    ]
    dests = groups // 2
    outs = []
    for number, start in enumerate(starts):
        sources = [moved(6, near_lasts[number], 0, 0)]
        if far is not None:
            sources.append(moved(7, far, 1, start))
        state = state_last.get(start)
        if state is None:
            sources += [own(4, 1, start), own(5, 0, start)]
        outs.append(attend(meta, query_proj, 1, start, size, sources, state, dests, None, "last_rest"))
    weight, *outs = lax.optimization_barrier((weight, *outs))
    weight = weight.reshape(groups, len(starts), size * LANES // 2, weight.shape[1])
    result = None
    for number, start in enumerate(starts):
        sources = [moved(1, prevs[number], 0, 0), moved(2, near_first, 0, start)]
        if far is not None:
            sources.append(moved(3, far, 0, start))
        state = (sums_first, marks_first, start)
        out = attend(meta, query_proj, 0, start, size, sources, state, dests, outs[number], "first_rest")
        got = lax.all_to_all(out, "head", split_axis=0, concat_axis=0, tiled=True)
        result = project(got, number, weight, result)
    return result


def solution(mesh):
    return jax.shard_map(
        shards,
        mesh=mesh,
        in_specs=(
            P("head", "frame", None),
            P("head", "frame", None),
            P("head", "frame", None),
            P(),
            P("head", None),
        ),
        out_specs=P(("frame", "head"), None),
        check_vma=False,
    )
```

```python
import functools
import math

import jax
import jax.numpy as jnp
from jax import lax
from jax.experimental import pallas as pl
from jax.experimental.pallas import tpu as pltpu
from jax.sharding import PartitionSpec as P

LANES = 128
STRIDES = (0, 1, 4, 16)
VMEM = 20 * 1024 * 1024
MOST = 62 * 1024 * 1024
WHOLE = 63 * 1024 * 1024
LOW = -1e30
WIDTH = 256


def swapped(x):
    return pltpu.roll(x, LANES // 2, 1)


def unpacked(blocks):
    return jnp.concatenate(blocks + [swapped(block) for block in blocks], axis=0)[:, : LANES // 2]


def matmul(a, b):
    return jnp.dot(a, b, preferred_element_type=jnp.float32)


def attend_kernel(slots, scale, half, width, has_state, first_head, final, meta_ref, q_ref, *refs):
    refs = list(refs)
    key_refs = [refs.pop(0) for _ in slots]
    value_refs = [refs.pop(0) for _ in slots]
    if has_state:
        sums_ref, marks_ref = refs.pop(0), refs.pop(0)
        sem, state_ref = refs.pop(), refs.pop()
    if final:
        if len(refs) > 6:
            refs.pop(0)
        out_ref = refs.pop(0)
    else:
        out_ref, mark_ref = refs.pop(0), refs.pop(0)
    q2_ref, even_ref, odd_ref, acc_ref, top_ref = refs
    if not final:
        acc_ref = out_ref
    pairs = q_ref.shape[0]
    size = LANES // 2
    depth = acc_ref.shape[0]
    tokens = 2 * pairs
    block = 2 * half
    if has_state:
        def state_copy():
            return pltpu.make_async_copy(sums_ref.at[first_head + pl.program_id(0)], state_ref, sem)

        state_copy().start()
    counts = [meta_ref[slot] for slot in slots]
    blocks = [(count + block - 1) // block for count in counts]
    total = sum(blocks)

    turned = jnp.transpose(q_ref[...])
    q2_ref[:, :pairs] = turned[:size]
    q2_ref[:, pairs:] = turned[size:]
    acc_ref[...] = jnp.zeros(acc_ref.shape, acc_ref.dtype)

    largest = None
    for key_ref in key_refs:
        top = jnp.max(jnp.abs(key_ref[...]), axis=0, keepdims=True).astype(jnp.float32)
        largest = top if largest is None else jnp.maximum(largest, top)
    largest = jnp.broadcast_to(largest, (8, LANES))
    largest = jnp.maximum(largest, swapped(largest))
    key_square = jnp.sum(largest * largest, axis=1, keepdims=True) * 0.5
    square = turned.astype(jnp.float32)
    square = square * square
    longest = jnp.maximum(
        jnp.sum(square[:size], axis=0, keepdims=True), jnp.sum(square[size:], axis=0, keepdims=True)
    )
    product = jnp.max(longest, axis=1, keepdims=True) * key_square[:1]
    if has_state:
        product = jnp.where(marks_ref[:1, :1] > 0.0, 1e30, product)
    safe = jnp.max(product) * (1.01 * scale * scale) < 1e4

    token = 2 * lax.broadcasted_iota(jnp.int32, (8, pairs), 1)
    for at, (value_ref, count) in enumerate(zip(value_refs, counts)):
        turned = jnp.transpose(value_ref[...])
        cols = slice(at * pairs, (at + 1) * pairs)
        for ref, part, later in ((even_ref, turned[:size], 0), (odd_ref, turned[size:], 1)):
            valid = (token + later < count).astype(jnp.float32)[:1].astype(ref.dtype)
            ref[:size, cols] = part * valid
            ref[size:, cols] = jnp.broadcast_to(valid, (depth - size, pairs))

    def place_of(index):
        which, start, rest = 0, 0, index
        for at, number in enumerate(blocks):
            here = (rest >= 0) & (rest < number)
            which = jnp.where(here, at, which)
            start = jnp.where(here, rest * half, start)
            rest = rest - number
        return which, pl.multiple_of(start, half)

    def keys_of(index):
        which, start = place_of(index)
        rows = pl.ds(start, half)
        keys = key_refs[0][rows, :]
        for at in range(1, len(slots)):
            keys = jnp.where(which == at, key_refs[at][rows, :], keys)
        return keys

    def values_at(first, number):
        cols = []
        for i in range(number):
            which, start = place_of(first + i)
            cols.append(pl.ds(pl.multiple_of(which * pairs + start, half), half))
        return jnp.concatenate([ref[:, at] for ref in (even_ref, odd_ref) for at in cols], axis=1)

    def tiles(parts):
        steps = []
        for first, number in parts:
            keys = unpacked([keys_of(first + i) for i in range(number)])
            values = values_at(first, number)
            steps += [(keys, values, at) for at in range(0, tokens, width)]

        def scores_at(step):
            keys, _, at = step
            return matmul(keys, q2_ref[:, at : at + width])

        scores = scores_at(steps[0])
        for step, after in zip(steps, steps[1:] + [None]):
            _, values, at = step
            later = scores_at(after) if after is not None else None
            acc_ref[:, at : at + width] += matmul(values, jnp.exp2(scores * scale).astype(jnp.bfloat16))
            scores = later

    @pl.when(safe)
    def _():
        def whole(index, carry):
            tiles([(index * 4, 2), (index * 4 + 2, 2)])
            return carry

        lax.fori_loop(0, total // 4, whole, 0)

        first = total // 4 * 4
        for rest in (1, 2, 3):

            @pl.when(total % 4 == rest)
            def _(rest=rest):
                tiles([(first, 2)] * (rest > 1) + [(total - 1, 1)] * (rest % 2))

    if has_state:
        state_copy().wait()

    @pl.when(jnp.logical_not(safe))
    def _():
        if has_state:
            marked = jnp.max(marks_ref[...]) > 0.0
            rows = state_ref[...]
            row = lax.broadcasted_iota(jnp.int32, rows.shape, 0)
            acc_ref[...] = jnp.where(marked & (row >= size), 1.0, rows)
            top_ref[...] = jnp.where(marked, rows[size : size + 8], 0.0)
        else:
            top_ref[...] = jnp.full(top_ref.shape, LOW)
        step = 2 * half
        row = lax.broadcasted_iota(jnp.int32, (block, step), 0)
        token = jnp.where(row < half, 2 * row, 2 * (row - half) + 1)
        for at_source, (key_ref, count, number) in enumerate(zip(key_refs, counts, blocks)):

            def one(index, carry, at_source=at_source, key_ref=key_ref, count=count):
                start = pl.multiple_of(index * half, half)
                keys = unpacked([key_ref[pl.ds(start, half), :]])
                cols = pl.ds(pl.multiple_of(at_source * pairs + start, half), half)
                values = jnp.concatenate([even_ref[:, cols], odd_ref[:, cols]], axis=1)

                def part(i, carry):
                    at = pl.ds(pl.multiple_of(i * step, step), step)
                    scores = jnp.where(token < count - index * block, matmul(keys, q2_ref[:, at]) * scale, LOW)
                    before = top_ref[:, at]
                    top = jnp.maximum(before, jnp.max(scores, axis=0, keepdims=True))
                    weights = jnp.exp2(scores - top[:1]).astype(jnp.bfloat16)
                    acc_ref[:, at] = acc_ref[:, at] * jnp.exp2(before - top)[:1] + matmul(values, weights)
                    top_ref[:, at] = top
                    return carry

                return lax.fori_loop(0, tokens // step, part, carry)

            lax.fori_loop(0, number, one, 0)

        if not final:
            rows = acc_ref[...]
            sums = rows[size : size + 1]
            row = lax.broadcasted_iota(jnp.int32, rows.shape, 0)
            acc_ref[...] = jnp.where(row < size, rows / sums, top_ref[:1, :] + jnp.log2(sums))

    if not final:
        mark_ref[...] = jnp.broadcast_to(jnp.where(safe, 0.0, 1.0), mark_ref.shape)
        return
    rows = acc_ref[...]
    if has_state:
        rows = rows + state_ref[...] * jnp.where(safe, 1.0, 0.0)
    result = (rows[:size] * (1.0 / rows[size : size + 1])).astype(out_ref.dtype)
    result = jnp.transpose(jnp.concatenate([result[:, :pairs], result[:, pairs:]], axis=0))
    out_ref[...] = result.reshape(out_ref.shape)


def attend(meta, queries, within, first_head, heads, sources, state, dests, out, name):
    pairs = queries.shape[1] // 2
    head_size = LANES // 2
    scale = math.log2(math.e) / math.sqrt(head_size)
    half = min(128, pairs)
    width = min(WIDTH, 2 * pairs)
    depth = head_size + 16

    def spec(lead, part, start):
        if lead is None:
            return pl.BlockSpec((None, pairs, LANES), lambda h, m: (h + start, part, 0))
        return pl.BlockSpec((None, None, pairs, LANES), lambda h, m: (lead, h + start, part, 0))

    in_specs, arrays = [spec(None, within, first_head)], [queries]
    for part in (1, 2):
        for source in sources:
            array, lead, part_of, start = source[part]
            in_specs.append(spec(lead, part_of, start))
            arrays.append(array)
    shapes = [(depth, 2 * pairs), (8, LANES)]
    if state is not None:
        sums, marks, start = state
        in_specs.append(pl.BlockSpec(memory_space=pltpu.HBM))
        in_specs.append(pl.BlockSpec((None, *shapes[1]), lambda h, m: (h + start, 0, 0)))
        arrays += [sums, marks]
    aliases = {}
    if dests is None:
        out_shape = [jax.ShapeDtypeStruct((heads, *shape), jnp.float32) for shape in shapes]
        out_spec = [pl.BlockSpec((None, *shape), lambda h, m: (h, 0, 0)) for shape in shapes]
    else:
        out_shape = jax.ShapeDtypeStruct((2 * dests, heads, pairs // dests, LANES), jnp.bfloat16)
        out_spec = pl.BlockSpec((dests, 1, pairs // dests, LANES), lambda h, m: (within, h, 0, 0))
        if out is not None:
            in_specs.append(pl.BlockSpec(memory_space=pl.ANY))
            aliases = {1 + len(arrays): 0}
            arrays.append(out)
    unpacked = len(sources) * pairs
    work = heads * len(sources) * (2 * pairs) ** 2
    return pl.pallas_call(
        functools.partial(
            attend_kernel,
            tuple(source[0] for source in sources),
            scale,
            half,
            width,
            state is not None,
            None if state is None else state[2],
            dests is not None,
        ),
        out_shape=out_shape,
        grid_spec=pltpu.PrefetchScalarGridSpec(
            num_scalar_prefetch=1,
            grid=(heads,),
            in_specs=in_specs,
            out_specs=out_spec,
            scratch_shapes=[
                pltpu.VMEM((head_size, 2 * pairs), jnp.bfloat16),
                pltpu.VMEM((depth, unpacked), jnp.bfloat16),
                pltpu.VMEM((depth, unpacked), jnp.bfloat16),
                pltpu.VMEM((depth, 2 * pairs), jnp.float32),
                pltpu.VMEM((8, 2 * pairs), jnp.float32),
            ]
            + [pltpu.VMEM(shapes[0], jnp.float32), pltpu.SemaphoreType.DMA] * (state is not None),
        ),
        input_output_aliases=aliases,
        compiler_params=pltpu.CompilerParams(vmem_limit_bytes=VMEM if out is None else WHOLE),
        cost_estimate=pl.CostEstimate(
            flops=work * head_size * (16 if dests is None else 4), bytes_accessed=8 * heads * pairs * LANES * 2, transcendentals=work
        ),
        name=name,
    )(meta, *arrays)


def project_kernel(rows, weight_ref, part_ref, *refs):
    out_ref = refs[-1]
    lane = lax.broadcasted_iota(jnp.int32, (rows, LANES), 1) < LANES // 2
    heads = [part_ref[s, k].astype(jnp.float32) for s in range(part_ref.shape[0]) for k in range(part_ref.shape[1])]
    even, odd = [], []
    for a, b in zip(heads[::2], heads[1::2]):
        even.append(jnp.where(lane, a, swapped(b)).astype(jnp.bfloat16))
        odd.append(jnp.where(lane, swapped(a), b).astype(jnp.bfloat16))
    stacked = jnp.concatenate([jnp.concatenate(even, axis=1), jnp.concatenate(odd, axis=1)], axis=0)
    token = lax.broadcasted_iota(jnp.int32, (2 * rows, 2 * rows), 0)
    place = lax.broadcasted_iota(jnp.int32, (2 * rows, 2 * rows), 1)
    order = (place == token // 2 + (token % 2) * rows).astype(jnp.bfloat16)
    tokens = matmul(order, stacked).astype(jnp.bfloat16)
    weight = weight_ref[...]
    result = matmul(tokens, weight.reshape(-1, weight.shape[-1]))
    if len(refs) > 1:
        result = result + refs[0][...].astype(jnp.float32)
    out_ref[...] = result.astype(out_ref.dtype)


def project(part, group, weight, before):
    pairs = part.shape[2]
    rows = LANES if pairs % LANES == 0 else pairs
    columns = weight.shape[3]
    out = pl.BlockSpec((2 * rows, columns), lambda i: (i, 0))
    return pl.pallas_call(
        functools.partial(project_kernel, rows),
        out_shape=jax.ShapeDtypeStruct((2 * pairs, columns), jnp.bfloat16),
        grid=(pairs // rows,),
        in_specs=[
            pl.BlockSpec((weight.shape[0], None, *weight.shape[2:]), lambda i: (0, group, 0, 0)),
            pl.BlockSpec((*part.shape[:2], rows, LANES), lambda i: (0, 0, i, 0)),
        ]
        + [out] * (before is not None),
        out_specs=out,
        compiler_params=pltpu.CompilerParams(vmem_limit_bytes=MOST),
        cost_estimate=pl.CostEstimate(
            flops=4 * pairs * weight.size // weight.shape[1], bytes_accessed=8 * 2**20, transcendentals=0
        ),
        name="project",
    )(weight, part, *([] if before is None else [before]))


def shifted(x, pairs):
    return lax.ppermute(x, "frame", pairs)


def shards(query_proj, key_proj, value_proj, lengths, out_weight):
    devices = lax.axis_size("frame")
    groups = lax.axis_size("head")
    index = lax.axis_index("frame")
    heads, rows, _ = query_proj.shape
    half = rows // 2
    frames = lengths.shape[0]
    weight = lax.all_gather(out_weight, "head", axis=0, tiled=True)

    wanted = jnp.stack([2 * index + within - stride for within in range(2) for stride in STRIDES])
    table = jnp.arange(frames, dtype=jnp.int32)
    meta = jnp.sum(jnp.where(wanted[:, None] == table[None, :], lengths[None, :], 0), axis=1, dtype=jnp.int32)
    meta = jnp.minimum(meta, rows)

    size = heads // 2 if heads % 2 == 0 else heads
    starts = range(0, heads, size)
    by_two = [(i, i + 2) for i in range(devices - 2)]
    first = jnp.stack((key_proj[:, :half], value_proj[:, :half]))
    lasts = [
        jnp.stack((key_proj[start : start + size, half:], value_proj[start : start + size, half:]))
        for start in starts
    ]
    near_lasts = [shifted(last, by_two) for last in lasts]
    near_first = shifted(first, by_two)
    far = None
    if devices > 8:
        both = jnp.stack((key_proj, value_proj))
        far = shifted(both, [(i, i + 8) for i in range(devices - 8)])

    def own(slot, part, start):
        return slot, (key_proj, None, part, start), (value_proj, None, part, start)

    def moved(slot, array, part, start):
        return slot, (array, 0, part, start), (array, 1, part, start)

    state_last = {}
    for start in starts[:-1]:
        sources = [own(4, 1, start), own(5, 0, start)]
        sums, marks = attend(meta, query_proj, 1, start, size, sources, None, None, None, "last_own")
        state_last[start] = (sums, marks, 0)
        near_lasts[0], sums = lax.optimization_barrier((near_lasts[0], sums))
        state_last[start] = (sums, marks, 0)
    near_lasts[0], held = lax.optimization_barrier((near_lasts[0], query_proj))
    sums_first, marks_first = attend(meta, held, 0, 0, heads, [own(0, 0, 0)], None, None, None, "first_own")
    if len(starts) > 1:
        near_lasts[1], sums_first = lax.optimization_barrier((near_lasts[1], sums_first))
    to_even = [(i + 1, i) for i in range(2, devices - 1, 2)]
    to_odd = [(i, i + 1) for i in range(0, devices - 1, 2)]
    prevs = [
        shifted(jnp.where(index % 2 == 0, last, near), to_even + to_odd) for last, near in zip(lasts, near_lasts)
    ]
    dests = groups // 2
    outs = []
    for number, start in enumerate(starts):
        sources = [moved(6, near_lasts[number], 0, 0)]
        if far is not None:
            sources.append(moved(7, far, 1, start))
        state = state_last.get(start)
        if state is None:
            sources += [own(4, 1, start), own(5, 0, start)]
        outs.append(attend(meta, query_proj, 1, start, size, sources, state, dests, None, "last_rest"))
    weight, *outs = lax.optimization_barrier((weight, *outs))
    weight = weight.reshape(groups, len(starts), size * LANES // 2, weight.shape[1])
    result = None
    for number, start in enumerate(starts):
        sources = [moved(1, prevs[number], 0, 0), moved(2, near_first, 0, start)]
        if far is not None:
            sources.append(moved(3, far, 0, start))
        state = (sums_first, marks_first, start)
        out = attend(meta, query_proj, 0, start, size, sources, state, dests, outs[number], "first_rest")
        got = lax.all_to_all(out, "head", split_axis=0, concat_axis=0, tiled=True)
        result = project(got, number, weight, result)
    return result


def solution(mesh):
    return jax.shard_map(
        shards,
        mesh=mesh,
        in_specs=(
            P("head", "frame", None),
            P("head", "frame", None),
            P("head", "frame", None),
            P(),
            P("head", None),
        ),
        out_specs=P(("frame", "head"), None),
        check_vma=False,
    )
```

```python
import functools
import math

import jax
import jax.numpy as jnp
from jax import lax
from jax.experimental import pallas as pl
from jax.experimental.pallas import tpu as pltpu
from jax.sharding import PartitionSpec as P

LANES = 128
STRIDES = (0, 1, 4, 16)
VMEM = 20 * 1024 * 1024
MOST = 62 * 1024 * 1024
WHOLE = 63 * 1024 * 1024 + 512 * 1024
LOW = -1e30
WIDTH = 256


def swapped(x):
    return pltpu.roll(x, LANES // 2, 1)


def unpacked(blocks):
    return jnp.concatenate(blocks + [swapped(block) for block in blocks], axis=0)[:, : LANES // 2]


def matmul(a, b):
    return jnp.dot(a, b, preferred_element_type=jnp.float32)


def attend_kernel(slots, scale, half, width, has_state, first_head, final, meta_ref, q_ref, *refs):
    refs = list(refs)
    key_refs = [refs.pop(0) for _ in slots]
    value_refs = [refs.pop(0) for _ in slots]
    if has_state:
        sums_ref, marks_ref = refs.pop(0), refs.pop(0)
        sem, state_ref = refs.pop(), refs.pop()
    if final:
        if len(refs) > 6:
            refs.pop(0)
        out_ref = refs.pop(0)
    else:
        out_ref, mark_ref = refs.pop(0), refs.pop(0)
    q2_ref, even_ref, odd_ref, acc_ref, top_ref = refs
    if not final:
        acc_ref = out_ref
    pairs = q_ref.shape[0]
    size = LANES // 2
    depth = acc_ref.shape[0]
    tokens = 2 * pairs
    block = 2 * half
    if has_state:
        def state_copy():
            return pltpu.make_async_copy(sums_ref.at[first_head + pl.program_id(0)], state_ref, sem)

        state_copy().start()
    counts = [meta_ref[slot] for slot in slots]
    blocks = [(count + block - 1) // block for count in counts]
    total = sum(blocks)

    turned = jnp.transpose(q_ref[...])
    q2_ref[:, :pairs] = turned[:size]
    q2_ref[:, pairs:] = turned[size:]
    acc_ref[...] = jnp.zeros(acc_ref.shape, acc_ref.dtype)

    largest = None
    for key_ref in key_refs:
        top = jnp.max(jnp.abs(key_ref[...]), axis=0, keepdims=True).astype(jnp.float32)
        largest = top if largest is None else jnp.maximum(largest, top)
    largest = jnp.broadcast_to(largest, (8, LANES))
    largest = jnp.maximum(largest, swapped(largest))
    key_square = jnp.sum(largest * largest, axis=1, keepdims=True) * 0.5
    square = turned.astype(jnp.float32)
    square = square * square
    longest = jnp.maximum(
        jnp.sum(square[:size], axis=0, keepdims=True), jnp.sum(square[size:], axis=0, keepdims=True)
    )
    product = jnp.max(longest, axis=1, keepdims=True) * key_square[:1]
    if has_state:
        product = jnp.where(marks_ref[:1, :1] > 0.0, 1e30, product)
    safe = jnp.max(product) * (1.01 * scale * scale) < 1e4

    token = 2 * lax.broadcasted_iota(jnp.int32, (8, pairs), 1)
    for at, (value_ref, count) in enumerate(zip(value_refs, counts)):
        turned = jnp.transpose(value_ref[...])
        cols = slice(at * pairs, (at + 1) * pairs)
        for ref, part, later in ((even_ref, turned[:size], 0), (odd_ref, turned[size:], 1)):
            valid = (token + later < count).astype(jnp.float32)[:1].astype(ref.dtype)
            ref[:size, cols] = part * valid
            ref[size:, cols] = jnp.broadcast_to(valid, (depth - size, pairs))

    def place_of(index):
        which, start, rest = 0, 0, index
        for at, number in enumerate(blocks):
            here = (rest >= 0) & (rest < number)
            which = jnp.where(here, at, which)
            start = jnp.where(here, rest * half, start)
            rest = rest - number
        return which, pl.multiple_of(start, half)

    def keys_of(index):
        which, start = place_of(index)
        rows = pl.ds(start, half)
        keys = key_refs[0][rows, :]
        for at in range(1, len(slots)):
            keys = jnp.where(which == at, key_refs[at][rows, :], keys)
        return keys

    def values_at(first, number):
        cols = []
        for i in range(number):
            which, start = place_of(first + i)
            cols.append(pl.ds(pl.multiple_of(which * pairs + start, half), half))
        return jnp.concatenate([ref[:, at] for ref in (even_ref, odd_ref) for at in cols], axis=1)

    def tiles(parts):
        steps = []
        for first, number in parts:
            keys = unpacked([keys_of(first + i) for i in range(number)])
            values = values_at(first, number)
            steps += [(keys, values, at) for at in range(0, tokens, width)]

        def scores_at(step):
            keys, _, at = step
            return matmul(keys, q2_ref[:, at : at + width])

        scores = scores_at(steps[0])
        for step, after in zip(steps, steps[1:] + [None]):
            _, values, at = step
            later = scores_at(after) if after is not None else None
            acc_ref[:, at : at + width] += matmul(values, jnp.exp2(scores * scale).astype(jnp.bfloat16))
            scores = later

    @pl.when(safe)
    def _():
        def whole(index, carry):
            tiles([(index * 4, 2), (index * 4 + 2, 2)])
            return carry

        lax.fori_loop(0, total // 4, whole, 0)

        first = total // 4 * 4
        for rest in (1, 2, 3):

            @pl.when(total % 4 == rest)
            def _(rest=rest):
                tiles([(first, 2)] * (rest > 1) + [(total - 1, 1)] * (rest % 2))

    if has_state:
        state_copy().wait()

    @pl.when(jnp.logical_not(safe))
    def _():
        if has_state:
            marked = jnp.max(marks_ref[...]) > 0.0
            rows = state_ref[...]
            row = lax.broadcasted_iota(jnp.int32, rows.shape, 0)
            acc_ref[...] = jnp.where(marked & (row >= size), 1.0, rows)
            top_ref[...] = jnp.where(marked, rows[size : size + 8], 0.0)
        else:
            top_ref[...] = jnp.full(top_ref.shape, LOW)
        step = 2 * half
        row = lax.broadcasted_iota(jnp.int32, (block, step), 0)
        token = jnp.where(row < half, 2 * row, 2 * (row - half) + 1)
        for at_source, (key_ref, count, number) in enumerate(zip(key_refs, counts, blocks)):

            def one(index, carry, at_source=at_source, key_ref=key_ref, count=count):
                start = pl.multiple_of(index * half, half)
                keys = unpacked([key_ref[pl.ds(start, half), :]])
                cols = pl.ds(pl.multiple_of(at_source * pairs + start, half), half)
                values = jnp.concatenate([even_ref[:, cols], odd_ref[:, cols]], axis=1)

                def part(i, carry):
                    at = pl.ds(pl.multiple_of(i * step, step), step)
                    scores = jnp.where(token < count - index * block, matmul(keys, q2_ref[:, at]) * scale, LOW)
                    before = top_ref[:, at]
                    top = jnp.maximum(before, jnp.max(scores, axis=0, keepdims=True))
                    weights = jnp.exp2(scores - top[:1]).astype(jnp.bfloat16)
                    acc_ref[:, at] = acc_ref[:, at] * jnp.exp2(before - top)[:1] + matmul(values, weights)
                    top_ref[:, at] = top
                    return carry

                return lax.fori_loop(0, tokens // step, part, carry)

            lax.fori_loop(0, number, one, 0)

        if not final:
            rows = acc_ref[...]
            sums = rows[size : size + 1]
            row = lax.broadcasted_iota(jnp.int32, rows.shape, 0)
            acc_ref[...] = jnp.where(row < size, rows / sums, top_ref[:1, :] + jnp.log2(sums))

    if not final:
        mark_ref[...] = jnp.broadcast_to(jnp.where(safe, 0.0, 1.0), mark_ref.shape)
        return
    rows = acc_ref[...]
    if has_state:
        rows = rows + state_ref[...] * jnp.where(safe, 1.0, 0.0)
    result = (rows[:size] * (1.0 / rows[size : size + 1])).astype(out_ref.dtype)
    result = jnp.transpose(jnp.concatenate([result[:, :pairs], result[:, pairs:]], axis=0))
    out_ref[...] = result.reshape(out_ref.shape)


def attend(meta, queries, within, first_head, heads, sources, state, dests, out, name):
    pairs = queries.shape[1] // 2
    head_size = LANES // 2
    scale = math.log2(math.e) / math.sqrt(head_size)
    half = min(128, pairs)
    width = min(WIDTH, 2 * pairs)
    depth = head_size + 16

    def spec(lead, part, start):
        if lead is None:
            return pl.BlockSpec((None, pairs, LANES), lambda h, m: (h + start, part, 0))
        return pl.BlockSpec((None, None, pairs, LANES), lambda h, m: (lead, h + start, part, 0))

    in_specs, arrays = [spec(None, within, first_head)], [queries]
    for part in (1, 2):
        for source in sources:
            array, lead, part_of, start = source[part]
            in_specs.append(spec(lead, part_of, start))
            arrays.append(array)
    shapes = [(depth, 2 * pairs), (8, LANES)]
    if state is not None:
        sums, marks, start = state
        in_specs.append(pl.BlockSpec(memory_space=pltpu.HBM))
        in_specs.append(pl.BlockSpec((None, *shapes[1]), lambda h, m: (h + start, 0, 0)))
        arrays += [sums, marks]
    aliases = {}
    if dests is None:
        out_shape = [jax.ShapeDtypeStruct((heads, *shape), jnp.float32) for shape in shapes]
        out_spec = [pl.BlockSpec((None, *shape), lambda h, m: (h, 0, 0)) for shape in shapes]
    else:
        out_shape = jax.ShapeDtypeStruct((2 * dests, heads, pairs // dests, LANES), jnp.bfloat16)
        out_spec = pl.BlockSpec((dests, 1, pairs // dests, LANES), lambda h, m: (within, h, 0, 0))
        if out is not None:
            in_specs.append(pl.BlockSpec(memory_space=pl.ANY))
            aliases = {1 + len(arrays): 0}
            arrays.append(out)
    unpacked = len(sources) * pairs
    work = heads * len(sources) * (2 * pairs) ** 2
    return pl.pallas_call(
        functools.partial(
            attend_kernel,
            tuple(source[0] for source in sources),
            scale,
            half,
            width,
            state is not None,
            None if state is None else state[2],
            dests is not None,
        ),
        out_shape=out_shape,
        grid_spec=pltpu.PrefetchScalarGridSpec(
            num_scalar_prefetch=1,
            grid=(heads,),
            in_specs=in_specs,
            out_specs=out_spec,
            scratch_shapes=[
                pltpu.VMEM((head_size, 2 * pairs), jnp.bfloat16),
                pltpu.VMEM((depth, unpacked), jnp.bfloat16),
                pltpu.VMEM((depth, unpacked), jnp.bfloat16),
                pltpu.VMEM((depth, 2 * pairs), jnp.float32),
                pltpu.VMEM((8, 2 * pairs), jnp.float32),
            ]
            + [pltpu.VMEM(shapes[0], jnp.float32), pltpu.SemaphoreType.DMA] * (state is not None),
        ),
        input_output_aliases=aliases,
        compiler_params=pltpu.CompilerParams(vmem_limit_bytes=VMEM if out is None else MOST),
        cost_estimate=pl.CostEstimate(
            flops=work * head_size * (16 if dests is None else 4), bytes_accessed=8 * heads * pairs * LANES * 2, transcendentals=work
        ),
        name=name,
    )(meta, *arrays)


def project_kernel(rows, weight_ref, part_ref, *refs):
    out_ref = refs[-1]
    lane = lax.broadcasted_iota(jnp.int32, (rows, LANES), 1) < LANES // 2
    heads = [part_ref[s, k].astype(jnp.float32) for s in range(part_ref.shape[0]) for k in range(part_ref.shape[1])]
    even, odd = [], []
    for a, b in zip(heads[::2], heads[1::2]):
        even.append(jnp.where(lane, a, swapped(b)).astype(jnp.bfloat16))
        odd.append(jnp.where(lane, swapped(a), b).astype(jnp.bfloat16))
    stacked = jnp.concatenate([jnp.concatenate(even, axis=1), jnp.concatenate(odd, axis=1)], axis=0)
    token = lax.broadcasted_iota(jnp.int32, (2 * rows, 2 * rows), 0)
    place = lax.broadcasted_iota(jnp.int32, (2 * rows, 2 * rows), 1)
    order = (place == token // 2 + (token % 2) * rows).astype(jnp.bfloat16)
    tokens = matmul(order, stacked).astype(jnp.bfloat16)
    weight = weight_ref[...]
    result = matmul(tokens, weight.reshape(-1, weight.shape[-1]))
    if len(refs) > 1:
        result = result + refs[0][...].astype(jnp.float32)
    out_ref[...] = result.astype(out_ref.dtype)


def project(part, group, weight, before):
    pairs = part.shape[2]
    rows = LANES if pairs % LANES == 0 else pairs
    columns = weight.shape[3]
    out = pl.BlockSpec((2 * rows, columns), lambda i: (i, 0))
    return pl.pallas_call(
        functools.partial(project_kernel, rows),
        out_shape=jax.ShapeDtypeStruct((2 * pairs, columns), jnp.bfloat16),
        grid=(pairs // rows,),
        in_specs=[
            pl.BlockSpec((weight.shape[0], None, *weight.shape[2:]), lambda i: (0, group, 0, 0)),
            pl.BlockSpec((*part.shape[:2], rows, LANES), lambda i: (0, 0, i, 0)),
        ]
        + [out] * (before is not None),
        out_specs=out,
        compiler_params=pltpu.CompilerParams(vmem_limit_bytes=WHOLE),
        cost_estimate=pl.CostEstimate(
            flops=4 * pairs * weight.size // weight.shape[1], bytes_accessed=8 * 2**20, transcendentals=0
        ),
        name="project",
    )(weight, part, *([] if before is None else [before]))


def shifted(x, pairs):
    return lax.ppermute(x, "frame", pairs)


def shards(query_proj, key_proj, value_proj, lengths, out_weight):
    devices = lax.axis_size("frame")
    groups = lax.axis_size("head")
    index = lax.axis_index("frame")
    heads, rows, _ = query_proj.shape
    half = rows // 2
    frames = lengths.shape[0]
    weight = lax.all_gather(out_weight, "head", axis=0, tiled=True)

    wanted = jnp.stack([2 * index + within - stride for within in range(2) for stride in STRIDES])
    table = jnp.arange(frames, dtype=jnp.int32)
    meta = jnp.sum(jnp.where(wanted[:, None] == table[None, :], lengths[None, :], 0), axis=1, dtype=jnp.int32)
    meta = jnp.minimum(meta, rows)

    size = heads // 2 if heads % 2 == 0 else heads
    starts = range(0, heads, size)
    by_two = [(i, i + 2) for i in range(devices - 2)]
    first = jnp.stack((key_proj[:, :half], value_proj[:, :half]))
    lasts = [
        jnp.stack((key_proj[start : start + size, half:], value_proj[start : start + size, half:]))
        for start in starts
    ]
    near_lasts = [shifted(last, by_two) for last in lasts]
    near_first = shifted(first, by_two)
    far = None
    if devices > 8:
        both = jnp.stack((key_proj, value_proj))
        far = shifted(both, [(i, i + 8) for i in range(devices - 8)])

    def own(slot, part, start):
        return slot, (key_proj, None, part, start), (value_proj, None, part, start)

    def moved(slot, array, part, start):
        return slot, (array, 0, part, start), (array, 1, part, start)

    state_last = {}
    for start in starts[:-1]:
        sources = [own(4, 1, start), own(5, 0, start)]
        sums, marks = attend(meta, query_proj, 1, start, size, sources, None, None, None, "last_own")
        state_last[start] = (sums, marks, 0)
        near_lasts[0], sums = lax.optimization_barrier((near_lasts[0], sums))
        state_last[start] = (sums, marks, 0)
    near_lasts[0], held = lax.optimization_barrier((near_lasts[0], query_proj))
    sums_first, marks_first = attend(meta, held, 0, 0, heads, [own(0, 0, 0)], None, None, None, "first_own")
    if len(starts) > 1:
        near_lasts[1], sums_first = lax.optimization_barrier((near_lasts[1], sums_first))
    to_even = [(i + 1, i) for i in range(2, devices - 1, 2)]
    to_odd = [(i, i + 1) for i in range(0, devices - 1, 2)]
    prevs = [
        shifted(jnp.where(index % 2 == 0, last, near), to_even + to_odd) for last, near in zip(lasts, near_lasts)
    ]
    dests = groups // 2
    outs = []
    for number, start in enumerate(starts):
        sources = [moved(6, near_lasts[number], 0, 0)]
        if far is not None:
            sources.append(moved(7, far, 1, start))
        state = state_last.get(start)
        if state is None:
            sources += [own(4, 1, start), own(5, 0, start)]
        outs.append(attend(meta, query_proj, 1, start, size, sources, state, dests, None, "last_rest"))
    weight, *outs = lax.optimization_barrier((weight, *outs))
    weight = weight.reshape(groups, len(starts), size * LANES // 2, weight.shape[1])
    result = None
    for number, start in enumerate(starts):
        sources = [moved(1, prevs[number], 0, 0), moved(2, near_first, 0, start)]
        if far is not None:
            sources.append(moved(3, far, 0, start))
        state = (sums_first, marks_first, start)
        out = attend(meta, query_proj, 0, start, size, sources, state, dests, outs[number], "first_rest")
        got = lax.all_to_all(out, "head", split_axis=0, concat_axis=0, tiled=True)
        result = project(got, number, weight, result)
    return result


def solution(mesh):
    return jax.shard_map(
        shards,
        mesh=mesh,
        in_specs=(
            P("head", "frame", None),
            P("head", "frame", None),
            P("head", "frame", None),
            P(),
            P("head", None),
        ),
        out_specs=P(("frame", "head"), None),
        check_vma=False,
    )
```

```python
import functools
import math

import jax
import jax.numpy as jnp
from jax import lax
from jax.experimental import pallas as pl
from jax.experimental.pallas import tpu as pltpu
from jax.sharding import PartitionSpec as P

LANES = 128
STRIDES = (0, 1, 4, 16)
VMEM = 20 * 1024 * 1024
MOST = 62 * 1024 * 1024
WHOLE = 63 * 1024 * 1024 + 512 * 1024
LOW = -1e30
WIDTH = 256


def swapped(x):
    return pltpu.roll(x, LANES // 2, 1)


def unpacked(blocks):
    return jnp.concatenate(blocks + [swapped(block) for block in blocks], axis=0)[:, : LANES // 2]


def matmul(a, b):
    return jnp.dot(a, b, preferred_element_type=jnp.float32)


def attend_kernel(slots, scale, half, width, has_state, first_head, final, meta_ref, q_ref, *refs):
    refs = list(refs)
    key_refs = [refs.pop(0) for _ in slots]
    value_refs = [refs.pop(0) for _ in slots]
    if has_state:
        sums_ref, marks_ref = refs.pop(0), refs.pop(0)
        sem, state_ref = refs.pop(), refs.pop()
    if final:
        if len(refs) > 6:
            refs.pop(0)
        out_ref = refs.pop(0)
    else:
        out_ref, mark_ref = refs.pop(0), refs.pop(0)
    q2_ref, even_ref, odd_ref, acc_ref, top_ref = refs
    if not final:
        acc_ref = out_ref
    pairs = q_ref.shape[0]
    size = LANES // 2
    depth = acc_ref.shape[0]
    tokens = 2 * pairs
    block = 2 * half
    if has_state:
        def state_copy():
            return pltpu.make_async_copy(sums_ref.at[first_head + pl.program_id(0)], state_ref, sem)

        state_copy().start()
    counts = [meta_ref[slot] for slot in slots]
    blocks = [(count + block - 1) // block for count in counts]
    total = sum(blocks)

    turned = jnp.transpose(q_ref[...])
    q2_ref[:, :pairs] = turned[:size]
    q2_ref[:, pairs:] = turned[size:]
    acc_ref[...] = jnp.zeros(acc_ref.shape, acc_ref.dtype)

    largest = None
    for key_ref in key_refs:
        top = jnp.max(jnp.abs(key_ref[...]), axis=0, keepdims=True).astype(jnp.float32)
        largest = top if largest is None else jnp.maximum(largest, top)
    largest = jnp.broadcast_to(largest, (8, LANES))
    largest = jnp.maximum(largest, swapped(largest))
    key_square = jnp.sum(largest * largest, axis=1, keepdims=True) * 0.5
    square = turned.astype(jnp.float32)
    square = square * square
    longest = jnp.maximum(
        jnp.sum(square[:size], axis=0, keepdims=True), jnp.sum(square[size:], axis=0, keepdims=True)
    )
    product = jnp.max(longest, axis=1, keepdims=True) * key_square[:1]
    if has_state:
        product = jnp.where(marks_ref[:1, :1] > 0.0, 1e30, product)
    safe = jnp.max(product) * (1.01 * scale * scale) < 1e4

    token = 2 * lax.broadcasted_iota(jnp.int32, (8, pairs), 1)
    for at, (value_ref, count) in enumerate(zip(value_refs, counts)):
        turned = jnp.transpose(value_ref[...])
        cols = slice(at * pairs, (at + 1) * pairs)
        for ref, part, later in ((even_ref, turned[:size], 0), (odd_ref, turned[size:], 1)):
            valid = (token + later < count).astype(jnp.float32)[:1].astype(ref.dtype)
            ref[:size, cols] = part * valid
            ref[size:, cols] = jnp.broadcast_to(valid, (depth - size, pairs))

    def place_of(index):
        which, start, rest = 0, 0, index
        for at, number in enumerate(blocks):
            here = (rest >= 0) & (rest < number)
            which = jnp.where(here, at, which)
            start = jnp.where(here, rest * half, start)
            rest = rest - number
        return which, pl.multiple_of(start, half)

    def keys_of(index):
        which, start = place_of(index)
        rows = pl.ds(start, half)
        keys = key_refs[0][rows, :]
        for at in range(1, len(slots)):
            keys = jnp.where(which == at, key_refs[at][rows, :], keys)
        return keys

    def values_at(first, number):
        cols = []
        for i in range(number):
            which, start = place_of(first + i)
            cols.append(pl.ds(pl.multiple_of(which * pairs + start, half), half))
        return jnp.concatenate([ref[:, at] for ref in (even_ref, odd_ref) for at in cols], axis=1)

    def tiles(parts):
        steps = []
        for first, number in parts:
            keys = unpacked([keys_of(first + i) for i in range(number)])
            values = values_at(first, number)
            steps += [(keys, values, at) for at in range(0, tokens, width)]

        def scores_at(step):
            keys, _, at = step
            return matmul(keys, q2_ref[:, at : at + width])

        scores = scores_at(steps[0])
        for step, after in zip(steps, steps[1:] + [None]):
            _, values, at = step
            later = scores_at(after) if after is not None else None
            acc_ref[:, at : at + width] += matmul(values, jnp.exp2(scores * scale).astype(jnp.bfloat16))
            scores = later

    @pl.when(safe)
    def _():
        def whole(index, carry):
            tiles([(index * 6 + at, 2) for at in (0, 2, 4)])
            return carry

        lax.fori_loop(0, total // 6, whole, 0)

        first = total // 6 * 6
        for rest in range(1, 6):

            @pl.when(total % 6 == rest)
            def _(rest=rest):
                tiles([(first + at, 2) for at in range(0, rest - 1, 2)] + [(total - 1, 1)] * (rest % 2))

    if has_state:
        state_copy().wait()

    @pl.when(jnp.logical_not(safe))
    def _():
        if has_state:
            marked = jnp.max(marks_ref[...]) > 0.0
            rows = state_ref[...]
            row = lax.broadcasted_iota(jnp.int32, rows.shape, 0)
            acc_ref[...] = jnp.where(marked & (row >= size), 1.0, rows)
            top_ref[...] = jnp.where(marked, rows[size : size + 8], 0.0)
        else:
            top_ref[...] = jnp.full(top_ref.shape, LOW)
        step = 2 * half
        row = lax.broadcasted_iota(jnp.int32, (block, step), 0)
        token = jnp.where(row < half, 2 * row, 2 * (row - half) + 1)
        for at_source, (key_ref, count, number) in enumerate(zip(key_refs, counts, blocks)):

            def one(index, carry, at_source=at_source, key_ref=key_ref, count=count):
                start = pl.multiple_of(index * half, half)
                keys = unpacked([key_ref[pl.ds(start, half), :]])
                cols = pl.ds(pl.multiple_of(at_source * pairs + start, half), half)
                values = jnp.concatenate([even_ref[:, cols], odd_ref[:, cols]], axis=1)

                def part(i, carry):
                    at = pl.ds(pl.multiple_of(i * step, step), step)
                    scores = jnp.where(token < count - index * block, matmul(keys, q2_ref[:, at]) * scale, LOW)
                    before = top_ref[:, at]
                    top = jnp.maximum(before, jnp.max(scores, axis=0, keepdims=True))
                    weights = jnp.exp2(scores - top[:1]).astype(jnp.bfloat16)
                    acc_ref[:, at] = acc_ref[:, at] * jnp.exp2(before - top)[:1] + matmul(values, weights)
                    top_ref[:, at] = top
                    return carry

                return lax.fori_loop(0, tokens // step, part, carry)

            lax.fori_loop(0, number, one, 0)

        if not final:
            rows = acc_ref[...]
            sums = rows[size : size + 1]
            row = lax.broadcasted_iota(jnp.int32, rows.shape, 0)
            acc_ref[...] = jnp.where(row < size, rows / sums, top_ref[:1, :] + jnp.log2(sums))

    if not final:
        mark_ref[...] = jnp.broadcast_to(jnp.where(safe, 0.0, 1.0), mark_ref.shape)
        return
    rows = acc_ref[...]
    if has_state:
        rows = rows + state_ref[...] * jnp.where(safe, 1.0, 0.0)
    result = (rows[:size] * (1.0 / rows[size : size + 1])).astype(out_ref.dtype)
    result = jnp.transpose(jnp.concatenate([result[:, :pairs], result[:, pairs:]], axis=0))
    out_ref[...] = result.reshape(out_ref.shape)


def attend(meta, queries, within, first_head, heads, sources, state, dests, out, name):
    pairs = queries.shape[1] // 2
    head_size = LANES // 2
    scale = math.log2(math.e) / math.sqrt(head_size)
    half = min(128, pairs)
    width = min(WIDTH, 2 * pairs)
    depth = head_size + 16

    def spec(lead, part, start):
        if lead is None:
            return pl.BlockSpec((None, pairs, LANES), lambda h, m: (h + start, part, 0))
        return pl.BlockSpec((None, None, pairs, LANES), lambda h, m: (lead, h + start, part, 0))

    in_specs, arrays = [spec(None, within, first_head)], [queries]
    for part in (1, 2):
        for source in sources:
            array, lead, part_of, start = source[part]
            in_specs.append(spec(lead, part_of, start))
            arrays.append(array)
    shapes = [(depth, 2 * pairs), (8, LANES)]
    if state is not None:
        sums, marks, start = state
        in_specs.append(pl.BlockSpec(memory_space=pltpu.HBM))
        in_specs.append(pl.BlockSpec((None, *shapes[1]), lambda h, m: (h + start, 0, 0)))
        arrays += [sums, marks]
    aliases = {}
    if dests is None:
        out_shape = [jax.ShapeDtypeStruct((heads, *shape), jnp.float32) for shape in shapes]
        out_spec = [pl.BlockSpec((None, *shape), lambda h, m: (h, 0, 0)) for shape in shapes]
    else:
        out_shape = jax.ShapeDtypeStruct((2 * dests, heads, pairs // dests, LANES), jnp.bfloat16)
        out_spec = pl.BlockSpec((dests, 1, pairs // dests, LANES), lambda h, m: (within, h, 0, 0))
        if out is not None:
            in_specs.append(pl.BlockSpec(memory_space=pl.ANY))
            aliases = {1 + len(arrays): 0}
            arrays.append(out)
    unpacked = len(sources) * pairs
    work = heads * len(sources) * (2 * pairs) ** 2
    return pl.pallas_call(
        functools.partial(
            attend_kernel,
            tuple(source[0] for source in sources),
            scale,
            half,
            width,
            state is not None,
            None if state is None else state[2],
            dests is not None,
        ),
        out_shape=out_shape,
        grid_spec=pltpu.PrefetchScalarGridSpec(
            num_scalar_prefetch=1,
            grid=(heads,),
            in_specs=in_specs,
            out_specs=out_spec,
            scratch_shapes=[
                pltpu.VMEM((head_size, 2 * pairs), jnp.bfloat16),
                pltpu.VMEM((depth, unpacked), jnp.bfloat16),
                pltpu.VMEM((depth, unpacked), jnp.bfloat16),
                pltpu.VMEM((depth, 2 * pairs), jnp.float32),
                pltpu.VMEM((8, 2 * pairs), jnp.float32),
            ]
            + [pltpu.VMEM(shapes[0], jnp.float32), pltpu.SemaphoreType.DMA] * (state is not None),
        ),
        input_output_aliases=aliases,
        compiler_params=pltpu.CompilerParams(vmem_limit_bytes=VMEM if out is None else MOST),
        cost_estimate=pl.CostEstimate(
            flops=work * head_size * (16 if dests is None else 4), bytes_accessed=8 * heads * pairs * LANES * 2, transcendentals=work
        ),
        name=name,
    )(meta, *arrays)


def project_kernel(rows, weight_ref, part_ref, *refs):
    out_ref = refs[-1]
    lane = lax.broadcasted_iota(jnp.int32, (rows, LANES), 1) < LANES // 2
    heads = [part_ref[s, k].astype(jnp.float32) for s in range(part_ref.shape[0]) for k in range(part_ref.shape[1])]
    even, odd = [], []
    for a, b in zip(heads[::2], heads[1::2]):
        even.append(jnp.where(lane, a, swapped(b)).astype(jnp.bfloat16))
        odd.append(jnp.where(lane, swapped(a), b).astype(jnp.bfloat16))
    stacked = jnp.concatenate([jnp.concatenate(even, axis=1), jnp.concatenate(odd, axis=1)], axis=0)
    token = lax.broadcasted_iota(jnp.int32, (2 * rows, 2 * rows), 0)
    place = lax.broadcasted_iota(jnp.int32, (2 * rows, 2 * rows), 1)
    order = (place == token // 2 + (token % 2) * rows).astype(jnp.bfloat16)
    tokens = matmul(order, stacked).astype(jnp.bfloat16)
    weight = weight_ref[...]
    result = matmul(tokens, weight.reshape(-1, weight.shape[-1]))
    if len(refs) > 1:
        result = result + refs[0][...].astype(jnp.float32)
    out_ref[...] = result.astype(out_ref.dtype)


def project(part, group, weight, before):
    pairs = part.shape[2]
    rows = LANES if pairs % LANES == 0 else pairs
    columns = weight.shape[3]
    out = pl.BlockSpec((2 * rows, columns), lambda i: (i, 0))
    return pl.pallas_call(
        functools.partial(project_kernel, rows),
        out_shape=jax.ShapeDtypeStruct((2 * pairs, columns), jnp.bfloat16),
        grid=(pairs // rows,),
        in_specs=[
            pl.BlockSpec((weight.shape[0], None, *weight.shape[2:]), lambda i: (0, group, 0, 0)),
            pl.BlockSpec((*part.shape[:2], rows, LANES), lambda i: (0, 0, i, 0)),
        ]
        + [out] * (before is not None),
        out_specs=out,
        compiler_params=pltpu.CompilerParams(vmem_limit_bytes=WHOLE),
        cost_estimate=pl.CostEstimate(
            flops=4 * pairs * weight.size // weight.shape[1], bytes_accessed=8 * 2**20, transcendentals=0
        ),
        name="project",
    )(weight, part, *([] if before is None else [before]))


def shifted(x, pairs):
    return lax.ppermute(x, "frame", pairs)


def shards(query_proj, key_proj, value_proj, lengths, out_weight):
    devices = lax.axis_size("frame")
    groups = lax.axis_size("head")
    index = lax.axis_index("frame")
    heads, rows, _ = query_proj.shape
    half = rows // 2
    frames = lengths.shape[0]
    weight = lax.all_gather(out_weight, "head", axis=0, tiled=True)

    wanted = jnp.stack([2 * index + within - stride for within in range(2) for stride in STRIDES])
    table = jnp.arange(frames, dtype=jnp.int32)
    meta = jnp.sum(jnp.where(wanted[:, None] == table[None, :], lengths[None, :], 0), axis=1, dtype=jnp.int32)
    meta = jnp.minimum(meta, rows)

    size = heads // 2 if heads % 2 == 0 else heads
    starts = range(0, heads, size)
    by_two = [(i, i + 2) for i in range(devices - 2)]
    first = jnp.stack((key_proj[:, :half], value_proj[:, :half]))
    lasts = [
        jnp.stack((key_proj[start : start + size, half:], value_proj[start : start + size, half:]))
        for start in starts
    ]
    near_lasts = [shifted(last, by_two) for last in lasts]
    near_first = shifted(first, by_two)
    far = None
    if devices > 8:
        both = jnp.stack((key_proj, value_proj))
        far = shifted(both, [(i, i + 8) for i in range(devices - 8)])

    def own(slot, part, start):
        return slot, (key_proj, None, part, start), (value_proj, None, part, start)

    def moved(slot, array, part, start):
        return slot, (array, 0, part, start), (array, 1, part, start)

    state_last = {}
    for start in starts[:-1]:
        sources = [own(4, 1, start), own(5, 0, start)]
        sums, marks = attend(meta, query_proj, 1, start, size, sources, None, None, None, "last_own")
        state_last[start] = (sums, marks, 0)
        near_lasts[0], sums = lax.optimization_barrier((near_lasts[0], sums))
        state_last[start] = (sums, marks, 0)
    near_lasts[0], held = lax.optimization_barrier((near_lasts[0], query_proj))
    sums_first, marks_first = attend(meta, held, 0, 0, heads, [own(0, 0, 0)], None, None, None, "first_own")
    if len(starts) > 1:
        near_lasts[1], sums_first = lax.optimization_barrier((near_lasts[1], sums_first))
    to_even = [(i + 1, i) for i in range(2, devices - 1, 2)]
    to_odd = [(i, i + 1) for i in range(0, devices - 1, 2)]
    prevs = [
        shifted(jnp.where(index % 2 == 0, last, near), to_even + to_odd) for last, near in zip(lasts, near_lasts)
    ]
    dests = groups // 2
    outs = []
    for number, start in enumerate(starts):
        sources = [moved(6, near_lasts[number], 0, 0)]
        if far is not None:
            sources.append(moved(7, far, 1, start))
        state = state_last.get(start)
        if state is None:
            sources += [own(4, 1, start), own(5, 0, start)]
        outs.append(attend(meta, query_proj, 1, start, size, sources, state, dests, None, "last_rest"))
    weight, *outs = lax.optimization_barrier((weight, *outs))
    weight = weight.reshape(groups, len(starts), size * LANES // 2, weight.shape[1])
    result = None
    for number, start in enumerate(starts):
        sources = [moved(1, prevs[number], 0, 0), moved(2, near_first, 0, start)]
        if far is not None:
            sources.append(moved(3, far, 0, start))
        state = (sums_first, marks_first, start)
        out = attend(meta, query_proj, 0, start, size, sources, state, dests, outs[number], "first_rest")
        got = lax.all_to_all(out, "head", split_axis=0, concat_axis=0, tiled=True)
        result = project(got, number, weight, result)
    return result


def solution(mesh):
    return jax.shard_map(
        shards,
        mesh=mesh,
        in_specs=(
            P("head", "frame", None),
            P("head", "frame", None),
            P("head", "frame", None),
            P(),
            P("head", None),
        ),
        out_specs=P(("frame", "head"), None),
        check_vma=False,
    )
```
